32 devices in a mesh: frame: 4 (over y, core), video: 8 (over z, x).
Axes of the slice: x: 2, y: 2, z: 4, core: 2. Of those that a mesh axis runs over, the one named last changes fastest.
Arguments:
- frames: bfloat16 [16, 16, 197, 768], P('video', 'frame'), may hold values from -6 to 6
- out_cotangent: bfloat16 [16, 16, 197, 768], P('video', 'frame'), may hold values from -6 to 6
- frame_counts: int32 [16], P('video'), may hold values from 8 to 16, as said below
- message_proj: bfloat16 [768, 768], replicated, may hold values from -0.21875 to 0.21875
- message_gain: float32 [768], replicated, may hold values from 0.5 to 1.5
- message_qkv: bfloat16 [768, 2304], replicated, may hold values from -0.21875 to 0.21875
- message_out: bfloat16 [768, 768], replicated, may hold values from -0.625 to 0.625
- attn_gain: float32 [768], replicated, may hold values from 0.5 to 1.5
- attn_qkv: bfloat16 [768, 2304], replicated, may hold values from -0.21875 to 0.21875
- attn_out: bfloat16 [768, 768], replicated, may hold values from -0.875 to 0.875
- mlp_gain: float32 [768], replicated, may hold values from 0.5 to 1.5
- mlp_up: bfloat16 [768, 3072], replicated, may hold values from -0.21875 to 0.21875
- mlp_down: bfloat16 [3072, 768], replicated, may hold values from -0.21875 to 0.21875
Outputs:
- encoded: bfloat16 [16, 16, 197, 768], P('video', 'frame')
- frames_grad: float32 [16, 16, 197, 768], P('video', 'frame')
- message_proj_grad: float32 [768, 768], P('video')
- message_gain_grad: float32 [768], P('video')
- message_qkv_grad: float32 [768, 2304], P('video')
- message_out_grad: float32 [768, 768], P('video')
- attn_gain_grad: float32 [768], P('video')
- attn_qkv_grad: float32 [768, 2304], P('video')
- attn_out_grad: float32 [768, 768], P('video')
- mlp_gain_grad: float32 [768], P('video')
- mlp_up_grad: float32 [768, 3072], P('video')
- mlp_down_grad: float32 [3072, 768], P('video')
The draws below stay inside these ranges and needn't reach their ends.
Inputs may be any that keep to these rules, and one draw needn't show every extreme that they name: `frame_counts`: each video has 8 or 16 frames, held in its first frame slots; among the 2 videos at each index of video at least one has 16.
All inputs are finite; a program needn't handle non-finite values.
Results may differ from the reference program's by a relative error of at most 0.028.
Values may be sent and summed in bfloat16 or wider, within the bound.
No kernel may reach another device: no remote copies, remote signals or barrier semaphores. Data moves between devices by JAX's collectives and lax.ppermute only.
A program may use at most 256 MiB of HBM per device.

```python
import math
import jax
import jax.numpy as jnp
from jax import lax

D = 768
H = 12
HD = 64
FF = 3072
PATCH = 197
FRAMES = 16
VIDS_DEV = 2
VIDEOS = 16


def draw_frame_counts(key, part):
    key = jax.random.fold_in(key, 11)
    first_key, second_key = jax.random.split(key)
    group_count = VIDEOS // VIDS_DEV
    chosen = jax.random.randint(first_key, (group_count,), 0, VIDS_DEV)
    extra = jax.random.randint(second_key, (VIDEOS,), 0, 8)
    position = jnp.arange(VIDEOS, dtype=jnp.int32)
    forced = chosen[position // VIDS_DEV] == position % VIDS_DEV
    return jnp.where(forced | (extra == 0), FRAMES, FRAMES // 2).astype(jnp.int32)


def levels(stream_key, shape, shards, smallest, top_value):
    loudness = 1.0
    for dim, parts in shards:
        draws = jax.random.uniform(jax.random.fold_in(jax.random.fold_in(stream_key, 6), dim), (parts,), jnp.float32, smallest / len(shards), top_value / len(shards))
        loudness = loudness * jnp.repeat(jnp.exp(draws), shape[dim] // parts).reshape((-1,) + (1,) * (len(shape) - 1 - dim))
    return loudness


def bell_draw(rng, dims, scale, reach, cuts=(), held_as=jnp.bfloat16):
    level = levels(rng, dims, cuts, -0.22, 0.18) if cuts else 1.0
    entries = jax.random.normal(rng, dims, jnp.float32) * scale * level
    return jnp.minimum(jnp.maximum(entries, -reach), reach).astype(held_as)


def setup_inputs(seed: int = 0) -> dict:
    key_list = jax.random.split(jax.random.key(seed), 14)
    return {
        "frames": bell_draw(key_list[0], (VIDEOS, FRAMES, PATCH, D), 1.0, 6.0, ((0, 8), (1, 4))),
        "out_cotangent": bell_draw(key_list[1], (VIDEOS, FRAMES, PATCH, D), 1.0, 6.0, ((0, 8), (1, 4))),
        "frame_counts": draw_frame_counts(jax.random.fold_in(key_list[13], 71), 0),
        "message_proj": bell_draw(key_list[3], (D, D), D ** -0.5, 0.21875),
        "message_gain": jnp.clip(1.0 + 0.1 * jax.random.normal(key_list[4], (D,), jnp.float32), 0.5, 1.5),
        "message_qkv": bell_draw(key_list[5], (D, 3 * D), D ** -0.5, 0.21875),
        "message_out": bell_draw(key_list[6], (D, D), (D // 8) ** -0.5, 0.625),
        "attn_gain": jnp.clip(1.0 + 0.1 * jax.random.normal(key_list[7], (D,), jnp.float32), 0.5, 1.5),
        "attn_qkv": bell_draw(key_list[8], (D, 3 * D), D ** -0.5, 0.21875),
        "attn_out": bell_draw(key_list[9], (D, D), (D // 16) ** -0.5, 0.875),
        "mlp_gain": jnp.clip(1.0 + 0.1 * jax.random.normal(key_list[10], (D,), jnp.float32), 0.5, 1.5),
        "mlp_up": bell_draw(key_list[11], (D, FF), D ** -0.5, 0.21875),
        "mlp_down": bell_draw(key_list[12], (FF, D), (FF // 4) ** -0.5, 0.21875),
    }


HIGHEST = lax.Precision.HIGHEST
EPSILON = 1e-05

@jax.custom_vjp
def low(v):
    return lax.optimization_barrier(v.astype(jnp.bfloat16)).astype(jnp.float32)

@jax.custom_vjp
def low_back(v):
    return v

def low_keep(v):
    return (low(v), None)

def low_pass(kept, grad):
    return (grad,)

def back_keep(v):
    return (v, None)

def back_low(kept, grad):
    return (low(grad),)
low.defvjp(low_keep, low_pass)
low_back.defvjp(back_keep, back_low)

def layer_norm(value, gain):
    centre = lax.optimization_barrier(jnp.mean(value, axis=-1, keepdims=True))
    centred = value - centre
    spread = lax.optimization_barrier(jnp.mean(centred * centred, axis=-1, keepdims=True))
    return centred * lax.rsqrt(spread + EPSILON) * gain

def product(left, right):
    return jnp.dot(left, right, precision=HIGHEST)

def attend(queries, keys, values, keeper):
    scale = 1.0 / math.sqrt(HD)
    scores = jnp.einsum('...qhd,...khd->...hqk', queries, keys, precision=HIGHEST) * scale
    scores = low_back(scores)
    scores = jnp.where(keeper, scores, -1e+30)
    weights = jax.nn.softmax(scores, axis=-1)
    return jnp.einsum('...hqk,...khd->...qhd', low(weights), values, precision=HIGHEST)

def per_video(video, count, weights):
    message_proj, message_gain, message_qkv, message_out, attn_gain, attn_qkv, attn_out, mlp_gain, mlp_up, mlp_down = weights
    width = video.shape[-1]
    frame_ids = jnp.arange(FRAMES, dtype=jnp.int32)
    alive = (frame_ids < count).astype(jnp.float32)
    message_pre = low_back(product(video[:, 0, :], message_proj))
    message = layer_norm(message_pre, message_gain)
    message_low = low(message)
    message_mix = low(low_back(product(message_low, message_qkv))).reshape(FRAMES, 3, H, HD)
    keeper = (frame_ids < count)[None, None, :]
    mcontext = attend(message_mix[:, 0], message_mix[:, 1], message_mix[:, 2], keeper)
    mcontext = low(low_back(mcontext.reshape(FRAMES, width)))
    message_two = message + low_back(product(mcontext, message_out))
    stream = jnp.concatenate([video, message_two[:, None, :]], axis=1)
    tokens = stream.shape[1]
    normed_one = low(layer_norm(stream, attn_gain))
    triple = low(low_back(product(normed_one, attn_qkv))).reshape(FRAMES, tokens, 3, H, HD)
    every_key = jnp.ones((1, 1, 1, 1), dtype=bool)
    context = attend(triple[:, :, 0], triple[:, :, 1], triple[:, :, 2], every_key)
    context = low(low_back(context.reshape(FRAMES, tokens, width)))
    hidden = stream + low_back(product(context, attn_out))
    normed_two = low(layer_norm(hidden, mlp_gain))
    up_value = low_back(product(normed_two, mlp_up))
    activation = low(up_value * jax.nn.sigmoid(1.702 * up_value))
    final = hidden + low_back(product(activation, mlp_down))
    return final[:, :PATCH, :] * alive[:, None, None]

def reference(frames, out_cotangent, frame_counts, message_proj, message_gain, message_qkv, message_out, attn_gain, attn_qkv, attn_out, mlp_gain, mlp_up, mlp_down):
    weights = (message_proj.astype(jnp.float32), message_gain.astype(jnp.float32), message_qkv.astype(jnp.float32), message_out.astype(jnp.float32), attn_gain.astype(jnp.float32), attn_qkv.astype(jnp.float32), attn_out.astype(jnp.float32), mlp_gain.astype(jnp.float32), mlp_up.astype(jnp.float32), mlp_down.astype(jnp.float32))

    def forward(video_all, weight_all):
        single = jax.checkpoint(lambda video, count: per_video(video, count, weight_all))
        return lax.map(lambda pair: single(pair[0], pair[1]), (video_all, frame_counts))
    result, pullback = jax.vjp(forward, frames.astype(jnp.float32), weights)
    frames_grad, grads = pullback(out_cotangent.astype(jnp.float32))
    return (result.astype(jnp.bfloat16), frames_grad, grads[0], grads[1], grads[2], grads[3], grads[4], grads[5], grads[6], grads[7], grads[8], grads[9])
```

```python
import functools
import math

import jax
import jax.numpy as jnp
from jax import lax
from jax.experimental import pallas as pl
from jax.experimental.pallas import tpu as pltpu
from jax.sharding import PartitionSpec as P

H = 12
HD = 64
EPSILON = 1e-05
LOW = jnp.bfloat16
F32 = jnp.float32
BOTH = ("frame", "video")
SCALE = 1.0 / math.sqrt(HD)
PAIR = 2 * HD
PAIRS = H // 2
MESSAGE_TILE = 256
GAIN_ROWS = 16


def dot_nn(left, right):
    return lax.dot_general(
        left, right, (((1,), (0,)), ((), ())), preferred_element_type=F32
    )


def dot_nt(left, right):
    return lax.dot_general(
        left, right, (((1,), (1,)), ((), ())), preferred_element_type=F32
    )


def dot_tn(left, right):
    return lax.dot_general(
        left, right, (((0,), (0,)), ((), ())), preferred_element_type=F32
    )


def normalise(value):
    centred = value - jnp.mean(value, axis=-1, keepdims=True)
    inverse = lax.rsqrt(jnp.mean(centred * centred, axis=-1, keepdims=True) + EPSILON)
    return centred * inverse, inverse


def norm_back(upstream, normal, inverse, gain):
    scaled = upstream * gain
    inner = (
        scaled
        - jnp.mean(scaled, axis=-1, keepdims=True)
        - normal * jnp.mean(scaled * normal, axis=-1, keepdims=True)
    )
    return inner * inverse


def half_masks():
    first = lax.broadcasted_iota(jnp.int32, (1, PAIR), 1) < HD
    plain = (jnp.where(first, 1.0, 0.0).astype(LOW), jnp.where(first, 0.0, 1.0).astype(LOW))
    scaled = (jnp.where(first, SCALE, 0.0).astype(LOW), jnp.where(first, 0.0, SCALE).astype(LOW))
    return plain, scaled


def pair_forward(query, key, value, bias, masks):
    plain, scaled = masks
    context, logs = None, []
    for one, by in zip(plain, scaled):
        score = dot_nt(query * by, key) + bias
        top = jnp.max(score, axis=-1, keepdims=True)
        raised = jnp.exp(score - top)
        total = jnp.sum(raised, axis=-1, keepdims=True)
        prob_low = (raised * (1.0 / total)).astype(LOW)
        logs.append(top + jnp.log(total))
        part = dot_nn(prob_low, value * one)
        context = part if context is None else context + part
    return context, logs


def pair_backward(query, key, value, grad, logs, bias, masks):
    plain, scaled = masks
    query_grad = key_grad = value_grad = None
    for one, by, log in zip(plain, scaled, logs):
        query_by, grad_one, key_by = query * by, grad * one, key * by
        prob = jnp.exp(dot_nt(query_by, key) + bias - log)
        prob_grad = dot_nt(grad_one, value)
        inner = jnp.sum(prob * prob_grad, axis=-1, keepdims=True)
        score_low = (prob * (prob_grad - inner)).astype(LOW)
        parts = (
            dot_nn(score_low, key_by),
            dot_tn(score_low, query_by),
            dot_tn(prob.astype(LOW), grad_one),
        )
        if query_grad is None:
            query_grad, key_grad, value_grad = parts
        else:
            query_grad, key_grad, value_grad = (
                query_grad + parts[0],
                key_grad + parts[1],
                value_grad + parts[2],
            )
    return query_grad, key_grad, value_grad


def heads_forward(read, write, write_log, rows, width, bias):
    masks = half_masks()
    lane = lax.broadcasted_iota(jnp.int32, (rows, 128), 1)
    logs = jnp.zeros((rows, 128), F32)
    for pair in range(PAIRS):
        at = pair * PAIR
        context, pair_logs = pair_forward(
            read(at), read(width + at), read(2 * width + at), bias, masks
        )
        write(at, context.astype(LOW))
        for head in range(2):
            logs = jnp.where(lane == 2 * pair + head, pair_logs[head], logs)
    write_log(logs)


def heads_backward(read, read_grad, read_log, write, width, bias):
    masks = half_masks()
    for pair in range(PAIRS):
        at = pair * PAIR
        grads = pair_backward(
            read(at),
            read(width + at),
            read(2 * width + at),
            read_grad(at),
            (read_log(2 * pair), read_log(2 * pair + 1)),
            bias,
            masks,
        )
        for part in range(3):
            write(part * width + at, grads[part].astype(LOW))


def key_bias(tokens, padded):
    return jnp.where(lax.broadcasted_iota(jnp.int32, (1, padded), 1) < tokens, 0.0, -1e30)


def message_bias(flag, per_index, slots, videos):
    rows = flag.shape[0]
    row = lax.broadcasted_iota(jnp.int32, (rows, rows), 0)
    column = lax.broadcasted_iota(jnp.int32, (rows, rows), 1)
    same = (row // per_index == column // per_index) & (
        (row // slots) % videos == (column // slots) % videos
    )
    first = (lax.broadcasted_iota(jnp.int32, (rows, 128), 1) == 0).astype(LOW)
    alive = dot_nt(first, flag) > 0.5
    return jnp.where(same & alive, 0.0, -1e30)


WHOLE = pl.BlockSpec(memory_space=pltpu.VMEM)
SCALARS = pl.BlockSpec(memory_space=pltpu.SMEM)


def params(megabytes):
    return pltpu.CompilerParams(vmem_limit_bytes=megabytes << 20)


def cost(macs, moved, raised=0):
    return pl.CostEstimate(flops=2 * macs, bytes_accessed=moved, transcendentals=raised)


def shape(dims, dtype):
    return jax.ShapeDtypeStruct(dims, dtype)


def message_forward(sizes, payload, gain, proj, qkv, out):
    rows, wide = payload.shape
    width = proj.shape[0]
    tile = min(MESSAGE_TILE, rows)

    def body(pay, gain, proj, qkv, out, pre_o, low_o, qkv_o, log_o, context_o, two_o):
        pre = dot_nn(pay[:, :width], proj[...])
        pre_o[...] = pre
        normal, _ = normalise(pre)
        message = normal * gain[...]
        low = message.astype(LOW)
        low_o[...] = low
        qkv_o[...] = dot_nn(low, qkv[...]).astype(LOW)
        bias = message_bias(pay[:, width:], *sizes)

        def write(at, value):
            context_o[:, at : at + PAIR] = value

        def write_log(value):
            log_o[...] = value

        heads_forward(
            lambda at: qkv_o[:, at : at + PAIR], write, write_log, tile, width, bias
        )
        two_o[...] = message + dot_nn(context_o[...], out[...])

    def block(lanes):
        return pl.BlockSpec((tile, lanes), lambda i: (i, 0))

    return pl.pallas_call(
        body,
        grid=(rows // tile,),
        in_specs=[block(wide), WHOLE, WHOLE, WHOLE, WHOLE],
        out_specs=[block(width), block(width), block(3 * width), block(128), block(width), block(width)],
        out_shape=[
            shape((rows, width), F32),
            shape((rows, width), LOW),
            shape((rows, 3 * width), LOW),
            shape((rows, 128), F32),
            shape((rows, width), LOW),
            shape((rows, width), F32),
        ],
        compiler_params=params(48),
        cost_estimate=cost(5 * rows * width * width, 12 * width * width + 20 * rows * width),
        name="message_forward",
    )(payload, gain, proj, qkv, out)


def message_backward(
    sizes, ids, payload, two_low, pre, low, qkv_rows, logs, context, gain, proj, qkv, out, share
):
    rows, wide = payload.shape
    width = proj.shape[0]
    tile = min(MESSAGE_TILE, rows)

    def body(
        ids, pay, two, pre, low, rows_qkv, log, context, gain, proj, qkv, out,
        class_o, gain_o, proj_o, qkv_o, out_o, grad_s, triple_s,
    ):
        @pl.when(pl.program_id(0) == 0)
        def _():
            gain_o[...] = jnp.zeros_like(gain_o)
            proj_o[...] = jnp.zeros_like(proj_o)
            qkv_o[...] = jnp.zeros_like(qkv_o)
            out_o[...] = jnp.zeros_like(out_o)

        pick = lax.broadcasted_iota(jnp.int32, (width, share), 0) == (
            lax.broadcasted_iota(jnp.int32, (width, share), 1) + ids[1] * share
        )
        pick = jnp.where(pick, 1.0, 0.0).astype(LOW)
        two_rows = two[...]
        grad_s[...] = dot_nt(two_rows, out[...]).astype(LOW)
        out_o[...] += dot_tn(dot_nn(context[...], pick).astype(LOW), two_rows)
        bias = message_bias(pay[:, width:], *sizes)

        def write(at, value):
            triple_s[:, at : at + PAIR] = value

        heads_backward(
            lambda at: rows_qkv[:, at : at + PAIR],
            lambda at: grad_s[:, at : at + PAIR],
            lambda head: log[:, head : head + 1],
            write,
            width,
            bias,
        )
        triple = triple_s[...]
        qkv_o[...] += dot_tn(dot_nn(low[...], pick).astype(LOW), triple)
        upstream = two_rows.astype(F32) + dot_nt(triple, qkv[...])
        normal, inverse = normalise(pre[...])
        gain_o[...] += jnp.sum(upstream * normal, axis=0, keepdims=True)
        pre_low = norm_back(upstream, normal, inverse, gain[...]).astype(LOW)
        proj_o[...] += dot_tn(dot_nn(pay[:, :width], pick).astype(LOW), pre_low)
        class_o[...] = dot_nt(pre_low, proj[...])

    def block(lanes):
        return pl.BlockSpec((tile, lanes), lambda i: (i, 0))

    def fixed(dims):
        return pl.BlockSpec(dims, lambda i: (0, 0))

    return pl.pallas_call(
        body,
        grid=(rows // tile,),
        in_specs=[
            SCALARS, block(wide), block(width), block(width), block(width), block(3 * width),
            block(128), block(width), WHOLE, WHOLE, WHOLE, WHOLE,
        ],
        out_specs=[
            block(width), fixed((1, width)), fixed((share, width)), fixed((share, 3 * width)),
            fixed((share, width)),
        ],
        out_shape=[
            shape((rows, width), F32),
            shape((1, width), F32),
            shape((share, width), F32),
            shape((share, 3 * width), F32),
            shape((share, width), F32),
        ],
        scratch_shapes=[pltpu.VMEM((tile, width), LOW), pltpu.VMEM((tile, 3 * width), LOW)],
        compiler_params=params(48),
        cost_estimate=cost(8 * rows * width * width, 16 * width * width + 20 * rows * width),
        name="message_backward",
    )(ids, payload, two_low, pre, low, qkv_rows, logs, context, gain, proj, qkv, out)


def frame_forward(alive, tokens_in, cotangent, message, gain_one, gain_two, qkv, out, padded, step):
    videos, patches, slots, width = tokens_in.shape
    frames = videos * slots
    per = slots // step
    rows = step * padded

    def body(
        alive, tokens, grads, message, gain_one, gain_two, qkv, out,
        one_o, qkv_o, context_o, log_o, hidden_o, two_o, final_o, split_s, stream_s, grad_s,
    ):
        index = pl.program_id(0)
        video, part = index // per, index % per

        @pl.when(index == 0)
        def _():
            stream_s[...] = jnp.zeros_like(stream_s)
            grad_s[...] = jnp.zeros_like(grad_s)

        @pl.when(part == 0)
        def _():
            split_s[...] = tokens[0].astype(F32)
            for slot in range(slots):
                stream_s[slot, :patches, :] = split_s[:, slot, :]
                stream_s[slot, patches : patches + 1, :] = message[pl.ds(video * slots + slot, 1), :]
            split_s[...] = grads[0].astype(F32)
            for slot in range(slots):
                grad_s[:patches, :] = split_s[:, slot, :] * alive[video * slots + slot]
                final_o[slot] = grad_s[...].astype(LOW)

        stream = stream_s[pl.ds(part * step, step)].reshape(rows, width)
        one_low = (normalise(stream)[0] * gain_one[...]).astype(LOW)
        one_o[...] = one_low.reshape(step, padded, width)
        for third in range(3):
            cut = slice(third * width, (third + 1) * width)
            qkv_o[:, :, cut] = dot_nn(one_low, qkv[:, cut]).astype(LOW).reshape(step, padded, width)
        bias = key_bias(patches + 1, padded)
        for frame in range(step):

            def read(at):
                return qkv_o[frame, :, at : at + PAIR]

            def write(at, value):
                context_o[frame, :, at : at + PAIR] = value

            def write_log(value):
                log_o[frame] = value

            heads_forward(read, write, write_log, padded, width, bias)
        hidden = stream + dot_nn(context_o[...].reshape(rows, width), out[...])
        hidden_o[...] = hidden.reshape(step, padded, width)
        two_o[...] = (normalise(hidden)[0] * gain_two[...]).astype(LOW).reshape(step, padded, width)

    def block(lanes):
        return pl.BlockSpec((step, padded, lanes), lambda i: (i, 0, 0))

    per_video = pl.BlockSpec((1, patches, slots, width), lambda i: (i // per, 0, 0, 0))
    macs = 4 * frames * padded * width * width
    return pl.pallas_call(
        body,
        grid=(frames // step,),
        in_specs=[SCALARS, per_video, per_video, WHOLE, WHOLE, WHOLE, WHOLE, WHOLE],
        out_specs=[
            block(width), block(3 * width), block(width), block(128), block(width), block(width),
            pl.BlockSpec((slots, padded, width), lambda i: (i // per, 0, 0)),
        ],
        out_shape=[
            shape((frames, padded, width), LOW),
            shape((frames, padded, 3 * width), LOW),
            shape((frames, padded, width), LOW),
            shape((frames, padded, 128), F32),
            shape((frames, padded, width), F32),
            shape((frames, padded, width), LOW),
            shape((frames, padded, width), LOW),
        ],
        scratch_shapes=[
            pltpu.VMEM((patches, slots, width), F32),
            pltpu.VMEM((slots, padded, width), F32),
            pltpu.VMEM((padded, width), F32),
        ],
        compiler_params=params(58),
        cost_estimate=cost(2 * macs, 40 * frames * padded * width),
        name="frame_forward",
    )(alive, tokens_in, cotangent, message, gain_one, gain_two, qkv, out)


def slot_of(index, me, count):
    away = index ^ me
    return (away & 1) * (count // 2) + (away >> 1)


def store_shares(full, keep, send, core, place):
    half = full.shape[1] // 2
    left, right = full[:, :half].astype(LOW), full[:, half:].astype(LOW)
    first = core == 0
    place(keep, jnp.where(first, left, right))
    place(send, jnp.where(first, right, left))


def feed_forward(ids, alive, hidden, two, final, context, gain, up, down, dims, count):
    videos, patches, slots, padded = dims
    rows, width = hidden.shape
    inner = up.shape[1]
    blocks = inner // width
    half = width // 2
    frames = videos * slots
    tile = 2 * padded
    share, down_share = width // count, inner // count
    per_block = width // down_share
    low_count = per_block // 2

    def body(
        ids, alive, hidden, two, final, context, gain, up, down,
        encoded_o, grad_o, grad_low_o, up_keep, up_send, down_keep, down_send, out_keep, out_send, gain_o,
        total_s, act_s, back_s, join_s,
    ):
        step = pl.program_id(0)
        core, me = ids[0], ids[1]

        @pl.when(step == 0)
        def _():
            total_s[...] = hidden[...]
            grad_o[...] = jnp.zeros_like(grad_o)

        for part in range(rows // tile):
            cut = slice(part * tile, (part + 1) * tile)
            value = dot_nn(two[cut, :], up[...])
            act_grad = dot_nt(final[cut, :], down[...])
            sigma = 0.5 * jnp.tanh(0.851 * value) + 0.5
            act = value * sigma
            slope = sigma + 1.702 * (act - act * sigma)
            act_low = act.astype(LOW)
            back_low = (act_grad * slope).astype(LOW)
            act_s[cut, :] = act_low
            back_s[cut, :] = back_low
            total_s[cut, :] += dot_nn(act_low, down[...])
            grad_o[cut, :] += dot_nt(back_low, up[...])

        def place_rows(ref, value):
            for index in range(count):
                ref[slot_of(index, me, count), 0] = value[index * share : (index + 1) * share]

        def place_down(ref, value):
            for index in range(per_block):
                low = (index ^ me) & 1
                high = (index >> 1) ^ ((me >> 1) % low_count)
                ref[low, high] = value[index * down_share : (index + 1) * down_share]

        store_shares(dot_tn(two[...], back_s[...]), up_keep, up_send, core, place_rows)
        store_shares(dot_tn(act_s[...], final[...]), down_keep, down_send, core, place_down)

        @pl.when(step == blocks - 1)
        def _():
            gain_sum = jnp.zeros((1, width), F32)
            for video in range(videos):
                for slot in range(slots):
                    frame = video * slots + slot
                    cut = slice(frame * padded, (frame + 1) * padded)
                    join_s[:, slot, :] = total_s[cut, :][:patches] * alive[frame]
                    normal, inverse = normalise(hidden[cut, :])
                    upstream = grad_o[cut, :]
                    gain_sum += jnp.sum(upstream * normal, axis=0, keepdims=True)
                    back = norm_back(upstream, normal, inverse, gain[...])
                    back = final[cut, :].astype(F32) + back
                    grad_o[cut, :] = back
                    grad_low_o[cut, :] = back.astype(LOW)
                encoded_o[video] = join_s[...].astype(LOW)
            gain_o[...] = gain_sum
            store_shares(
                dot_tn(context[...], grad_low_o[...]), out_keep, out_send, core, place_rows
            )

    up_block = pl.BlockSpec((count, 1, share, half), lambda j, ids: (0, j, 0, 0))
    down_block = pl.BlockSpec(
        (2, low_count, down_share, half),
        lambda j, ids: (0, j ^ ((ids[1] >> 1) // low_count), 0, 0),
    )
    out_block = pl.BlockSpec((count, 1, share, half), lambda j, ids: (0, 0, 0, 0))
    up_shape = shape((count, blocks, share, half), LOW)
    down_shape = shape((2, count // 2, down_share, half), LOW)
    out_shape = shape((count, 1, share, half), LOW)
    return pl.pallas_call(
        body,
        grid_spec=pltpu.PrefetchScalarGridSpec(
            num_scalar_prefetch=1,
            grid=(blocks,),
            in_specs=[
                SCALARS, WHOLE, WHOLE, WHOLE, WHOLE, WHOLE,
                pl.BlockSpec((width, width), lambda j, ids: (0, j)),
                pl.BlockSpec((width, width), lambda j, ids: (j, 0)),
            ],
            out_specs=[
                WHOLE, WHOLE, WHOLE, up_block, up_block, down_block, down_block, out_block, out_block,
                WHOLE,
            ],
            scratch_shapes=[
                pltpu.VMEM((rows, width), F32),
                pltpu.VMEM((rows, width), LOW),
                pltpu.VMEM((rows, width), LOW),
                pltpu.VMEM((patches, slots, width), F32),
            ],
        ),
        out_shape=[
            shape((videos, patches, slots, width), LOW),
            shape((rows, width), F32),
            shape((rows, width), LOW),
            up_shape, up_shape, down_shape, down_shape, out_shape, out_shape,
            shape((1, width), F32),
        ],
        compiler_params=params(62),
        cost_estimate=cost(8 * rows * width * inner, 8 * width * inner + 20 * rows * width),
        name="feed_forward",
    )(ids, alive, hidden, two, final, context, gain, up, down)


def frame_backward(grad_low, qkv_rows, logs, out, tokens, step):
    frames, padded, width = grad_low.shape
    rows = step * padded

    def body(grad, rows_qkv, log, out, triple_o, context_s):
        context_s[...] = (
            dot_nt(grad[...].reshape(rows, width), out[...]).astype(LOW).reshape(step, padded, width)
        )
        bias = key_bias(tokens, padded)
        for frame in range(step):

            def write(at, value):
                triple_o[frame, :, at : at + PAIR] = value

            heads_backward(
                lambda at: rows_qkv[frame, :, at : at + PAIR],
                lambda at: context_s[frame, :, at : at + PAIR],
                lambda head: log[frame, :, head : head + 1],
                write,
                width,
                bias,
            )

    def block(lanes):
        return pl.BlockSpec((step, padded, lanes), lambda i: (i, 0, 0))

    return pl.pallas_call(
        body,
        grid=(frames // step,),
        in_specs=[block(width), block(3 * width), block(128), WHOLE],
        out_specs=block(3 * width),
        out_shape=shape((frames, padded, 3 * width), LOW),
        scratch_shapes=[pltpu.VMEM((step, padded, width), LOW)],
        compiler_params=params(56),
        cost_estimate=cost(22 * frames * padded * width * width // 4, 16 * frames * padded * width),
        name="frame_backward",
    )(grad_low, qkv_rows, logs, out)


def qkv_weight_grad(ids, one, triple, count):
    rows, width = one.shape
    blocks = triple.shape[1] // width
    share, half = width // count, width // 2

    def body(ids, one, triple, keep, send):
        me = ids[1]

        def place_rows(ref, value):
            for index in range(count):
                ref[slot_of(index, me, count), 0] = value[index * share : (index + 1) * share]

        store_shares(dot_tn(one[...], triple[...]), keep, send, ids[0], place_rows)

    block = pl.BlockSpec((count, 1, share, half), lambda j: (0, j, 0, 0))
    out = shape((count, blocks, share, half), LOW)
    return pl.pallas_call(
        body,
        grid=(blocks,),
        in_specs=[SCALARS, WHOLE, pl.BlockSpec((rows, width), lambda j: (0, j))],
        out_specs=[block, block],
        out_shape=[out, out],
        compiler_params=params(48),
        cost_estimate=cost(3 * rows * width * width, 8 * rows * width + 6 * width * width),
        name="qkv_weight_grad",
    )(ids, one, triple)


def stream_backward(tokens_in, message, grad, triple, gain, qkv, feed_gain, step):
    videos, patches, slots, width = tokens_in.shape
    frames, padded, _ = grad.shape
    per = slots // step
    rows = step * padded

    def body(
        tokens, message, grad, triple, gain, qkv, feed_gain, stream_o, message_o,
        split_s, stream_s, back_s, row_s, gain_s,
    ):
        index = pl.program_id(0)
        video, part = index // per, index % per

        @pl.when(index == 0)
        def _():
            stream_s[...] = jnp.zeros_like(stream_s)
            row_s[...] = jnp.zeros_like(row_s)
            gain_s[...] = jnp.zeros_like(gain_s)

        @pl.when(part == 0)
        def _():
            split_s[...] = tokens[0].astype(F32)
            for slot in range(slots):
                stream_s[slot, :patches, :] = split_s[:, slot, :]
                stream_s[slot, patches : patches + 1, :] = message[pl.ds(video * slots + slot, 1), :]

        upstream = dot_nt(triple[...].reshape(rows, 3 * width), qkv[...])
        normal, inverse = normalise(stream_s[pl.ds(part * step, step)].reshape(rows, width))
        gain_s[...] += jnp.sum(upstream * normal, axis=0, keepdims=True)
        back = norm_back(upstream, normal, inverse, gain[...]).reshape(step, padded, width)
        back = grad[...] + back
        back_s[pl.ds(part * step, step)] = back
        for frame in range(step):
            row_s[pl.ds(index * step + frame, 1), :] = back[frame, patches : patches + 1, :]

        @pl.when(part == per - 1)
        def _():
            for slot in range(slots):
                stream_o[0, :, slot, :] = back_s[slot, :patches, :]

        @pl.when(index == frames // step - 1)
        def _():
            row_s[frames : frames + 1, :] = gain_s[...]
            row_s[frames + 1 : frames + 2, :] = feed_gain[...]
            message_o[...] = row_s[...].astype(LOW)

    def block(lanes):
        return pl.BlockSpec((step, padded, lanes), lambda i: (i, 0, 0))

    per_video = pl.BlockSpec((1, patches, slots, width), lambda i: (i // per, 0, 0, 0))
    return pl.pallas_call(
        body,
        grid=(frames // step,),
        in_specs=[per_video, WHOLE, block(width), block(3 * width), WHOLE, WHOLE, WHOLE],
        out_specs=[per_video, pl.BlockSpec((GAIN_ROWS, width), lambda i: (0, 0))],
        out_shape=[shape((videos, patches, slots, width), F32), shape((GAIN_ROWS, width), LOW)],
        scratch_shapes=[
            pltpu.VMEM((patches, slots, width), F32),
            pltpu.VMEM((slots, padded, width), F32),
            pltpu.VMEM((slots, padded, width), F32),
            pltpu.VMEM((GAIN_ROWS, width), F32),
            pltpu.VMEM((1, width), F32),
        ],
        compiler_params=params(56),
        cost_estimate=cost(3 * frames * padded * width * width, 16 * frames * padded * width),
        name="stream_backward",
    )(tokens_in, message, grad, triple, gain, qkv, feed_gain)


def swap(value, frame_bits, video_bits):
    frames, videos = lax.axis_size("frame"), lax.axis_size("video")
    pairs = [
        (f * videos + v, (f ^ frame_bits) * videos + (v ^ video_bits))
        for f in range(frames)
        for v in range(videos)
    ]
    return lax.ppermute(value, BOTH, pairs)


def gather_all(value):
    frames, videos = lax.axis_size("frame"), lax.axis_size("video")
    value = jnp.stack([value] + [swap(value, 0, 2 * z) for z in range(1, videos // 2)], axis=0)
    value = jnp.stack([value] + [swap(value, 2 * y, 0) for y in range(1, frames // 2)], axis=1)
    value = jnp.stack([value, swap(value, 0, 1)], axis=0)
    value = jnp.stack([value, swap(value, 1, 0)], axis=2)
    return value.reshape(videos, frames, *value.shape[4:])


def reduce_shares(keep, send):
    frames, videos = lax.axis_size("frame"), lax.axis_size("video")
    half = videos // 2
    core = lax.axis_index("frame") & 1
    got = [swap(s, 1, 0) for s in send]

    def first(k, g, cut):
        return k[cut].astype(F32) + g[cut].astype(F32)

    out = [first(k, g, slice(half, None)).astype(LOW) for k, g in zip(keep, got)]
    across = [swap(o, 0, 1) for o in out]
    total = []
    for k, g, a in zip(keep, got, across):
        near = [first(k, g, slice(z, z + 1)) + a[z : z + 1].astype(F32) for z in range(half)]
        parts = [swap(near[z].astype(LOW), 0, 2 * z) for z in range(1, half)]
        summed = near[0]
        for part in parts:
            summed = summed + part.astype(F32)
        total.append(summed[0].astype(LOW))
    bit = 2
    while bit < frames:
        total = lax.optimization_barrier(total)
        total = [(t.astype(F32) + swap(t, bit, 0).astype(F32)).astype(LOW) for t in total]
        bit *= 2
    total = lax.optimization_barrier(total)
    other = [swap(t, 1, 0) for t in total]
    result = []
    for mine, theirs in zip(total, other):
        left = jnp.where(core == 0, mine, theirs)
        right = jnp.where(core == 0, theirs, mine)
        both = jnp.stack([left, right], axis=2)
        blocks, share, _, columns = both.shape
        both = both.transpose(1, 0, 2, 3).reshape(share, blocks * 2 * columns)
        result.append(both.astype(F32))
    return result


def on_device(
    frames,
    out_cotangent,
    frame_counts,
    message_proj,
    message_gain,
    message_qkv,
    message_out,
    attn_gain,
    attn_qkv,
    attn_out,
    mlp_gain,
    mlp_up,
    mlp_down,
):
    videos, slots, patches, width = frames.shape
    tokens = patches + 1
    padded = -(-tokens // 16) * 16
    frame_total = videos * slots
    row_total = frame_total * padded
    frame_axis, video_axis = lax.axis_size("frame"), lax.axis_size("video")
    frame_index, video_index = lax.axis_index("frame"), lax.axis_index("video")
    share = width // video_axis
    ids = jnp.stack([frame_index & 1, video_index]).astype(jnp.int32)
    slot_ids = frame_index * slots + jnp.arange(slots, dtype=jnp.int32)
    alive = (slot_ids[None, :] < frame_counts[:, None]).astype(F32).reshape(frame_total)
    gains = [g.reshape(1, width) for g in (message_gain, attn_gain, mlp_gain)]
    tokens_in = frames.transpose(0, 2, 1, 3)
    cotangent = out_cotangent.transpose(0, 2, 1, 3)

    class_rows = tokens_in[:, 0].reshape(frame_total, width)
    flags = jnp.broadcast_to(alive.astype(LOW)[:, None], (frame_total, 128))
    sizes = (frame_axis * frame_total, slots, videos)
    payload = gather_all(jnp.concatenate([class_rows, flags], axis=1))
    payload = payload.reshape(-1, width + 128)
    pre, low, qkv_rows, message_logs, mcontext, message_two = message_forward(
        sizes, payload, gains[0], message_proj, message_qkv, message_out
    )
    message_two = message_two[:frame_total]

    step = min(2, slots)
    one, triple, context, logs, hidden, two, final = frame_forward(
        alive, tokens_in, cotangent, message_two, gains[1], gains[2], attn_qkv, attn_out, padded, step
    )
    (
        encoded, hidden_grad, hidden_low, up_keep, up_send, down_keep, down_send, out_keep, out_send,
        feed_gain,
    ) = feed_forward(
        ids,
        alive,
        hidden.reshape(row_total, width),
        two.reshape(row_total, width),
        final.reshape(row_total, width),
        context.reshape(row_total, width),
        gains[2],
        mlp_up,
        mlp_down,
        (videos, patches, slots, padded),
        video_axis,
    )
    down_keep, down_send = (
        a.reshape(video_axis, 1, *a.shape[2:]) for a in (down_keep, down_send)
    )
    up_sum, down_sum, out_sum = reduce_shares(
        [up_keep, down_keep, out_keep], [up_send, down_send, out_send]
    )

    triple_grad = frame_backward(
        hidden_low.reshape(frame_total, padded, width), triple, logs, attn_out, tokens, step
    )
    qkv_keep, qkv_send = qkv_weight_grad(
        ids, one.reshape(row_total, width), triple_grad.reshape(row_total, 3 * width), video_axis
    )
    (qkv_sum,) = reduce_shares([qkv_keep], [qkv_send])
    stream_grad, rows_out = stream_backward(
        tokens_in,
        message_two,
        hidden_grad.reshape(frame_total, padded, width),
        triple_grad,
        gains[1],
        attn_qkv,
        feed_gain,
        step,
    )
    rows_all = gather_all(rows_out)
    two_low = rows_all[:, :, :frame_total].reshape(-1, width)
    gain_sums = rows_all[:, :, frame_total : frame_total + 2].astype(F32).sum(axis=(0, 1))
    class_grad, message_gain_grad, proj_sum, mqkv_sum, message_out_sum = message_backward(
        sizes, ids, payload, two_low, pre, low, qkv_rows, message_logs, mcontext,
        gains[0], message_proj, message_qkv, message_out, share,
    )
    class_grad = class_grad[:frame_total].reshape(videos, 1, slots, width)
    stream_grad = lax.dynamic_update_slice(
        stream_grad, stream_grad[:, :1] + class_grad, (0, 0, 0, 0)
    )
    cut = video_index * share
    message_gain_sum = lax.dynamic_slice(message_gain_grad[0], (cut,), (share,))
    attn_gain_sum = lax.dynamic_slice(gain_sums[0], (cut,), (share,))
    mlp_gain_sum = lax.dynamic_slice(gain_sums[1], (cut,), (share,))
    return (
        encoded.transpose(0, 2, 1, 3),
        stream_grad.transpose(0, 2, 1, 3),
        proj_sum,
        message_gain_sum,
        mqkv_sum,
        message_out_sum,
        attn_gain_sum,
        qkv_sum,
        out_sum,
        mlp_gain_sum,
        up_sum,
        down_sum,
    )


def solution(mesh):
    return jax.shard_map(
        on_device,
        mesh=mesh,
        in_specs=(
            P("video", "frame", None, None),
            P("video", "frame", None, None),
            P("video"),
            P(),
            P(),
            P(),
            P(),
            P(),
            P(),
            P(),
            P(),
            P(),
            P(),
        ),
        out_specs=(
            P("video", "frame", None, None),
            P("video", "frame", None, None),
            P("video", None),
            P("video"),
            P("video", None),
            P("video", None),
            P("video"),
            P("video", None),
            P("video", None),
            P("video"),
            P("video", None),
            P("video", None),
        ),
        check_vma=False,
    )
```

```python
import functools
import math

import jax
import jax.numpy as jnp
from jax import lax
from jax.experimental import pallas as pl
from jax.experimental.pallas import tpu as pltpu
from jax.sharding import PartitionSpec as P

H = 12
HD = 64
EPSILON = 1e-05
LOW = jnp.bfloat16
F32 = jnp.float32
BOTH = ("frame", "video")
SCALE = 1.0 / math.sqrt(HD)
PAIR = 2 * HD
PAIRS = H // 2
LOG_ROWS = 16
MESSAGE_TILE = 256


def dot_nn(left, right):
    return lax.dot_general(
        left, right, (((1,), (0,)), ((), ())), preferred_element_type=F32
    )


def dot_nt(left, right):
    return lax.dot_general(
        left, right, (((1,), (1,)), ((), ())), preferred_element_type=F32
    )


def dot_tn(left, right):
    return lax.dot_general(
        left, right, (((0,), (0,)), ((), ())), preferred_element_type=F32
    )


def normalise(value):
    centred = value - jnp.mean(value, axis=-1, keepdims=True)
    inverse = lax.rsqrt(jnp.mean(centred * centred, axis=-1, keepdims=True) + EPSILON)
    return centred * inverse, inverse


def norm_back(upstream, normal, inverse, gain):
    scaled = upstream * gain
    inner = (
        scaled
        - jnp.mean(scaled, axis=-1, keepdims=True)
        - normal * jnp.mean(scaled * normal, axis=-1, keepdims=True)
    )
    return inner * inverse


def half_masks():
    first = lax.broadcasted_iota(jnp.int32, (1, PAIR), 1) < HD
    plain = (jnp.where(first, 1.0, 0.0).astype(LOW), jnp.where(first, 0.0, 1.0).astype(LOW))
    scaled = (jnp.where(first, SCALE, 0.0).astype(LOW), jnp.where(first, 0.0, SCALE).astype(LOW))
    return plain, scaled


def pair_forward(query, key, value, bias, masks):
    plain, scaled = masks
    context, logs = None, []
    for one, by in zip(plain, scaled):
        score = dot_nt(key, query * by) + bias
        top = jnp.max(score, axis=0, keepdims=True)
        raised = jnp.exp(score - top)
        total = jnp.sum(raised, axis=0, keepdims=True)
        prob_low = (raised * (1.0 / total)).astype(LOW)
        logs.append(top + jnp.log(total))
        part = dot_tn(prob_low, value * one)
        context = part if context is None else context + part
    return context, logs


def pair_backward(query, key, value, grad, logs, bias, masks):
    plain, scaled = masks
    query_grad = key_grad = value_grad = None
    for one, by, log in zip(plain, scaled, logs):
        query_by, grad_one, key_by = query * by, grad * one, key * by
        prob = jnp.exp(dot_nt(key, query_by) + bias - log)
        prob_grad = dot_nt(value, grad_one)
        inner = jnp.sum(prob * prob_grad, axis=0, keepdims=True)
        score_low = (prob * (prob_grad - inner)).astype(LOW)
        parts = (
            dot_tn(score_low, key_by),
            dot_nn(score_low, query_by),
            dot_nn(prob.astype(LOW), grad_one),
        )
        if query_grad is None:
            query_grad, key_grad, value_grad = parts
        else:
            query_grad, key_grad, value_grad = (
                query_grad + parts[0],
                key_grad + parts[1],
                value_grad + parts[2],
            )
    return query_grad, key_grad, value_grad


def heads_forward(read, write, write_log, width, bias):
    masks = half_masks()
    for pair in range(PAIRS):
        at = pair * PAIR
        context, pair_logs = pair_forward(
            read(at), read(width + at), read(2 * width + at), bias, masks
        )
        write(at, context.astype(LOW))
        for head in range(2):
            write_log(2 * pair + head, pair_logs[head])


def heads_backward(read, read_grad, read_log, write, width, bias):
    masks = half_masks()
    for pair in range(PAIRS):
        at = pair * PAIR
        grads = pair_backward(
            read(at),
            read(width + at),
            read(2 * width + at),
            read_grad(at),
            (read_log(2 * pair), read_log(2 * pair + 1)),
            bias,
            masks,
        )
        for part in range(3):
            write(part * width + at, grads[part].astype(LOW))


def key_bias(tokens, padded):
    return jnp.where(lax.broadcasted_iota(jnp.int32, (padded, 1), 0) < tokens, 0.0, -1e30)


def message_bias(flag, per_index, slots, videos):
    rows = flag.shape[0]
    row = lax.broadcasted_iota(jnp.int32, (rows, rows), 0)
    column = lax.broadcasted_iota(jnp.int32, (rows, rows), 1)
    same = (row // per_index == column // per_index) & (
        (row // slots) % videos == (column // slots) % videos
    )
    first = (lax.broadcasted_iota(jnp.int32, (rows, 128), 1) == 0).astype(LOW)
    alive = dot_nt(flag, first) > 0.5
    return jnp.where(same & alive, 0.0, -1e30)


WHOLE = pl.BlockSpec(memory_space=pltpu.VMEM)
SCALARS = pl.BlockSpec(memory_space=pltpu.SMEM)
ANY = pl.BlockSpec(memory_space=pl.ANY)


def params(megabytes):
    return pltpu.CompilerParams(vmem_limit_bytes=megabytes << 20)


def cost(macs, moved, raised=0):
    return pl.CostEstimate(flops=2 * macs, bytes_accessed=moved, transcendentals=raised)


def shape(dims, dtype):
    return jax.ShapeDtypeStruct(dims, dtype)


def message_token(sizes, payload, gain, proj, qkv, out, next_gain, next_qkv):
    rows, wide = payload.shape
    width = proj.shape[0]

    def body(pay, gain, proj, qkv, out, next_gain, next_qkv, two_o, one_o, triple_o, rows_s, context_s):
        message = normalise(dot_nn(pay[:, :width], proj[...]))[0] * gain[...]
        rows_s[...] = dot_nn(message.astype(LOW), qkv[...]).astype(LOW)
        bias = message_bias(pay[:, width:], *sizes)

        def write(at, value):
            context_s[:, at : at + PAIR] = value

        heads_forward(
            lambda at: rows_s[:, at : at + PAIR], write, lambda head, value: None, width, bias
        )
        two = message + dot_nn(context_s[...], out[...])
        two_o[...] = two
        one_low = (normalise(two)[0] * next_gain[...]).astype(LOW)
        one_o[...] = one_low
        triple_o[...] = dot_nn(one_low, next_qkv[...]).astype(LOW)

    return pl.pallas_call(
        body,
        in_specs=[WHOLE] * 7,
        out_specs=[WHOLE] * 3,
        out_shape=[shape((rows, width), F32), shape((rows, width), LOW), shape((rows, 3 * width), LOW)],
        scratch_shapes=[pltpu.VMEM((rows, 3 * width), LOW), pltpu.VMEM((rows, width), LOW)],
        compiler_params=params(48),
        cost_estimate=cost(8 * rows * width * width, 16 * width * width + 20 * rows * width),
        name="message_token",
    )(payload, gain, proj, qkv, out, next_gain, next_qkv)


def message_backward(sizes, ids, gathered, gain, proj, qkv, out, share, after=()):
    rows, wide = gathered.shape
    width = proj.shape[0]
    tile = min(MESSAGE_TILE, rows)

    def body(ids, given, gain, proj, qkv, out, *rest):
        class_o, gain_o, proj_o, qkv_o, out_o = rest[len(after) : len(after) + 5]
        rows_s, context_s, grad_s, triple_s, log_s = rest[len(after) + 5 :]

        @pl.when(pl.program_id(0) == 0)
        def _():
            gain_o[...] = jnp.zeros_like(gain_o)
            proj_o[...] = jnp.zeros_like(proj_o)
            qkv_o[...] = jnp.zeros_like(qkv_o)
            out_o[...] = jnp.zeros_like(out_o)

        pick = lax.broadcasted_iota(jnp.int32, (width, share), 0) == (
            lax.broadcasted_iota(jnp.int32, (width, share), 1) + ids[1] * share
        )
        pick = jnp.where(pick, 1.0, 0.0).astype(LOW)

        def picked(value):
            return dot_nn(value, pick).astype(LOW)

        classes, two_rows = given[:, :width], given[:, width + 128 :]
        normal, inverse = normalise(dot_nn(classes, proj[...]))
        low = (normal * gain[...]).astype(LOW)
        rows_s[...] = dot_nn(low, qkv[...]).astype(LOW)
        bias = message_bias(given[:, width : width + 128], *sizes)

        def read(at):
            return rows_s[:, at : at + PAIR]

        def write_context(at, value):
            context_s[:, at : at + PAIR] = value

        def write_log(head, value):
            log_s[head : head + 1, :] = value

        heads_forward(read, write_context, write_log, width, bias)
        grad_s[...] = dot_nt(two_rows, out[...]).astype(LOW)
        out_o[...] += dot_tn(picked(context_s[...]), two_rows)

        def write(at, value):
            triple_s[:, at : at + PAIR] = value

        heads_backward(
            read,
            lambda at: grad_s[:, at : at + PAIR],
            lambda head: log_s[head : head + 1, :],
            write,
            width,
            bias,
        )
        triple = triple_s[...]
        qkv_o[...] += dot_tn(picked(low), triple)
        upstream = two_rows.astype(F32) + dot_nt(triple, qkv[...])
        gain_o[...] += jnp.sum(upstream * normal, axis=0, keepdims=True)
        pre_low = norm_back(upstream, normal, inverse, gain[...]).astype(LOW)
        proj_o[...] += dot_tn(picked(classes), pre_low)
        class_o[...] = dot_nt(pre_low, proj[...])

    def fixed(dims):
        return pl.BlockSpec(dims, lambda i: (0, 0))

    return pl.pallas_call(
        body,
        grid=(rows // tile,),
        in_specs=[SCALARS, pl.BlockSpec((tile, wide), lambda i: (i, 0)), WHOLE, WHOLE, WHOLE, WHOLE]
        + [ANY] * len(after),
        out_specs=[
            pl.BlockSpec((tile, width), lambda i: (i, 0)),
            fixed((1, width)), fixed((share, width)), fixed((share, 3 * width)), fixed((share, width)),
        ],
        out_shape=[
            shape((rows, width), F32),
            shape((1, width), F32),
            shape((share, width), F32),
            shape((share, 3 * width), F32),
            shape((share, width), F32),
        ],
        scratch_shapes=[
            pltpu.VMEM((tile, 3 * width), LOW),
            pltpu.VMEM((tile, width), LOW),
            pltpu.VMEM((tile, width), LOW),
            pltpu.VMEM((tile, 3 * width), LOW),
            pltpu.VMEM((LOG_ROWS, tile), F32),
        ],
        compiler_params=params(48),
        cost_estimate=cost(14 * rows * width * width, 16 * width * width + 20 * rows * width),
        name="message_backward",
    )(ids, gathered, gain, proj, qkv, out, *after)


def frame_project(alive, tokens_in, cotangent, gain, qkv, padded, step):
    videos, patches, slots, width = tokens_in.shape
    frames = videos * slots
    per = slots // step
    rows = step * padded

    def body(alive, tokens, grads, gain, qkv, one_o, qkv_o, final_o, split_s, stream_s, grad_s):
        index = pl.program_id(0)
        video, part = index // per, index % per

        @pl.when(index == 0)
        def _():
            stream_s[...] = jnp.zeros_like(stream_s)
            grad_s[...] = jnp.zeros_like(grad_s)

        @pl.when(part == 0)
        def _():
            split_s[...] = tokens[0].astype(F32)
            for slot in range(slots):
                stream_s[slot, :patches, :] = split_s[:, slot, :]
            split_s[...] = grads[0].astype(F32)
            for slot in range(slots):
                grad_s[:patches, :] = split_s[:, slot, :] * alive[video * slots + slot]
                final_o[slot] = grad_s[...].astype(LOW)

        stream = stream_s[pl.ds(part * step, step)].reshape(rows, width)
        one_low = (normalise(stream)[0] * gain[...]).astype(LOW)
        one_o[...] = one_low.reshape(step, padded, width)
        for third in range(3):
            cut = slice(third * width, (third + 1) * width)
            qkv_o[:, :, cut] = dot_nn(one_low, qkv[:, cut]).astype(LOW).reshape(step, padded, width)

    def block(lanes):
        return pl.BlockSpec((step, padded, lanes), lambda i: (i, 0, 0))

    per_video = pl.BlockSpec((1, patches, slots, width), lambda i: (i // per, 0, 0, 0))
    return pl.pallas_call(
        body,
        grid=(frames // step,),
        in_specs=[SCALARS, per_video, per_video, WHOLE, WHOLE],
        out_specs=[
            block(width), block(3 * width),
            pl.BlockSpec((slots, padded, width), lambda i: (i // per, 0, 0)),
        ],
        out_shape=[
            shape((frames, padded, width), LOW),
            shape((frames, padded, 3 * width), LOW),
            shape((frames, padded, width), LOW),
        ],
        scratch_shapes=[
            pltpu.VMEM((patches, slots, width), F32),
            pltpu.VMEM((slots, padded, width), F32),
            pltpu.VMEM((padded, width), F32),
        ],
        compiler_params=params(50),
        cost_estimate=cost(4 * frames * padded * width * width, 16 * frames * padded * width),
        name="frame_project",
    )(alive, tokens_in, cotangent, gain, qkv)


def frame_attend(tokens_in, message, qkv_rows, gain, out, step):
    videos, patches, slots, width = tokens_in.shape
    frames, padded, _ = qkv_rows.shape
    per = slots // step
    rows = step * padded

    def body(
        tokens, message, rows_qkv, gain, out,
        context_o, log_o, hidden_o, two_o, split_s, stream_s,
    ):
        index = pl.program_id(0)
        video, part = index // per, index % per

        @pl.when(index == 0)
        def _():
            stream_s[...] = jnp.zeros_like(stream_s)

        @pl.when(part == 0)
        def _():
            split_s[...] = tokens[0].astype(F32)
            for slot in range(slots):
                stream_s[slot, :patches, :] = split_s[:, slot, :]
                stream_s[slot, patches : patches + 1, :] = message[pl.ds(video * slots + slot, 1), :]

        bias = key_bias(patches + 1, padded)
        for frame in range(step):

            def read(at):
                return rows_qkv[frame, :, at : at + PAIR]

            def write(at, value):
                context_o[frame, :, at : at + PAIR] = value

            def write_log(head, value):
                log_o[frame, head : head + 1, :] = value

            heads_forward(read, write, write_log, width, bias)
        stream = stream_s[pl.ds(part * step, step)].reshape(rows, width)
        hidden = stream + dot_nn(context_o[...].reshape(rows, width), out[...])
        hidden_o[...] = hidden.reshape(step, padded, width)
        two_o[...] = (normalise(hidden)[0] * gain[...]).astype(LOW).reshape(step, padded, width)

    def block(lanes):
        return pl.BlockSpec((step, padded, lanes), lambda i: (i, 0, 0))

    per_video = pl.BlockSpec((1, patches, slots, width), lambda i: (i // per, 0, 0, 0))
    return pl.pallas_call(
        body,
        grid=(frames // step,),
        in_specs=[per_video, WHOLE, block(3 * width), WHOLE, WHOLE],
        out_specs=[block(width), pl.BlockSpec((step, LOG_ROWS, padded), lambda i: (i, 0, 0)), block(width), block(width)],
        out_shape=[
            shape((frames, padded, width), LOW),
            shape((frames, LOG_ROWS, padded), F32),
            shape((frames, padded, width), F32),
            shape((frames, padded, width), LOW),
        ],
        scratch_shapes=[
            pltpu.VMEM((patches, slots, width), F32),
            pltpu.VMEM((slots, padded, width), F32),
        ],
        compiler_params=params(50),
        cost_estimate=cost(8 * frames * padded * width * width, 24 * frames * padded * width),
        name="frame_attend",
    )(tokens_in, message, qkv_rows, gain, out)


def place_of(index, part, core, ids):
    away = index ^ ids[1]
    x, y = away & 1, part ^ (ids[2] & 1)
    straight = core == 0
    return jnp.where(straight, x, y), jnp.where(straight, y, x), away >> 1


def place_shares(ref, value, core, ids, count):
    rows = value.shape[0] // count // 2
    for index in range(count):
        for part in range(2):
            at = (2 * index + part) * rows
            first, second, z = place_of(index, part, core, ids)
            ref[first, second, z, 0] = value[at : at + rows]


def store_shares(full, keep, send, core, place):
    half = full.shape[1] // 2
    left, right = full[:, :half].astype(LOW), full[:, half:].astype(LOW)
    first = core == 0
    place(keep, jnp.where(first, left, right), core)
    place(send, jnp.where(first, right, left), 1 - core)


def feed_forward(ids, alive, hidden, two, final, context, gain, up, down, dims, count):
    videos, patches, slots, padded = dims
    rows, width = hidden.shape
    inner = up.shape[1]
    blocks = inner // width
    half = width // 2
    step = min(2, slots)
    per = slots // step
    last = blocks - 1
    tile = step * padded
    tails = rows // tile
    share, down_share = width // count, inner // count
    per_block = width // down_share
    low_count = per_block // 2

    def body(
        ids, alive, hidden, two, final, context, gain, up, down,
        encoded_o, grad_o, grad_low_o, up_keep, up_send, down_keep, down_send,
        total_s, back_sum_s, act_s, back_s, join_s, split_s, out_s,
    ):
        index = pl.program_id(0)
        core = ids[0]

        def place_rows(ref, value, core):
            place_shares(ref, value, core, ids, count)

        def place_down(ref, value, core):
            for at in range(per_block):
                for part in range(2):
                    row = (2 * at + part) * down_share // 2
                    first, second, z = place_of(at, part, core, ids)
                    ref[first, second, z % low_count] = value[row : row + down_share // 2]

        @pl.when(index == 0)
        def _():
            total_s[...] = jnp.zeros_like(total_s)
            back_sum_s[...] = jnp.zeros_like(back_sum_s)
            out_s[...] = jnp.zeros_like(out_s)

        @pl.when(index < blocks)
        def _():
            for part in range(rows // tile):
                cut = slice(part * tile, (part + 1) * tile)
                value = dot_nn(two[cut, :], up[...])
                act_grad = dot_nt(final[cut, :], down[...])
                sigma = 0.5 * jnp.tanh(0.851 * value) + 0.5
                act = value * sigma
                slope = sigma + 1.702 * (act - act * sigma)
                act_low = act.astype(LOW)
                back_low = (act_grad * slope).astype(LOW)
                act_s[cut, :] = act_low
                back_s[cut, :] = back_low
                total_s[cut, :] += dot_nn(act_low, down[...])
                back_sum_s[cut, :] += dot_nt(back_low, up[...])
            store_shares(dot_tn(two[...], back_s[...]), up_keep, up_send, core, place_rows)
            store_shares(dot_tn(act_s[...], final[...]), down_keep, down_send, core, place_down)

        @pl.when(index >= blocks)
        def _():
            tail = index - blocks
            cut = pl.ds(pl.multiple_of(tail * tile, tile), tile)
            value = hidden[...]
            total = (value + total_s[cut, :]).reshape(step, padded, width)
            for frame in range(step):
                join_s[(tail % per) * step + frame] = total[frame, :patches] * alive[tail * step + frame]
            normal, inverse = normalise(value)
            back = norm_back(back_sum_s[cut, :], normal, inverse, gain[...])
            back = final[cut, :].astype(F32) + back
            back_low = back.astype(LOW)
            grad_o[...] = back
            grad_low_o[...] = back_low
            out_s[...] += dot_tn(context[...], back_low)

            @pl.when(tail % per == per - 1)
            def _():
                for slot in range(slots):
                    split_s[:, slot, :] = join_s[slot]
                encoded_o[0] = split_s[...].astype(LOW)

            @pl.when(tail == tails - 1)
            def _():
                store_shares(out_s[...], up_keep, up_send, core, place_rows)

    def tail_of(j):
        return jnp.maximum(j - blocks, 0)

    up_block = pl.BlockSpec(
        (2, 2, count // 2, 1, share // 2, half), lambda j, ids: (0, 0, 0, jnp.minimum(j, blocks), 0, 0)
    )
    down_block = pl.BlockSpec(
        (2, 2, low_count, down_share // 2, half),
        lambda j, ids: (0, 0, jnp.minimum(j, last) ^ ((ids[1] >> 1) // low_count), 0, 0),
    )
    rows_block = pl.BlockSpec((tile, width), lambda j, ids: (tail_of(j), 0))
    up_shape = shape((2, 2, count // 2, blocks + 1, share // 2, half), LOW)
    down_shape = shape((2, 2, count // 2, down_share // 2, half), LOW)
    return pl.pallas_call(
        body,
        grid_spec=pltpu.PrefetchScalarGridSpec(
            num_scalar_prefetch=1,
            grid=(blocks + tails,),
            in_specs=[
                SCALARS, rows_block, WHOLE, WHOLE, rows_block, WHOLE,
                pl.BlockSpec((width, width), lambda j, ids: (0, jnp.minimum(j, last))),
                pl.BlockSpec((width, width), lambda j, ids: (jnp.minimum(j, last), 0)),
            ],
            out_specs=[
                pl.BlockSpec((1, patches, slots, width), lambda j, ids: (tail_of(j) // per, 0, 0, 0)),
                rows_block, rows_block, up_block, up_block, down_block, down_block,
            ],
            scratch_shapes=[
                pltpu.VMEM((rows, width), F32),
                pltpu.VMEM((rows, width), F32),
                pltpu.VMEM((rows, width), LOW),
                pltpu.VMEM((rows, width), LOW),
                pltpu.VMEM((slots, patches, width), F32),
                pltpu.VMEM((patches, slots, width), F32),
                pltpu.VMEM((width, width), F32),
            ],
        ),
        out_shape=[
            shape((videos, patches, slots, width), LOW),
            shape((rows, width), F32),
            shape((rows, width), LOW),
            up_shape, up_shape, down_shape, down_shape,
        ],
        compiler_params=params(60),
        cost_estimate=cost(8 * rows * width * inner, 8 * width * inner + 20 * rows * width),
        name="feed_forward",
    )(ids, alive, hidden, two, final, context, gain, up, down)


def frame_backward(grad_low, qkv_rows, logs, out, tokens, step, first, steps, into=None, after=()):
    frames, padded, width = grad_low.shape
    rows = step * padded
    into = () if into is None else (into,)
    extra = len(into) + len(after)

    def body(grad, rows_qkv, log, out, *rest):
        triple_o, context_s = rest[extra:]
        context_s[...] = (
            dot_nt(grad[...].reshape(rows, width), out[...]).astype(LOW).reshape(step, padded, width)
        )
        bias = key_bias(tokens, padded)
        for frame in range(step):
            def write(at, value):
                triple_o[frame, :, at : at + PAIR] = value

            heads_backward(
                lambda at: rows_qkv[frame, :, at : at + PAIR],
                lambda at: context_s[frame, :, at : at + PAIR],
                lambda head: log[frame, head : head + 1, :],
                write,
                width,
                bias,
            )

    def block(lanes):
        return pl.BlockSpec((step, padded, lanes), lambda i: (i + first, 0, 0))

    return pl.pallas_call(
        body,
        grid=(steps,),
        in_specs=[block(width), block(3 * width), pl.BlockSpec((step, LOG_ROWS, padded), lambda i: (i + first, 0, 0)), WHOLE] + [ANY] * extra,
        out_specs=block(3 * width),
        out_shape=shape((frames, padded, 3 * width), LOW),
        scratch_shapes=[pltpu.VMEM((step, padded, width), LOW)],
        input_output_aliases={4: 0} if into else {},
        compiler_params=params(50),
        cost_estimate=cost(20 * steps * rows * width * width, 16 * steps * rows * width),
        name="frame_backward",
    )(grad_low, qkv_rows, logs, out, *into, *after)


def qkv_weight_grad(ids, one, triple, count, third, into=(), after=()):
    rows, width = one.shape
    share, half = width // count, width // 2

    def body(ids, one, triple, *rest):
        keep, send = rest[len(into) + len(after) :]

        def place_rows(ref, value, core):
            place_shares(ref, value, core, ids, count)

        store_shares(dot_tn(one[...], triple[...]), keep, send, ids[0], place_rows)

    def whole(dims, at):
        return pl.BlockSpec(dims, lambda i: at)

    block = whole((2, 2, count // 2, 1, share // 2, half), (0, 0, 0, third, 0, 0))
    out = shape((2, 2, count // 2, triple.shape[1] // width, share // 2, half), LOW)
    return pl.pallas_call(
        body,
        grid=(1,),
        in_specs=[SCALARS, whole((rows, width), (0, 0)), whole((rows, width), (0, third))]
        + [ANY] * (len(into) + len(after)),
        out_specs=[block, block],
        out_shape=[out, out],
        input_output_aliases={3: 0, 4: 1} if into else {},
        compiler_params=params(48),
        cost_estimate=cost(2 * rows * width * width, 4 * rows * width + 2 * width * width),
        name="qkv_weight_grad",
    )(ids, one, triple, *into, *after)


def message_rows(rows_triple, message, grad, gain, qkv):
    count, width = message.shape

    def body(rows_triple, message, grad, gain, qkv, rows_o):
        normal, inverse = normalise(message[...])
        back = norm_back(dot_nt(rows_triple[...], qkv[...]), normal, inverse, gain[...])
        rows_o[...] = (grad[...] + back).astype(LOW)

    return pl.pallas_call(
        body,
        in_specs=[WHOLE] * 5,
        out_specs=WHOLE,
        out_shape=shape((count, width), LOW),
        compiler_params=params(32),
        cost_estimate=cost(20 * count * width * width, 6 * width * width),
        name="message_rows",
    )(rows_triple, message, grad, gain, qkv)


def stream_backward(tokens_in, grad, triple, class_grad, gain, qkv, step, first, steps, into=None, after=()):
    videos, patches, slots, width = tokens_in.shape
    frames, padded, _ = grad.shape
    per = slots // step
    rows = step * padded
    into = () if into is None else (into,)
    extra = len(into) + len(after)

    def body(tokens, grad, triple, class_grad, gain, qkv, *rest):
        stream_o, split_s, stream_s, back_s = rest[extra:]
        index = pl.program_id(0)
        part = index % per

        @pl.when(index == 0)
        def _():
            stream_s[...] = jnp.zeros_like(stream_s)

        @pl.when(part == 0)
        def _():
            split_s[...] = tokens[0].astype(F32)
            for slot in range(slots):
                stream_s[slot, :patches, :] = split_s[:, slot, :]

        upstream = dot_nt(triple[...].reshape(rows, 3 * width), qkv[...])
        normal, inverse = normalise(stream_s[pl.ds(part * step, step)].reshape(rows, width))
        back = norm_back(upstream, normal, inverse, gain[...]).reshape(step, padded, width)
        back_s[pl.ds(part * step, step)] = grad[...] + back

        @pl.when(part == per - 1)
        def _():
            for slot in range(slots):
                stream_o[0, :, slot, :] = back_s[slot, :patches, :]
            stream_o[0, 0] += class_grad[first + index // per]

    def block(lanes):
        return pl.BlockSpec((step, padded, lanes), lambda i: (i + first * per, 0, 0))

    per_video = pl.BlockSpec((1, patches, slots, width), lambda i: (first + i // per, 0, 0, 0))
    return pl.pallas_call(
        body,
        grid=(steps * per,),
        in_specs=[per_video, block(width), block(3 * width), WHOLE, WHOLE, WHOLE] + [ANY] * extra,
        out_specs=per_video,
        out_shape=shape((videos, patches, slots, width), F32),
        scratch_shapes=[
            pltpu.VMEM((patches, slots, width), F32),
            pltpu.VMEM((slots, padded, width), F32),
            pltpu.VMEM((slots, padded, width), F32),
        ],
        input_output_aliases={6: 0} if into else {},
        compiler_params=params(50),
        cost_estimate=cost(6 * steps * per * rows * width * width, 16 * steps * per * rows * width),
        name="stream_backward",
    )(tokens_in, grad, triple, class_grad, gain, qkv, *into, *after)


def join_shares(ids, own, other, sections):
    parts = len(own)
    half = own[0].shape[1]
    extra = [(w, g) for _, _, w, g in sections if w is not None]

    def body(ids, *refs):
        own_r, other_r = refs[:parts], refs[parts : 2 * parts]
        extra_r = refs[2 * parts : 2 * parts + 2 * len(extra)]
        outs = refs[2 * parts + 2 * len(extra) : -1]
        column_s = refs[-1]
        first = ids[0] == 0
        y = ids[2] & 1

        def pick(pieces, part, cut):
            value = pieces[0][cut, :]
            for away in range(1, parts):
                value = jnp.where((part ^ y) == away, pieces[away][cut, :], value)
            return value

        at = given = 0
        for index, (blocks, rows, weight, _) in enumerate(sections):
            for part in range(parts):
                to = slice(part * rows, (part + 1) * rows)
                total = jnp.zeros((rows, 1), F32)
                for block in range(blocks):
                    cut = slice(at + block * rows, at + (block + 1) * rows)
                    mine, theirs = pick(own_r, part, cut), pick(other_r, part, cut)
                    sides = (jnp.where(first, mine, theirs), jnp.where(first, theirs, mine))
                    for side, value in enumerate(sides):
                        columns = slice((2 * block + side) * half, (2 * block + side + 1) * half)
                        value = value.astype(F32)
                        outs[index][to, columns] = value
                        if weight is not None:
                            product = value * extra_r[2 * given][to, columns].astype(F32)
                            total += jnp.sum(product, axis=1, keepdims=True)
                column_s[to, :] = jnp.broadcast_to(total, (rows, 128))
            at += blocks * rows
            if weight is not None:
                sums = column_s[...].T[:1, : parts * rows]
                outs[len(sections) + given][...] = sums / extra_r[2 * given + 1][...]
                given += 1

    extra_specs, extra_args = [], []
    for (blocks, rows, weight, gain) in sections:
        if weight is not None:
            extra_specs += [
                pl.BlockSpec((parts * rows, weight.shape[1]), lambda i, ids: (ids[1], 0)), WHOLE
            ]
            extra_args += [weight, gain]
    high = -(-max(parts * rows for _, rows, _, _ in sections) // 128) * 128
    return pl.pallas_call(
        body,
        grid_spec=pltpu.PrefetchScalarGridSpec(
            num_scalar_prefetch=1,
            grid=(1,),
            in_specs=[WHOLE] * (2 * parts) + extra_specs,
            out_specs=[WHOLE] * (len(sections) + len(extra)),
            scratch_shapes=[pltpu.VMEM((high, 128), F32)],
        ),
        out_shape=[
            shape((parts * rows, blocks * 2 * half), F32) for blocks, rows, _, _ in sections
        ]
        + [shape((1, parts * rows), F32) for _, rows, weight, _ in sections if weight is not None],
        compiler_params=params(32),
        cost_estimate=cost(1 << 20, 8 * own[0].size * parts),
        name="join_shares",
    )(ids, *own, *other, *extra_args)


def swap(value, *bits):
    frames, videos = lax.axis_size("frame"), lax.axis_size("video")
    pairs = []
    for f in range(frames):
        frame_bits, video_bits = bits[f % len(bits)]
        for v in range(videos):
            pairs.append((f * videos + v, (f ^ frame_bits) * videos + (v ^ video_bits)))
    return lax.ppermute(value, BOTH, pairs)


CORE = ((1, 0),)
ACROSS = ((2, 0),)
FIRST = ((0, 1), (2, 0))
SECOND = ((2, 0), (0, 1))


def spread(value, axis, bits):
    return jnp.stack([value] + [swap(value, bit) for bit in bits], axis=axis)


def bits_of(name):
    frames, videos = lax.axis_size("frame"), lax.axis_size("video")
    return {
        "core": [(1, 0)],
        "y": [(2 * y, 0) for y in range(1, frames // 2)],
        "x": [(0, 1)],
        "z": [(0, 2 * z) for z in range(1, videos // 2)],
    }[name]


class Gather:
    def __init__(self, value):
        self.value = value

    def start(self, axis, name):
        self.axis = axis
        self.moved = [swap(self.value, bit) for bit in bits_of(name)]
        return [self.value]

    def finish(self, after=None):
        moved = self.moved if after is None else tie(self.moved, after)
        self.value = jnp.stack([self.value] + moved, axis=self.axis)
        return [self.value]


def wide(value):
    return value.astype(F32)


def add_low(*values):
    return functools.reduce(jnp.add, [wide(v) for v in values]).astype(LOW)


def tie(values, after):
    return lax.optimization_barrier((values, after))[0]


class Share:
    def __init__(self, keep, send):
        self.keep, self.send = keep, send

    def move(self, sends, bits):
        self.moved = [swap(send, *bit) for send, bit in zip(sends, bits)]
        return sends

    def hold(self, after):
        self.moved = tie(self.moved, after)
        return self

    def core_swap(self):
        self.sums = [self.keep]
        return self.move([self.send], [CORE])

    def halve(self, bits):
        sums = self.sums + self.moved
        self.sums = [s[0] for s in sums]
        return self.move([add_low(*[s[1] for s in sums])], [bits])

    def first_swap(self):
        return self.halve(FIRST)

    def second_swap(self):
        return self.halve(SECOND)

    def z_scatter(self):
        sums = self.sums + self.moved
        self.sums = [s[0] for s in sums]
        zs = range(1, lax.axis_size("video") // 2)
        return self.move([add_low(*[s[z] for s in sums]) for z in zs], [((0, 2 * z),) for z in zs])

    def total(self):
        total = add_low(*self.sums, *self.moved)
        bit = 4
        while bit < lax.axis_size("frame"):
            total = lax.optimization_barrier(total)
            total = add_low(total, swap(total, (bit, 0)))
            bit *= 2
        return flat(lax.optimization_barrier(total))


class Join:
    def __init__(self, total):
        self.own = [total]
        self.moved = [swap(total, *ACROSS), swap(total, *CORE), swap(total, (3, 0))]

    def hold(self, after):
        self.moved = tie(self.moved, after)
        return self

    def parts(self):
        across, core, both = self.moved
        return self.own + [across], [core, both]


def flat(value):
    return value.reshape(-1, value.shape[-1])


def on_device(
    frames,
    out_cotangent,
    frame_counts,
    message_proj,
    message_gain,
    message_qkv,
    message_out,
    attn_gain,
    attn_qkv,
    attn_out,
    mlp_gain,
    mlp_up,
    mlp_down,
):
    videos, slots, patches, width = frames.shape
    tokens = patches + 1
    padded = -(-tokens // 16) * 16
    frame_total = videos * slots
    row_total = frame_total * padded
    frame_axis, video_axis = lax.axis_size("frame"), lax.axis_size("video")
    frame_index, video_index = lax.axis_index("frame"), lax.axis_index("video")
    share = width // video_axis
    ids = jnp.stack([frame_index & 1, video_index, frame_index >> 1]).astype(jnp.int32)
    slot_ids = frame_index * slots + jnp.arange(slots, dtype=jnp.int32)
    alive = (slot_ids[None, :] < frame_counts[:, None]).astype(F32).reshape(frame_total)
    gains = [g.reshape(1, width) for g in (message_gain, attn_gain, mlp_gain)]
    tokens_in = frames.transpose(0, 2, 1, 3)
    cotangent = out_cotangent.transpose(0, 2, 1, 3)

    class_rows = tokens_in[:, 0].reshape(frame_total, width)
    flags = jnp.broadcast_to(alive.astype(LOW)[:, None], (frame_total, 128))
    sizes = (frame_axis * frame_total, slots, videos)
    payload = jnp.concatenate([class_rows, flags], axis=1)
    near = spread(spread(payload, 0, bits_of("y")), 0, bits_of("core")).reshape(-1, width + 128)

    step = min(2, slots)
    one, triple, final = frame_project(
        alive, tokens_in, cotangent, gains[1], attn_qkv, padded, step
    )
    message_two, one_rows, triple_rows = message_token(
        sizes, near, gains[0], message_proj, message_qkv, message_out, gains[1], attn_qkv
    )
    message_two = message_two[:frame_total]
    one = lax.dynamic_update_slice(one, one_rows[:frame_total, None], (0, patches, 0))
    triple = lax.dynamic_update_slice(triple, triple_rows[:frame_total, None], (0, patches, 0))
    context, logs, hidden, two = frame_attend(
        tokens_in, message_two, triple, gains[2], attn_out, step
    )
    (
        encoded, hidden_grad, hidden_low, up_keep, up_send, down_keep, down_send,
    ) = feed_forward(
        ids,
        alive,
        hidden.reshape(row_total, width),
        two.reshape(row_total, width),
        final.reshape(row_total, width),
        context.reshape(row_total, width),
        gains[2],
        mlp_up,
        mlp_down,
        (videos, patches, slots, padded),
        video_axis,
    )
    up_share, down_share = Share(up_keep, up_send), Share(down_keep, down_send)

    hidden_low = hidden_low.reshape(frame_total, padded, width)
    hidden_grad = hidden_grad.reshape(frame_total, padded, width)
    first_steps = max(1, frame_total // step // 2)
    up_share.core_swap(), down_share.core_swap()
    triple_grad = frame_backward(
        hidden_low, triple, logs, attn_out, tokens, step, 0, first_steps
    )
    up_share.hold(triple_grad)
    triple_grad = frame_backward(
        hidden_low, triple, logs, attn_out, tokens, step, first_steps,
        frame_total // step - first_steps, triple_grad, up_share.first_swap(),
    )
    up_share.hold(triple_grad), down_share.hold(triple_grad)
    waits = up_share.second_swap() + down_share.first_swap()
    two_rows = message_rows(
        triple_grad[:, patches], message_two, hidden_grad[:, patches], gains[1], attn_qkv
    )
    one_flat, grad_flat = one.reshape(row_total, width), triple_grad.reshape(row_total, 3 * width)
    gather, parts = Gather(jnp.concatenate([payload, two_rows], axis=1)), ()
    for third, (axis, name) in enumerate([(0, "z"), (1, "y"), (0, "x")]):
        waits = waits + gather.start(axis, name)
        parts = qkv_weight_grad(ids, one_flat, grad_flat, video_axis, third, parts, waits)
        gather.finish(parts)
        waits = []
    gather.start(2, "core")
    qkv_share = Share(*parts)
    qkv_share.core_swap()
    up_share.hold(parts), down_share.hold(parts)
    waits = up_share.z_scatter() + down_share.second_swap()
    gathered = gather.finish()[0]
    class_grad, message_gain_grad, proj_sum, mqkv_sum, message_out_sum = message_backward(
        sizes, ids, gathered.reshape(-1, gathered.shape[-1]), gains[0], message_proj, message_qkv,
        message_out, share, waits,
    )
    up_share.hold(class_grad), down_share.hold(class_grad), qkv_share.hold(class_grad)
    up_total = up_share.total()
    waits = [up_total] + down_share.z_scatter() + qkv_share.first_swap()
    class_grad = class_grad[:frame_total].reshape(videos, slots, width)
    stream_grad = stream_backward(
        tokens_in, hidden_grad, triple_grad, class_grad, gains[1], attn_qkv, step, 0, 1, None, waits
    )
    down_share.hold(stream_grad), qkv_share.hold(stream_grad)
    feed_total = jnp.concatenate([up_total, down_share.total()], axis=0)
    feed_join = Join(feed_total)
    waits = [feed_total] + qkv_share.second_swap()
    stream_grad = stream_backward(
        tokens_in, hidden_grad, triple_grad, class_grad, gains[1], attn_qkv, step, 1, videos - 1,
        stream_grad, waits,
    )
    feed_join.hold(stream_grad), qkv_share.hold(stream_grad)
    waits = qkv_share.z_scatter()
    cut = video_index * share

    def own_gain(gain):
        return lax.dynamic_slice(gain, (0, cut), (1, share))

    half_share = share // 2
    up_sum, out_sum, down_sum, mlp_gain_sum = join_shares(
        ids, *feed_join.parts(),
        [
            (mlp_up.shape[1] // width, half_share, mlp_up, own_gain(gains[2])),
            (1, half_share, None, None),
            (1, mlp_down.shape[0] // video_axis // 2, None, None),
        ],
    )
    qkv_sum, attn_gain_sum = join_shares(
        ids, *Join(qkv_share.total()).parts(), [(3, half_share, attn_qkv, own_gain(gains[1]))]
    )
    message_gain_sum = lax.dynamic_slice(message_gain_grad[0], (cut,), (share,))
    attn_gain_sum, mlp_gain_sum = attn_gain_sum[0], mlp_gain_sum[0]
    return (
        encoded.transpose(0, 2, 1, 3),
        stream_grad.transpose(0, 2, 1, 3),
        proj_sum,
        message_gain_sum,
        mqkv_sum,
        message_out_sum,
        attn_gain_sum,
        qkv_sum,
        out_sum,
        mlp_gain_sum,
        up_sum,
        down_sum,
    )


def solution(mesh):
    return jax.shard_map(
        on_device,
        mesh=mesh,
        in_specs=(
            P("video", "frame", None, None),
            P("video", "frame", None, None),
            P("video"),
            P(),
            P(),
            P(),
            P(),
            P(),
            P(),
            P(),
            P(),
            P(),
            P(),
        ),
        out_specs=(
            P("video", "frame", None, None),
            P("video", "frame", None, None),
            P("video", None),
            P("video"),
            P("video", None),
            P("video", None),
            P("video"),
            P("video", None),
            P("video", None),
            P("video"),
            P("video", None),
            P("video", None),
        ),
        check_vma=False,
    )
```

```python
import functools
import math

import jax
import jax.numpy as jnp
from jax import lax
from jax.experimental import pallas as pl
from jax.experimental.pallas import tpu as pltpu
from jax.sharding import PartitionSpec as P

H = 12
HD = 64
EPSILON = 1e-05
LOW = jnp.bfloat16
F32 = jnp.float32
BOTH = ("frame", "video")
SCALE = 1.0 / math.sqrt(HD)
PAIR = 2 * HD
PAIRS = H // 2
LOG_ROWS = 16
MESSAGE_TILE = 256


def dot_nn(left, right):
    return lax.dot_general(
        left, right, (((1,), (0,)), ((), ())), preferred_element_type=F32
    )


def dot_nt(left, right):
    return lax.dot_general(
        left, right, (((1,), (1,)), ((), ())), preferred_element_type=F32
    )


def dot_tn(left, right):
    return lax.dot_general(
        left, right, (((0,), (0,)), ((), ())), preferred_element_type=F32
    )


def normalise(value):
    centred = value - jnp.mean(value, axis=-1, keepdims=True)
    inverse = lax.rsqrt(jnp.mean(centred * centred, axis=-1, keepdims=True) + EPSILON)
    return centred * inverse, inverse


def norm_back(upstream, normal, inverse, gain):
    scaled = upstream * gain
    inner = (
        scaled
        - jnp.mean(scaled, axis=-1, keepdims=True)
        - normal * jnp.mean(scaled * normal, axis=-1, keepdims=True)
    )
    return inner * inverse


def half_masks():
    first = lax.broadcasted_iota(jnp.int32, (1, PAIR), 1) < HD
    plain = (jnp.where(first, 1.0, 0.0).astype(LOW), jnp.where(first, 0.0, 1.0).astype(LOW))
    scaled = (jnp.where(first, SCALE, 0.0).astype(LOW), jnp.where(first, 0.0, SCALE).astype(LOW))
    return plain, scaled


def pair_forward(query, key, value, bias, masks):
    plain, scaled = masks
    context, logs = None, []
    for one, by in zip(plain, scaled):
        score = dot_nt(key, query * by) + bias
        top = jnp.max(score, axis=0, keepdims=True)
        raised = jnp.exp(score - top)
        total = jnp.sum(raised, axis=0, keepdims=True)
        prob_low = (raised * (1.0 / total)).astype(LOW)
        logs.append(top + jnp.log(total))
        part = dot_tn(prob_low, value * one)
        context = part if context is None else context + part
    return context, logs


def pair_backward(query, key, value, grad, logs, bias, masks):
    plain, scaled = masks
    query_grad = key_grad = value_grad = None
    for one, by, log in zip(plain, scaled, logs):
        query_by, grad_one, key_by = query * by, grad * one, key * by
        prob = jnp.exp(dot_nt(key, query_by) + bias - log)
        prob_grad = dot_nt(value, grad_one)
        inner = jnp.sum(prob * prob_grad, axis=0, keepdims=True)
        score_low = (prob * (prob_grad - inner)).astype(LOW)
        parts = (
            dot_tn(score_low, key_by),
            dot_nn(score_low, query_by),
            dot_nn(prob.astype(LOW), grad_one),
        )
        if query_grad is None:
            query_grad, key_grad, value_grad = parts
        else:
            query_grad, key_grad, value_grad = (
                query_grad + parts[0],
                key_grad + parts[1],
                value_grad + parts[2],
            )
    return query_grad, key_grad, value_grad


def heads_forward(read, write, write_log, width, bias):
    masks = half_masks()
    for pair in range(PAIRS):
        at = pair * PAIR
        context, pair_logs = pair_forward(
            read(at), read(width + at), read(2 * width + at), bias, masks
        )
        write(at, context.astype(LOW))
        for head in range(2):
            write_log(2 * pair + head, pair_logs[head])


def heads_backward(read, read_grad, read_log, write, width, bias):
    masks = half_masks()
    for pair in range(PAIRS):
        at = pair * PAIR
        grads = pair_backward(
            read(at),
            read(width + at),
            read(2 * width + at),
            read_grad(at),
            (read_log(2 * pair), read_log(2 * pair + 1)),
            bias,
            masks,
        )
        for part in range(3):
            write(part * width + at, grads[part].astype(LOW))


def key_bias(tokens, padded):
    return jnp.where(lax.broadcasted_iota(jnp.int32, (padded, 1), 0) < tokens, 0.0, -1e30)


def message_bias(flag, per_index, slots, videos):
    rows = flag.shape[0]
    row = lax.broadcasted_iota(jnp.int32, (rows, rows), 0)
    column = lax.broadcasted_iota(jnp.int32, (rows, rows), 1)
    same = (row // per_index == column // per_index) & (
        (row // slots) % videos == (column // slots) % videos
    )
    first = (lax.broadcasted_iota(jnp.int32, (rows, 128), 1) == 0).astype(LOW)
    alive = dot_nt(flag, first) > 0.5
    return jnp.where(same & alive, 0.0, -1e30)


WHOLE = pl.BlockSpec(memory_space=pltpu.VMEM)
SCALARS = pl.BlockSpec(memory_space=pltpu.SMEM)
ANY = pl.BlockSpec(memory_space=pl.ANY)


def held(array):
    zeros = (0,) * array.ndim
    return pl.BlockSpec(array.shape, lambda *_: zeros, pipeline_mode=pl.Buffered(1))


def far(array):
    return pltpu.with_memory_space_constraint(array, pltpu.HBM)


def params(megabytes):
    return pltpu.CompilerParams(vmem_limit_bytes=megabytes << 20)


def cost(macs, moved, raised=0):
    return pl.CostEstimate(flops=2 * macs * 8, bytes_accessed=moved * 8, transcendentals=raised)


def shape(dims, dtype):
    return jax.ShapeDtypeStruct(dims, dtype)


def message_forward(sizes, payload, gain, proj, qkv, out, after=()):
    rows, wide = payload.shape
    width = proj.shape[0]
    tile = min(MESSAGE_TILE, rows)

    def body(pay, gain, proj, qkv, out, *rest):
        pre_o, low_o, qkv_o, log_o, context_o = rest[len(after) :]
        pre = dot_nn(pay[:, :width], proj[...])
        pre_o[...] = pre
        normal, _ = normalise(pre)
        message = normal * gain[...]
        low = message.astype(LOW)
        low_o[...] = low
        qkv_o[...] = dot_nn(low, qkv[...]).astype(LOW)
        bias = message_bias(pay[:, width:], *sizes)

        def write(at, value):
            context_o[:, at : at + PAIR] = value

        def write_log(head, value):
            log_o[head : head + 1, :] = value

        heads_forward(lambda at: qkv_o[:, at : at + PAIR], write, write_log, width, bias)

    def block(lanes):
        return pl.BlockSpec((tile, lanes), lambda i: (i, 0))

    return pl.pallas_call(
        body,
        grid=(rows // tile,),
        in_specs=[block(wide), WHOLE, held(proj), held(qkv), held(out)] + [ANY] * len(after),
        out_specs=[
            block(width), block(width), block(3 * width),
            pl.BlockSpec((LOG_ROWS, tile), lambda i: (0, i)), block(width),
        ],
        out_shape=[
            shape((rows, width), F32),
            shape((rows, width), LOW),
            shape((rows, 3 * width), LOW),
            shape((LOG_ROWS, rows), F32),
            shape((rows, width), LOW),
        ],
        compiler_params=params(48),
        cost_estimate=cost(5 * rows * width * width, 12 * width * width + 20 * rows * width),
        name="message_forward",
    )(payload, gain, far(proj), far(qkv), far(out), *after)


def message_token(sizes, payload, gain, proj, qkv, out, next_gain, next_qkv):
    rows, wide = payload.shape
    width = proj.shape[0]

    def body(pay, gain, proj, qkv, out, next_gain, next_qkv, two_o, one_o, triple_o, rows_s, context_s):
        message = normalise(dot_nn(pay[:, :width], proj[...]))[0] * gain[...]
        rows_s[...] = dot_nn(message.astype(LOW), qkv[...]).astype(LOW)
        bias = message_bias(pay[:, width:], *sizes)

        def write(at, value):
            context_s[:, at : at + PAIR] = value

        heads_forward(
            lambda at: rows_s[:, at : at + PAIR], write, lambda head, value: None, width, bias
        )
        two = message + dot_nn(context_s[...], out[...])
        two_o[...] = two
        one_low = (normalise(two)[0] * next_gain[...]).astype(LOW)
        one_o[...] = one_low.astype(F32)
        triple_o[...] = dot_nn(one_low, next_qkv[...])

    return pl.pallas_call(
        body,
        grid=(1,),
        in_specs=[
            WHOLE, WHOLE, held(proj), held(qkv), held(out), WHOLE, held(next_qkv),
        ],
        out_specs=[WHOLE] * 3,
        out_shape=[shape((rows, width), F32), shape((rows, width), F32), shape((rows, 3 * width), F32)],
        scratch_shapes=[pltpu.VMEM((rows, 3 * width), LOW), pltpu.VMEM((rows, width), LOW)],
        compiler_params=params(48),
        cost_estimate=cost(8 * rows * width * width, 16 * width * width + 20 * rows * width),
        name="message_token",
    )(payload, gain, far(proj), far(qkv), far(out), next_gain, far(next_qkv))


def message_backward(
    sizes, ids, payload, two_low, pre, low, qkv_rows, logs, context, gain, proj, qkv, out, share,
    after=(),
):
    rows, wide = payload.shape
    width = proj.shape[0]
    tile = min(MESSAGE_TILE, rows)

    def body(
        ids, pay, two, pre, low, rows_qkv, log, context, gain, proj, qkv, out, *rest
    ):
        class_o, gain_o, proj_o, qkv_o, out_o, grad_s, triple_s = rest[len(after) :]

        @pl.when(pl.program_id(0) == 0)
        def _():
            gain_o[...] = jnp.zeros_like(gain_o)
            proj_o[...] = jnp.zeros_like(proj_o)
            qkv_o[...] = jnp.zeros_like(qkv_o)
            out_o[...] = jnp.zeros_like(out_o)

        pick = lax.broadcasted_iota(jnp.int32, (width, share), 0) == (
            lax.broadcasted_iota(jnp.int32, (width, share), 1) + ids[1] * share
        )
        pick = jnp.where(pick, 1.0, 0.0).astype(LOW)
        two_rows = two[...]
        grad_s[...] = dot_nt(two_rows, out[...]).astype(LOW)
        out_o[...] += dot_tn(dot_nn(context[...], pick).astype(LOW), two_rows)
        bias = message_bias(pay[:, width:], *sizes)

        def write(at, value):
            triple_s[:, at : at + PAIR] = value

        heads_backward(
            lambda at: rows_qkv[:, at : at + PAIR],
            lambda at: grad_s[:, at : at + PAIR],
            lambda head: log[head : head + 1, :],
            write,
            width,
            bias,
        )
        triple = triple_s[...]
        qkv_o[...] += dot_tn(dot_nn(low[...], pick).astype(LOW), triple)
        upstream = two_rows.astype(F32) + dot_nt(triple, qkv[...])
        normal, inverse = normalise(pre[...])
        gain_o[...] += jnp.sum(upstream * normal, axis=0, keepdims=True)
        pre_low = norm_back(upstream, normal, inverse, gain[...]).astype(LOW)
        proj_o[...] += dot_tn(dot_nn(pay[:, :width], pick).astype(LOW), pre_low)
        class_o[...] = dot_nt(pre_low, proj[...])

    def block(lanes):
        return pl.BlockSpec((tile, lanes), lambda i: (i, 0))

    def fixed(dims):
        return pl.BlockSpec(dims, lambda i: (0, 0))

    return pl.pallas_call(
        body,
        grid=(rows // tile,),
        in_specs=[
            SCALARS, block(wide), block(width), block(width), block(width), block(3 * width),
            pl.BlockSpec((LOG_ROWS, tile), lambda i: (0, i)), block(width), WHOLE,
            held(proj), held(qkv), held(out),
        ]
        + [ANY] * len(after),
        out_specs=[
            block(width), fixed((1, width)), fixed((share, width)), fixed((share, 3 * width)),
            fixed((share, width)),
        ],
        out_shape=[
            shape((rows, width), F32),
            shape((1, width), F32),
            shape((share, width), F32),
            shape((share, 3 * width), F32),
            shape((share, width), F32),
        ],
        scratch_shapes=[pltpu.VMEM((tile, width), LOW), pltpu.VMEM((tile, 3 * width), LOW)],
        compiler_params=params(48),
        cost_estimate=cost(8 * rows * width * width, 16 * width * width + 20 * rows * width),
        name="message_backward",
    )(
        ids, payload, two_low, pre, low, qkv_rows, logs, context, gain, far(proj), far(qkv), far(out),
        *after,
    )


def frame_project(alive, tokens_in, cotangent, gain, qkv, padded, step):
    videos, patches, slots, width = tokens_in.shape
    frames = videos * slots
    per = slots // step
    rows = step * padded

    def body(alive, tokens, grads, gain, qkv, one_o, qkv_o, final_o, split_s, stream_s, grad_s):
        index = pl.program_id(0)
        video, part = index // per, index % per

        @pl.when(index == 0)
        def _():
            stream_s[...] = jnp.zeros_like(stream_s)
            grad_s[...] = jnp.zeros_like(grad_s)

        @pl.when(part == 0)
        def _():
            split_s[...] = tokens[0].astype(F32)
            for slot in range(slots):
                stream_s[slot, :patches, :] = split_s[:, slot, :]
            split_s[...] = grads[0].astype(F32)
            for slot in range(slots):
                grad_s[:patches, :] = split_s[:, slot, :] * alive[video * slots + slot]
                final_o[slot] = grad_s[...].astype(LOW)

        stream = stream_s[pl.ds(part * step, step)].reshape(rows, width)
        one_low = (normalise(stream)[0] * gain[...]).astype(LOW)
        one_o[...] = one_low.reshape(step, padded, width)
        for third in range(3):
            cut = slice(third * width, (third + 1) * width)
            qkv_o[:, :, cut] = dot_nn(one_low, qkv[:, cut]).astype(LOW).reshape(step, padded, width)

    def block(lanes):
        return pl.BlockSpec((step, padded, lanes), lambda i: (i, 0, 0))

    per_video = pl.BlockSpec((1, patches, slots, width), lambda i: (i // per, 0, 0, 0))
    return pl.pallas_call(
        body,
        grid=(frames // step,),
        in_specs=[SCALARS, per_video, per_video, WHOLE, held(qkv)],
        out_specs=[
            block(width), block(3 * width),
            pl.BlockSpec((slots, padded, width), lambda i: (i // per, 0, 0)),
        ],
        out_shape=[
            shape((frames, padded, width), LOW),
            shape((frames, padded, 3 * width), LOW),
            shape((frames, padded, width), LOW),
        ],
        scratch_shapes=[
            pltpu.VMEM((patches, slots, width), F32),
            pltpu.VMEM((slots, padded, width), F32),
            pltpu.VMEM((padded, width), F32),
        ],
        compiler_params=params(50),
        cost_estimate=cost(4 * frames * padded * width * width, 16 * frames * padded * width),
        name="frame_project",
    )(alive, far(tokens_in), far(cotangent), gain, far(qkv))


def frame_attend(tokens_in, message, message_one, message_qkv, one, qkv_rows, gain, out, step, after=()):
    videos, patches, slots, width = tokens_in.shape
    frames, padded, _ = qkv_rows.shape
    per = slots // step
    rows = step * padded

    def body(
        tokens, message, message_one, message_qkv, one, rows_qkv, gain, out, *rest
    ):
        one_o, full_o, context_o, log_o, hidden_o, two_o, split_s, stream_s = rest[len(after) :]
        index = pl.program_id(0)
        video, part = index // per, index % per

        @pl.when(index == 0)
        def _():
            stream_s[...] = jnp.zeros_like(stream_s)

        @pl.when(part == 0)
        def _():
            split_s[...] = tokens[0].astype(F32)
            for slot in range(slots):
                stream_s[slot, :patches, :] = split_s[:, slot, :]
                stream_s[slot, patches : patches + 1, :] = message[pl.ds(video * slots + slot, 1), :]

        here = lax.broadcasted_iota(jnp.int32, (padded, 1), 0) == patches
        for frame in range(step):
            row = message_one[pl.ds(index * step + frame, 1), :]
            one_o[frame] = jnp.where(here, row, one[frame].astype(F32)).astype(LOW)
            row = message_qkv[pl.ds(index * step + frame, 1), :]
            full_o[frame] = jnp.where(here, row, rows_qkv[frame].astype(F32)).astype(LOW)
        bias = key_bias(patches + 1, padded)
        for frame in range(step):

            def read(at):
                return full_o[frame, :, at : at + PAIR]

            def write(at, value):
                context_o[frame, :, at : at + PAIR] = value

            def write_log(head, value):
                log_o[frame, head : head + 1, :] = value

            heads_forward(read, write, write_log, width, bias)
        stream = stream_s[pl.ds(part * step, step)].reshape(rows, width)
        hidden = stream + dot_nn(context_o[...].reshape(rows, width), out[...])
        hidden_o[...] = hidden.reshape(step, padded, width)
        two_o[...] = (normalise(hidden)[0] * gain[...]).astype(LOW).reshape(step, padded, width)

    def block(lanes):
        return pl.BlockSpec((step, padded, lanes), lambda i: (i, 0, 0))

    per_video = pl.BlockSpec((1, patches, slots, width), lambda i: (i // per, 0, 0, 0))
    return pl.pallas_call(
        body,
        grid=(frames // step,),
        in_specs=[
            per_video, WHOLE, WHOLE, WHOLE, block(width), block(3 * width), WHOLE, held(out),
        ]
        + [ANY] * len(after),
        out_specs=[
            block(width), block(3 * width), block(width), pl.BlockSpec((step, LOG_ROWS, padded), lambda i: (i, 0, 0)),
            block(width), block(width),
        ],
        out_shape=[
            shape((frames, padded, width), LOW),
            shape((frames, padded, 3 * width), LOW),
            shape((frames, padded, width), LOW),
            shape((frames, LOG_ROWS, padded), F32),
            shape((frames, padded, width), F32),
            shape((frames, padded, width), LOW),
        ],
        scratch_shapes=[
            pltpu.VMEM((patches, slots, width), F32),
            pltpu.VMEM((slots, padded, width), F32),
        ],
        compiler_params=params(52),
        cost_estimate=cost(8 * frames * padded * width * width, 24 * frames * padded * width),
        name="frame_attend",
    )(
        far(tokens_in), message, message_one, message_qkv, far(one), far(qkv_rows), gain, far(out), *after
    )


def place_of(index, part, core, ids):
    away = index ^ ids[1]
    x, y = away & 1, part ^ (ids[2] & 1)
    straight = core == 0
    return jnp.where(straight, x, y), jnp.where(straight, y, x), away >> 1


def place_shares(ref, value, core, ids, count):
    rows = value.shape[0] // count // 2
    for index in range(count):
        for part in range(2):
            at = (2 * index + part) * rows
            first, second, z = place_of(index, part, core, ids)
            ref[first, second, z, 0] = value[at : at + rows]


def pitch_of(rows):
    return -(-rows // 16) * 16


def store_shares(full, keep, send, core, place):
    half = full.shape[1] // 2
    left, right = full[:, :half].astype(LOW), full[:, half:].astype(LOW)
    first = core == 0
    place(keep, jnp.where(first, left, right), core)
    place(send, jnp.where(first, right, left), 1 - core)


def feed_forward(ids, alive, hidden, two, final, context, gain, up, down, dims, count, after=()):
    videos, patches, slots, padded = dims
    rows, width = hidden.shape
    inner = up.shape[1]
    blocks = inner // width
    half = width // 2
    step = min(2, slots)
    per = slots // step
    last = blocks - 1
    tile = step * padded
    tails = rows // tile
    share, down_share = width // count, inner // count
    half_share = share // 2
    pitch = pitch_of(half_share)
    per_block = width // down_share
    low_count = per_block // 2

    def body(
        ids, alive, hidden, two, final, context, gain, up, down, *rest
    ):
        encoded_o, grad_o, grad_low_o, keep_o, send_o = rest[len(after) :][:5]
        (
            total_s, back_sum_s, act_s, back_s, join_s, split_s, out_s,
            up_keep, up_send, down_keep, down_send, sem,
        ) = rest[len(after) + 5 :]
        index = pl.program_id(0)
        core = ids[0]

        def up_moves(step):
            rows = pl.ds(pl.multiple_of(jnp.minimum(step, blocks) * pitch, pitch), pitch)
            return [
                pltpu.make_async_copy(
                    stage.at[step % 2], place.at[:, :, :, rows, :], sem.at[step % 2, n]
                )
                for n, (stage, place) in enumerate(((up_keep, keep_o), (up_send, send_o)))
            ]

        def down_moves(step):
            block = jnp.minimum(step, last) ^ ((ids[1] >> 1) // low_count)
            zs = pl.ds(block * low_count, low_count)
            rows = pl.ds((blocks + 1) * pitch, down_share // 2)
            return [
                pltpu.make_async_copy(
                    stage.at[step % 2], place.at[:, :, zs, rows, :], sem.at[step % 2, 2 + n]
                )
                for n, (stage, place) in enumerate(((down_keep, keep_o), (down_send, send_o)))
            ]

        def start(copies):
            for copy in copies:
                copy.start()

        def wait(copies):
            for copy in copies:
                copy.wait()

        def place_rows(ref, value, core):
            rows = half_share
            for at in range(count):
                for part in range(2):
                    first, second, z = place_of(at, part, core, ids)
                    row = (2 * at + part) * rows
                    ref[index % 2, first, second, z, :rows, :] = value[row : row + rows]

        def place_down(ref, value, core):
            for at in range(per_block):
                for part in range(2):
                    row = (2 * at + part) * down_share // 2
                    first, second, z = place_of(at, part, core, ids)
                    ref[index % 2, first, second, z % low_count] = value[row : row + down_share // 2]

        @pl.when(index == 0)
        def _():
            total_s[...] = jnp.zeros_like(total_s)
            back_sum_s[...] = jnp.zeros_like(back_sum_s)
            out_s[...] = jnp.zeros_like(out_s)

        @pl.when(index < blocks)
        def _():
            for part in range(rows // tile):
                cut = slice(part * tile, (part + 1) * tile)
                value = dot_nn(two[cut, :], up[...])
                act_grad = dot_nt(final[cut, :], down[...])
                sigma = 0.5 * jnp.tanh(0.851 * value) + 0.5
                act = value * sigma
                slope = sigma + 1.702 * (act - act * sigma)
                act_low = act.astype(LOW)
                back_low = (act_grad * slope).astype(LOW)
                act_s[cut, :] = act_low
                back_s[cut, :] = back_low
                total_s[cut, :] += dot_nn(act_low, down[...])
                back_sum_s[cut, :] += dot_nt(back_low, up[...])

            @pl.when(index >= 2)
            def _():
                wait(up_moves(index - 2) + down_moves(index - 2))

            store_shares(dot_tn(two[...], back_s[...]), up_keep, up_send, core, place_rows)
            store_shares(dot_tn(act_s[...], final[...]), down_keep, down_send, core, place_down)
            start(up_moves(index) + down_moves(index))

        @pl.when(index >= blocks)
        def _():
            tail = index - blocks

            @pl.when(tail == 0)
            def _():
                for step in range(max(0, blocks - 2), blocks):
                    wait(up_moves(step) + down_moves(step))

            cut = pl.ds(pl.multiple_of(tail * tile, tile), tile)
            value = hidden[...]
            total = (value + total_s[cut, :]).reshape(step, padded, width)
            for frame in range(step):
                join_s[(tail % per) * step + frame] = total[frame, :patches] * alive[tail * step + frame]
            normal, inverse = normalise(value)
            back = norm_back(back_sum_s[cut, :], normal, inverse, gain[...])
            back = final[cut, :].astype(F32) + back
            back_low = back.astype(LOW)
            grad_o[...] = back
            grad_low_o[...] = back_low
            out_s[...] += dot_tn(context[...], back_low)

            @pl.when(tail % per == per - 1)
            def _():
                for slot in range(slots):
                    split_s[:, slot, :] = join_s[slot]
                encoded_o[0] = split_s[...].astype(LOW)

            @pl.when(tail == tails - 1)
            def _():
                store_shares(out_s[...], up_keep, up_send, core, place_rows)
                copies = up_moves(index)
                start(copies)
                wait(copies)

    def tail_of(j):
        return jnp.maximum(j - blocks, 0)

    rows_block = pl.BlockSpec((tile, width), lambda j, ids: (tail_of(j), 0))
    packed = shape((2, 2, count // 2, (blocks + 1) * pitch + down_share // 2, half), LOW)
    up_stage = pltpu.VMEM((2, 2, 2, count // 2, pitch, half), LOW)
    down_stage = pltpu.VMEM((2, 2, 2, low_count, down_share // 2, half), LOW)
    return pl.pallas_call(
        body,
        grid_spec=pltpu.PrefetchScalarGridSpec(
            num_scalar_prefetch=1,
            grid=(blocks + tails,),
            in_specs=[
                SCALARS, rows_block, WHOLE, WHOLE, rows_block, WHOLE,
                pl.BlockSpec((width, width), lambda j, ids: (0, jnp.minimum(j, last))),
                pl.BlockSpec((width, width), lambda j, ids: (jnp.minimum(j, last), 0)),
            ]
            + [ANY] * len(after),
            out_specs=[
                pl.BlockSpec((1, patches, slots, width), lambda j, ids: (tail_of(j) // per, 0, 0, 0)),
                rows_block, rows_block, ANY, ANY,
            ],
            scratch_shapes=[
                pltpu.VMEM((rows, width), F32),
                pltpu.VMEM((rows, width), F32),
                pltpu.VMEM((rows, width), LOW),
                pltpu.VMEM((rows, width), LOW),
                pltpu.VMEM((slots, patches, width), F32),
                pltpu.VMEM((patches, slots, width), F32),
                pltpu.VMEM((width, width), F32),
                up_stage, up_stage, down_stage, down_stage,
                pltpu.SemaphoreType.DMA((2, 4)),
            ],
        ),
        out_shape=[
            shape((videos, patches, slots, width), LOW),
            shape((rows, width), F32),
            shape((rows, width), LOW),
            packed, packed,
        ],
        compiler_params=params(60),
        cost_estimate=cost(8 * rows * width * inner, 8 * width * inner + 20 * rows * width),
        name="feed_forward",
    )(ids, alive, far(hidden), two, final, far(context), gain, far(up), far(down), *after)


def frame_backward(grad_low, qkv_rows, logs, out, tokens, step, first, steps, into=None, after=()):
    frames, padded, width = grad_low.shape
    rows = step * padded
    into = () if into is None else (into,)
    extra = len(into) + len(after)

    def body(grad, rows_qkv, log, out, *rest):
        triple_o, context_s = rest[extra:]
        context_s[...] = (
            dot_nt(grad[...].reshape(rows, width), out[...]).astype(LOW).reshape(step, padded, width)
        )
        bias = key_bias(tokens, padded)
        for frame in range(step):
            def write(at, value):
                triple_o[frame, :, at : at + PAIR] = value

            heads_backward(
                lambda at: rows_qkv[frame, :, at : at + PAIR],
                lambda at: context_s[frame, :, at : at + PAIR],
                lambda head: log[frame, head : head + 1, :],
                write,
                width,
                bias,
            )

    def block(lanes):
        return pl.BlockSpec((step, padded, lanes), lambda i: (i + first, 0, 0))

    return pl.pallas_call(
        body,
        grid=(steps,),
        in_specs=[
            block(width), block(3 * width),
            pl.BlockSpec((step, LOG_ROWS, padded), lambda i: (i + first, 0, 0)), held(out),
        ]
        + [ANY] * extra,
        out_specs=block(3 * width),
        out_shape=shape((frames, padded, 3 * width), LOW),
        scratch_shapes=[pltpu.VMEM((step, padded, width), LOW)],
        input_output_aliases={4: 0} if into else {},
        compiler_params=params(50),
        cost_estimate=cost(20 * steps * rows * width * width, 16 * steps * rows * width),
        name="frame_backward",
    )(far(grad_low), far(qkv_rows), far(logs), far(out), *into, *after)


def qkv_weight_grad(ids, one, triple, count, after=()):
    rows, width = one.shape
    blocks = triple.shape[1] // width
    share, half = width // count, width // 2

    def body(ids, one, triple, *rest):
        keep, send = rest[len(after) :]

        def place_rows(ref, value, core):
            place_shares(ref, value, core, ids, count)

        store_shares(dot_tn(one[...], triple[...]), keep, send, ids[0], place_rows)

    block = pl.BlockSpec((2, 2, count // 2, 1, share // 2, half), lambda j: (0, 0, 0, j, 0, 0))
    out = shape((2, 2, count // 2, blocks, share // 2, half), LOW)
    return pl.pallas_call(
        body,
        grid=(blocks,),
        in_specs=[SCALARS, held(one), pl.BlockSpec((rows, width), lambda j: (0, j))]
        + [ANY] * len(after),
        out_specs=[block, block],
        out_shape=[out, out],
        compiler_params=params(48),
        cost_estimate=cost(3 * rows * width * width, 8 * rows * width + 6 * width * width),
        name="qkv_weight_grad",
    )(ids, far(one), far(triple), *after)


def message_rows(triple, message, grad, at, gain, qkv):
    frames, _, width = grad.shape
    tile = 16

    def body(triple, message, grad, gain, qkv, rows_o, triple_s, grad_s):
        triple_s[...] = triple[...].astype(F32)
        grad_s[...] = grad[...]
        normal, inverse = normalise(message[:frames, :])
        upstream = dot_nt(triple_s[:, at % tile, :].astype(LOW), qkv[...])
        back = norm_back(upstream, normal, inverse, gain[...])
        rows_o[...] = (grad_s[:, at % tile, :] + back).astype(LOW)

    def rows(lanes):
        return pl.BlockSpec((frames, tile, lanes), lambda i: (0, at // tile, 0))

    return pl.pallas_call(
        body,
        grid=(1,),
        in_specs=[rows(3 * width), held(message), rows(width), held(gain), held(qkv)],
        out_specs=pl.BlockSpec((frames, width), lambda i: (0, 0)),
        out_shape=shape((frames, width), LOW),
        scratch_shapes=[
            pltpu.VMEM((frames, tile, 3 * width), F32), pltpu.VMEM((frames, tile, width), F32)
        ],
        compiler_params=params(32),
        cost_estimate=cost(20 * frames * width * width, 6 * width * width),
        name="message_rows",
    )(far(triple), message, far(grad), gain, far(qkv))


def stream_backward(tokens_in, grad, triple, gain, qkv, step, first, steps, into=None, after=()):
    videos, patches, slots, width = tokens_in.shape
    frames, padded, _ = grad.shape
    per = slots // step
    rows = step * padded
    into = () if into is None else (into,)
    extra = len(into) + len(after)

    def body(tokens, grad, triple, gain, qkv, *rest):
        stream_o, split_s, stream_s, back_s = rest[extra:]
        index = pl.program_id(0)
        part = index % per

        @pl.when(index == 0)
        def _():
            stream_s[...] = jnp.zeros_like(stream_s)

        @pl.when(part == 0)
        def _():
            split_s[...] = tokens[0].astype(F32)
            for slot in range(slots):
                stream_s[slot, :patches, :] = split_s[:, slot, :]

        upstream = dot_nt(triple[...].reshape(rows, 3 * width), qkv[...])
        normal, inverse = normalise(stream_s[pl.ds(part * step, step)].reshape(rows, width))
        back = norm_back(upstream, normal, inverse, gain[...]).reshape(step, padded, width)
        back_s[pl.ds(part * step, step)] = grad[...] + back

        @pl.when(part == per - 1)
        def _():
            for slot in range(slots):
                stream_o[0, :, slot, :] = back_s[slot, :patches, :]

    def block(lanes):
        return pl.BlockSpec((step, padded, lanes), lambda i: (i + first * per, 0, 0))

    per_video = pl.BlockSpec((1, patches, slots, width), lambda i: (first + i // per, 0, 0, 0))
    return pl.pallas_call(
        body,
        grid=(steps * per,),
        in_specs=[per_video, block(width), block(3 * width), WHOLE, held(qkv)] + [ANY] * extra,
        out_specs=per_video,
        out_shape=shape((videos, patches, slots, width), F32),
        scratch_shapes=[
            pltpu.VMEM((patches, slots, width), F32),
            pltpu.VMEM((slots, padded, width), F32),
            pltpu.VMEM((slots, padded, width), F32),
        ],
        input_output_aliases={5: 0} if into else {},
        compiler_params=params(50),
        cost_estimate=cost(6 * steps * per * rows * width * width, 16 * steps * per * rows * width),
        name="stream_backward",
    )(far(tokens_in), far(grad), far(triple), gain, far(qkv), *into, *after)


def join_shares(ids, own, other, sections, after=(), through=None):
    passed = () if through is None else (through,)
    parts = len(own)
    half = own[0].shape[1]
    extra = [(w, g) for _, _, _, w, g in sections if w is not None]

    def body(ids, *refs):
        own_r, other_r = refs[:parts], refs[parts : 2 * parts]
        extra_r = refs[2 * parts : 2 * parts + 2 * len(extra)]
        at = 2 * parts + 2 * len(extra)
        outs = refs[at + len(after) + len(passed) : -1]
        column_s = refs[-1]
        if passed:
            outs[-1][...] = refs[at][...]
        first = ids[0] == 0
        y = ids[2] & 1

        def pick(pieces, part, cut):
            value = pieces[0][cut, :]
            for away in range(1, parts):
                value = jnp.where((part ^ y) == away, pieces[away][cut, :], value)
            return value

        at = given = 0
        for index, (blocks, rows, pitch, weight, _) in enumerate(sections):
            for part in range(parts):
                to = slice(part * rows, (part + 1) * rows)
                total = jnp.zeros((rows, 1), F32)
                for block in range(blocks):
                    cut = slice(at + block * pitch, at + block * pitch + rows)
                    mine, theirs = pick(own_r, part, cut), pick(other_r, part, cut)
                    sides = (jnp.where(first, mine, theirs), jnp.where(first, theirs, mine))
                    for side, value in enumerate(sides):
                        columns = slice((2 * block + side) * half, (2 * block + side + 1) * half)
                        value = value.astype(F32)
                        outs[index][to, columns] = value
                        if weight is not None:
                            product = value * extra_r[2 * given][to, columns].astype(F32)
                            total += jnp.sum(product, axis=1, keepdims=True)
                column_s[to, :] = jnp.broadcast_to(total, (rows, 128))
            at += blocks * pitch
            if weight is not None:
                sums = column_s[...].T[:1, : parts * rows]
                outs[len(sections) + given][...] = sums / extra_r[2 * given + 1][...]
                given += 1

    extra_specs, extra_args = [], []
    for blocks, rows, _, weight, gain in sections:
        if weight is not None:
            extra_specs += [
                pl.BlockSpec((parts * rows, weight.shape[1]), lambda i, ids: (ids[1], 0)), WHOLE
            ]
            extra_args += [far(weight), gain]
    high = -(-max(parts * rows for _, rows, _, _, _ in sections) // 128) * 128
    return pl.pallas_call(
        body,
        grid_spec=pltpu.PrefetchScalarGridSpec(
            num_scalar_prefetch=1,
            grid=(1,),
            in_specs=[WHOLE] * (2 * parts) + extra_specs + [WHOLE] * len(passed) + [ANY] * len(after),
            out_specs=[WHOLE] * (len(sections) + len(extra) + len(passed)),
            scratch_shapes=[pltpu.VMEM((high, 128), F32)],
        ),
        out_shape=[
            shape((parts * rows, blocks * 2 * half), F32) for blocks, rows, _, _, _ in sections
        ]
        + [shape((1, parts * rows), F32) for _, rows, _, weight, _ in sections if weight is not None]
        + [shape(value.shape, value.dtype) for value in passed],
        compiler_params=params(32),
        cost_estimate=cost(1 << 20, 8 * own[0].size * parts),
        name="join_shares",
    )(ids, *own, *other, *extra_args, *passed, *after)


def swap(value, *bits):
    frames, videos = lax.axis_size("frame"), lax.axis_size("video")
    pairs = []
    for f in range(frames):
        frame_bits, video_bits = bits[f % len(bits)]
        for v in range(videos):
            pairs.append((f * videos + v, (f ^ frame_bits) * videos + (v ^ video_bits)))
    return lax.ppermute(value, BOTH, pairs)


CORE = ((1, 0),)
ACROSS = ((2, 0),)
FIRST = ((0, 1), (2, 0))
SECOND = ((2, 0), (0, 1))


def spread(value, axis, bits):
    return jnp.stack([value] + [swap(value, bit) for bit in bits], axis=axis)


def bits_of(name):
    frames, videos = lax.axis_size("frame"), lax.axis_size("video")
    return {
        "core": [(1, 0)],
        "y": [(2 * y, 0) for y in range(1, frames // 2)],
        "x": [(0, 1)],
        "z": [(0, 2 * z) for z in range(1, videos // 2)],
    }[name]


class Gather:
    def __init__(self, value):
        self.value = value

    def start(self, axis, name):
        self.axis = axis
        self.moved = [swap(self.value, bit) for bit in bits_of(name)]
        return [self.value]

    def finish(self, after=None):
        moved = self.moved if after is None else tie(self.moved, after)
        self.value = jnp.stack([self.value] + moved, axis=self.axis)
        return [self.value]


def wide(value):
    return value.astype(F32)


def add_low(*values):
    return functools.reduce(jnp.add, [wide(v) for v in values]).astype(LOW)


def tie(values, after):
    return lax.optimization_barrier((values, after))[0]


class Share:
    def __init__(self, keep, send):
        self.sums, self.send = [keep], send

    def move(self, send, bits):
        self.moved = [swap(send, *bits)]
        return [send]

    def hold(self, after):
        self.moved = tie(self.moved, after)
        return self

    def core_swap(self):
        return self.move(self.send, CORE)

    def halve(self, bits):
        sums = self.sums + self.moved
        self.sums = [s[0] for s in sums]
        return self.move(add_low(*[s[1] for s in sums]), bits)

    def first_swap(self):
        return self.halve(FIRST)

    def second_swap(self):
        return self.halve(SECOND)

    def z_sends(self):
        sums = self.sums + self.moved
        self.sums, self.moved = [s[0] for s in sums], []
        self.sends = [
            add_low(*[s[z] for s in sums]) for z in range(1, lax.axis_size("video") // 2)
        ]
        return self.sends

    def z_swap(self, zs, after):
        sends = tie([self.sends[z - 1] for z in zs], after)
        self.moved = self.moved + [swap(send, (0, 2 * z)) for send, z in zip(sends, zs)]

    def total(self):
        total = add_low(*self.sums, *self.moved)
        bit = 4
        while bit < lax.axis_size("frame"):
            total = lax.optimization_barrier(total)
            total = add_low(total, swap(total, (bit, 0)))
            bit *= 2
        return lax.optimization_barrier(total)


def rows_of(value, lead):
    return value.reshape(*value.shape[:lead], -1, value.shape[-1])


class Join:
    def __init__(self, total):
        self.own = [total]
        self.moved = [swap(total, *ACROSS), swap(total, *CORE), swap(total, (3, 0))]

    def hold(self, after):
        self.moved = tie(self.moved, after)
        return self

    def parts(self):
        across, core, both = self.moved
        return self.own + [across], [core, both]


def flat(value):
    return value.reshape(-1, value.shape[-1])


def on_device(
    frames,
    out_cotangent,
    frame_counts,
    message_proj,
    message_gain,
    message_qkv,
    message_out,
    attn_gain,
    attn_qkv,
    attn_out,
    mlp_gain,
    mlp_up,
    mlp_down,
):
    videos, slots, patches, width = frames.shape
    tokens = patches + 1
    padded = -(-tokens // 16) * 16
    frame_total = videos * slots
    row_total = frame_total * padded
    frame_axis, video_axis = lax.axis_size("frame"), lax.axis_size("video")
    frame_index, video_index = lax.axis_index("frame"), lax.axis_index("video")
    share = width // video_axis
    ids = jnp.stack([frame_index & 1, video_index, frame_index >> 1]).astype(jnp.int32)
    slot_ids = frame_index * slots + jnp.arange(slots, dtype=jnp.int32)
    alive = (slot_ids[None, :] < frame_counts[:, None]).astype(F32).reshape(frame_total)
    gains = [g.reshape(1, width) for g in (message_gain, attn_gain, mlp_gain)]
    tokens_in = frames.transpose(0, 2, 1, 3)
    cotangent = out_cotangent.transpose(0, 2, 1, 3)

    class_rows = tokens_in[:, 0].reshape(frame_total, width)
    flags = jnp.broadcast_to(alive.astype(LOW)[:, None], (frame_total, 128))
    sizes = (frame_axis * frame_total, slots, videos)
    payload = jnp.concatenate([class_rows, flags], axis=1)
    payload = spread(spread(payload, 0, bits_of("y")), 0, bits_of("core"))
    near = payload.reshape(-1, width + 128)

    step = min(2, slots)
    one, triple, final = frame_project(
        alive, tokens_in, cotangent, gains[1], attn_qkv, padded, step
    )
    classes = Gather(payload)
    classes.start(0, "z")
    message_two, one_rows, triple_rows = message_token(
        sizes, near, gains[0], message_proj, message_qkv, message_out, gains[1], attn_qkv
    )
    waits = classes.finish(message_two)
    classes.start(0, "x")
    one, triple, context, logs, hidden, two = frame_attend(
        tokens_in, message_two, one_rows, triple_rows, one, triple, gains[2], attn_out, step, waits
    )
    waits = classes.finish(two)
    payload = flat(classes.value)
    (
        encoded, hidden_grad, hidden_low, feed_keep, feed_send,
    ) = feed_forward(
        ids,
        alive,
        hidden.reshape(row_total, width),
        two.reshape(row_total, width),
        final.reshape(row_total, width),
        context.reshape(row_total, width),
        gains[2],
        mlp_up,
        mlp_down,
        (videos, patches, slots, padded),
        video_axis,
        waits,
    )

    hidden_low = hidden_low.reshape(frame_total, padded, width)
    hidden_grad = hidden_grad.reshape(frame_total, padded, width)
    feed = Share(feed_keep, feed_send)
    feed.core_swap()
    first_steps = 1
    triple_grad = frame_backward(
        hidden_low, triple, logs, attn_out, tokens, step, 0, first_steps
    )
    waits = feed.hold(triple_grad).first_swap()
    triple_grad = frame_backward(
        hidden_low, triple, logs, attn_out, tokens, step, first_steps,
        frame_total // step - first_steps, triple_grad, waits,
    )
    two_rows = message_rows(
        triple_grad, message_two, hidden_grad, patches, gains[1], attn_qkv
    )
    gather = Gather(two_rows)
    gather.start(0, "z")
    waits = feed.hold(triple_grad).second_swap() + gather.finish()
    keep, send = qkv_weight_grad(
        ids, one.reshape(row_total, width), triple_grad.reshape(row_total, 3 * width), video_axis, waits
    )
    rest = Share(rows_of(keep, 3), rows_of(send, 3))
    rest.core_swap()
    zs = list(range(1, video_axis // 2))
    waits = feed.hold(keep).z_sends()
    feed.z_swap(zs[:1], keep)
    gather.start(1, "y")
    pre, low, qkv_rows, message_logs, mcontext = message_forward(
        sizes, payload, gains[0], message_proj, message_qkv, message_out, waits
    )
    waits = gather.finish(pre) + rest.hold(pre).first_swap()
    gather.start(0, "x")
    feed.hold(pre).z_swap(zs[1:2], pre)
    stream_grad = stream_backward(
        tokens_in, hidden_grad, triple_grad, gains[1], attn_qkv, step, 0, 1, None, waits
    )
    waits = gather.finish(stream_grad) + rest.hold(stream_grad).second_swap()
    gather.start(2, "core")
    feed.hold(stream_grad).z_swap(zs[2:], stream_grad)
    stream_grad = stream_backward(
        tokens_in, hidden_grad, triple_grad, gains[1], attn_qkv, step, 1, videos - 1, stream_grad, waits
    )
    gather.finish(stream_grad)
    feed_total = feed.hold(stream_grad).total()
    feed_join = Join(feed_total)
    waits = [feed_total] + rest.hold(stream_grad).z_sends()
    rest.z_swap(zs[::-1], stream_grad)
    two_rows = flat(gather.value)
    class_grad, message_gain_grad, proj_sum, mqkv_sum, message_out_sum = message_backward(
        sizes, ids, payload, two_rows, pre, low, qkv_rows, message_logs, mcontext,
        gains[0], message_proj, message_qkv, message_out, share, waits,
    )
    feed_join.hold(class_grad), rest.hold(class_grad)
    cut = video_index * share

    def own_gain(gain):
        return lax.dynamic_slice(gain, (0, cut), (1, share))

    half_share = share // 2
    pitch, down_half = pitch_of(half_share), mlp_down.shape[0] // video_axis // 2
    up_sum, out_sum, down_sum, mlp_gain_sum, class_grad = join_shares(
        ids, *feed_join.parts(),
        [
            (mlp_up.shape[1] // width, half_share, pitch, mlp_up, own_gain(gains[2])),
            (1, half_share, pitch, None, None),
            (1, down_half, down_half, None, None),
        ],
        rest.moved,
        class_grad[:frame_total],
    )
    stream_grad = lax.dynamic_update_slice(
        stream_grad,
        stream_grad[:, :1] + class_grad.reshape(videos, 1, slots, width),
        (0, 0, 0, 0),
    )
    qkv_sum, attn_gain_sum = join_shares(
        ids, *Join(rest.total()).parts(), [(3, half_share, half_share, attn_qkv, own_gain(gains[1]))]
    )
    message_gain_sum = lax.dynamic_slice(message_gain_grad[0], (cut,), (share,))
    attn_gain_sum, mlp_gain_sum = attn_gain_sum[0], mlp_gain_sum[0]
    return (
        encoded.transpose(0, 2, 1, 3),
        stream_grad.transpose(0, 2, 1, 3),
        proj_sum,
        message_gain_sum,
        mqkv_sum,
        message_out_sum,
        attn_gain_sum,
        qkv_sum,
        out_sum,
        mlp_gain_sum,
        up_sum,
        down_sum,
    )


def solution(mesh):
    return jax.shard_map(
        on_device,
        mesh=mesh,
        in_specs=(
            P("video", "frame", None, None),
            P("video", "frame", None, None),
            P("video"),
            P(),
            P(),
            P(),
            P(),
            P(),
            P(),
            P(),
            P(),
            P(),
            P(),
        ),
        out_specs=(
            P("video", "frame", None, None),
            P("video", "frame", None, None),
            P("video", None),
            P("video"),
            P("video", None),
            P("video", None),
            P("video"),
            P("video", None),
            P("video", None),
            P("video"),
            P("video", None),
            P("video", None),
        ),
        check_vma=False,
    )
```

```python
import functools
import math

import jax
import jax.numpy as jnp
from jax import lax
from jax.experimental import pallas as pl
from jax.experimental.pallas import tpu as pltpu
from jax.sharding import PartitionSpec as P

H = 12
HD = 64
EPSILON = 1e-05
LOW = jnp.bfloat16
F32 = jnp.float32
BOTH = ("frame", "video")
SCALE = 1.0 / math.sqrt(HD)
PAIR = 2 * HD
PAIRS = H // 2
LOG_ROWS = 16
MESSAGE_TILE = 256


def dot_nn(left, right):
    return lax.dot_general(
        left, right, (((1,), (0,)), ((), ())), preferred_element_type=F32
    )


def dot_nt(left, right):
    return lax.dot_general(
        left, right, (((1,), (1,)), ((), ())), preferred_element_type=F32
    )


def dot_tn(left, right):
    return lax.dot_general(
        left, right, (((0,), (0,)), ((), ())), preferred_element_type=F32
    )


def normalise(value):
    centred = value - jnp.mean(value, axis=-1, keepdims=True)
    inverse = lax.rsqrt(jnp.mean(centred * centred, axis=-1, keepdims=True) + EPSILON)
    return centred * inverse, inverse


def norm_back(upstream, normal, inverse, gain):
    scaled = upstream * gain
    inner = (
        scaled
        - jnp.mean(scaled, axis=-1, keepdims=True)
        - normal * jnp.mean(scaled * normal, axis=-1, keepdims=True)
    )
    return inner * inverse


def half_masks():
    first = lax.broadcasted_iota(jnp.int32, (1, PAIR), 1) < HD
    plain = (jnp.where(first, 1.0, 0.0).astype(LOW), jnp.where(first, 0.0, 1.0).astype(LOW))
    scaled = (jnp.where(first, SCALE, 0.0).astype(LOW), jnp.where(first, 0.0, SCALE).astype(LOW))
    return plain, scaled


def pair_forward(query, key, value, bias, masks):
    plain, scaled = masks
    context, logs = None, []
    for one, by in zip(plain, scaled):
        score = dot_nt(key, query * by) + bias
        top = jnp.max(score, axis=0, keepdims=True)
        raised = jnp.exp(score - top)
        total = jnp.sum(raised, axis=0, keepdims=True)
        prob_low = (raised * (1.0 / total)).astype(LOW)
        logs.append(top + jnp.log(total))
        part = dot_tn(prob_low, value * one)
        context = part if context is None else context + part
    return context, logs


def pair_backward(query, key, value, grad, logs, bias, masks):
    plain, scaled = masks
    query_grad = key_grad = value_grad = None
    for one, by, log in zip(plain, scaled, logs):
        query_by, grad_one, key_by = query * by, grad * one, key * by
        prob = jnp.exp(dot_nt(key, query_by) + bias - log)
        prob_grad = dot_nt(value, grad_one)
        inner = jnp.sum(prob * prob_grad, axis=0, keepdims=True)
        score_low = (prob * (prob_grad - inner)).astype(LOW)
        parts = (
            dot_tn(score_low, key_by),
            dot_nn(score_low, query_by),
            dot_nn(prob.astype(LOW), grad_one),
        )
        if query_grad is None:
            query_grad, key_grad, value_grad = parts
        else:
            query_grad, key_grad, value_grad = (
                query_grad + parts[0],
                key_grad + parts[1],
                value_grad + parts[2],
            )
    return query_grad, key_grad, value_grad


def heads_forward(read, write, write_log, width, bias):
    masks = half_masks()
    for pair in range(PAIRS):
        at = pair * PAIR
        context, pair_logs = pair_forward(
            read(at), read(width + at), read(2 * width + at), bias, masks
        )
        write(at, context.astype(LOW))
        for head in range(2):
            write_log(2 * pair + head, pair_logs[head])


def heads_backward(read, read_grad, read_log, write, width, bias):
    masks = half_masks()
    for pair in range(PAIRS):
        at = pair * PAIR
        grads = pair_backward(
            read(at),
            read(width + at),
            read(2 * width + at),
            read_grad(at),
            (read_log(2 * pair), read_log(2 * pair + 1)),
            bias,
            masks,
        )
        for part in range(3):
            write(part * width + at, grads[part].astype(LOW))


def key_bias(tokens, padded):
    return jnp.where(lax.broadcasted_iota(jnp.int32, (padded, 1), 0) < tokens, 0.0, -1e30)


def message_bias(flag, per_index, slots, videos):
    rows = flag.shape[0]
    row = lax.broadcasted_iota(jnp.int32, (rows, rows), 0)
    column = lax.broadcasted_iota(jnp.int32, (rows, rows), 1)
    same = (row // per_index == column // per_index) & (
        (row // slots) % videos == (column // slots) % videos
    )
    first = (lax.broadcasted_iota(jnp.int32, (rows, 128), 1) == 0).astype(LOW)
    alive = dot_nt(flag, first) > 0.5
    return jnp.where(same & alive, 0.0, -1e30)


WHOLE = pl.BlockSpec(memory_space=pltpu.VMEM)
SCALARS = pl.BlockSpec(memory_space=pltpu.SMEM)
ANY = pl.BlockSpec(memory_space=pl.ANY)


def held(array):
    zeros = (0,) * array.ndim
    return pl.BlockSpec(array.shape, lambda *_: zeros, pipeline_mode=pl.Buffered(1))


def far(array):
    return pltpu.with_memory_space_constraint(array, pltpu.HBM)


def params(megabytes):
    return pltpu.CompilerParams(vmem_limit_bytes=megabytes << 20)


def cost(macs, moved, raised=0):
    return pl.CostEstimate(flops=2 * macs * 8, bytes_accessed=moved * 8, transcendentals=raised)


def shape(dims, dtype):
    return jax.ShapeDtypeStruct(dims, dtype)


def message_forward(sizes, payload, gain, proj, qkv, out, after=()):
    rows, wide = payload.shape
    width = proj.shape[0]
    tile = min(MESSAGE_TILE, rows)

    def body(pay, gain, proj, qkv, out, *rest):
        pre_o, low_o, qkv_o, log_o, context_o = rest[len(after) :]
        pre = dot_nn(pay[:, :width], proj[...])
        pre_o[...] = pre
        normal, _ = normalise(pre)
        message = normal * gain[...]
        low = message.astype(LOW)
        low_o[...] = low
        qkv_o[...] = dot_nn(low, qkv[...]).astype(LOW)
        bias = message_bias(pay[:, width:], *sizes)

        def write(at, value):
            context_o[:, at : at + PAIR] = value

        def write_log(head, value):
            log_o[head : head + 1, :] = value

        heads_forward(lambda at: qkv_o[:, at : at + PAIR], write, write_log, width, bias)

    def block(lanes):
        return pl.BlockSpec((tile, lanes), lambda i: (i, 0))

    return pl.pallas_call(
        body,
        grid=(rows // tile,),
        in_specs=[block(wide), WHOLE, held(proj), held(qkv), held(out)] + [ANY] * len(after),
        out_specs=[
            block(width), block(width), block(3 * width),
            pl.BlockSpec((LOG_ROWS, tile), lambda i: (0, i)), block(width),
        ],
        out_shape=[
            shape((rows, width), F32),
            shape((rows, width), LOW),
            shape((rows, 3 * width), LOW),
            shape((LOG_ROWS, rows), F32),
            shape((rows, width), LOW),
        ],
        compiler_params=params(48),
        cost_estimate=cost(5 * rows * width * width, 12 * width * width + 20 * rows * width),
        name="message_forward",
    )(payload, gain, proj, qkv, out, *after)


def message_token(sizes, payload, gain, proj, qkv, out, next_gain, next_qkv):
    rows, wide = payload.shape
    width = proj.shape[0]

    def body(pay, gain, proj, qkv, out, next_gain, next_qkv, two_o, one_o, triple_o, rows_s, context_s):
        message = normalise(dot_nn(pay[:, :width], proj[...]))[0] * gain[...]
        rows_s[...] = dot_nn(message.astype(LOW), qkv[...]).astype(LOW)
        bias = message_bias(pay[:, width:], *sizes)

        def write(at, value):
            context_s[:, at : at + PAIR] = value

        heads_forward(
            lambda at: rows_s[:, at : at + PAIR], write, lambda head, value: None, width, bias
        )
        two = message + dot_nn(context_s[...], out[...])
        two_o[...] = two
        one_low = (normalise(two)[0] * next_gain[...]).astype(LOW)
        one_o[...] = one_low.astype(F32)
        triple_o[...] = dot_nn(one_low, next_qkv[...])

    return pl.pallas_call(
        body,
        grid=(1,),
        in_specs=[
            WHOLE, WHOLE, held(proj), held(qkv), held(out), WHOLE, held(next_qkv),
        ],
        out_specs=[WHOLE] * 3,
        out_shape=[shape((rows, width), F32), shape((rows, width), F32), shape((rows, 3 * width), F32)],
        scratch_shapes=[pltpu.VMEM((rows, 3 * width), LOW), pltpu.VMEM((rows, width), LOW)],
        compiler_params=params(48),
        cost_estimate=cost(8 * rows * width * width, 16 * width * width + 20 * rows * width),
        name="message_token",
    )(payload, gain, proj, qkv, out, next_gain, next_qkv)


def message_backward(
    sizes, ids, payload, two_low, pre, low, qkv_rows, logs, context, gain, proj, qkv, out, share,
    after=(),
):
    rows, wide = payload.shape
    width = proj.shape[0]
    tile = min(MESSAGE_TILE, rows)

    def body(
        ids, pay, two, pre, low, rows_qkv, log, context, gain, proj, qkv, out, *rest
    ):
        class_o, gain_o, proj_o, qkv_o, out_o, grad_s, triple_s = rest[len(after) :]

        @pl.when(pl.program_id(0) == 0)
        def _():
            gain_o[...] = jnp.zeros_like(gain_o)
            proj_o[...] = jnp.zeros_like(proj_o)
            qkv_o[...] = jnp.zeros_like(qkv_o)
            out_o[...] = jnp.zeros_like(out_o)

        pick = lax.broadcasted_iota(jnp.int32, (width, share), 0) == (
            lax.broadcasted_iota(jnp.int32, (width, share), 1) + ids[1] * share
        )
        pick = jnp.where(pick, 1.0, 0.0).astype(LOW)
        two_rows = two[...]
        grad_s[...] = dot_nt(two_rows, out[...]).astype(LOW)
        out_o[...] += dot_tn(dot_nn(context[...], pick).astype(LOW), two_rows)
        bias = message_bias(pay[:, width:], *sizes)

        def write(at, value):
            triple_s[:, at : at + PAIR] = value

        heads_backward(
            lambda at: rows_qkv[:, at : at + PAIR],
            lambda at: grad_s[:, at : at + PAIR],
            lambda head: log[head : head + 1, :],
            write,
            width,
            bias,
        )
        triple = triple_s[...]
        qkv_o[...] += dot_tn(dot_nn(low[...], pick).astype(LOW), triple)
        upstream = two_rows.astype(F32) + dot_nt(triple, qkv[...])
        normal, inverse = normalise(pre[...])
        gain_o[...] += jnp.sum(upstream * normal, axis=0, keepdims=True)
        pre_low = norm_back(upstream, normal, inverse, gain[...]).astype(LOW)
        proj_o[...] += dot_tn(dot_nn(pay[:, :width], pick).astype(LOW), pre_low)
        class_o[...] = dot_nt(pre_low, proj[...])

    def block(lanes):
        return pl.BlockSpec((tile, lanes), lambda i: (i, 0))

    def fixed(dims):
        return pl.BlockSpec(dims, lambda i: (0, 0))

    return pl.pallas_call(
        body,
        grid=(rows // tile,),
        in_specs=[
            SCALARS, block(wide), block(width), block(width), block(width), block(3 * width),
            pl.BlockSpec((LOG_ROWS, tile), lambda i: (0, i)), block(width), WHOLE,
            held(proj), held(qkv), held(out),
        ]
        + [ANY] * len(after),
        out_specs=[
            block(width), fixed((1, width)), fixed((share, width)), fixed((share, 3 * width)),
            fixed((share, width)),
        ],
        out_shape=[
            shape((rows, width), F32),
            shape((1, width), F32),
            shape((share, width), F32),
            shape((share, 3 * width), F32),
            shape((share, width), F32),
        ],
        scratch_shapes=[pltpu.VMEM((tile, width), LOW), pltpu.VMEM((tile, 3 * width), LOW)],
        compiler_params=params(48),
        cost_estimate=cost(8 * rows * width * width, 16 * width * width + 20 * rows * width),
        name="message_backward",
    )(
        ids, payload, two_low, pre, low, qkv_rows, logs, context, gain, proj, qkv, out,
        *after,
    )


def frame_project(alive, tokens_in, cotangent, gain, qkv, padded, step):
    videos, patches, slots, width = tokens_in.shape
    frames = videos * slots
    per = slots // step
    rows = step * padded

    def body(alive, tokens, grads, gain, qkv, one_o, qkv_o, final_o, inverse_o, split_s, stream_s, grad_s):
        index = pl.program_id(0)
        video, part = index // per, index % per

        @pl.when(index == 0)
        def _():
            stream_s[...] = jnp.zeros_like(stream_s)
            grad_s[...] = jnp.zeros_like(grad_s)

        @pl.when(part == 0)
        def _():
            split_s[...] = tokens[0].astype(F32)
            for slot in range(slots):
                stream_s[slot, :patches, :] = split_s[:, slot, :]
            split_s[...] = grads[0].astype(F32)
            for slot in range(slots):
                grad_s[:patches, :] = split_s[:, slot, :] * alive[video * slots + slot]
                final_o[slot] = grad_s[...].astype(LOW)

        stream = stream_s[pl.ds(part * step, step)].reshape(rows, width)
        normal, inverse = normalise(stream)
        one_low = (normal * gain[...]).astype(LOW)
        one_o[...] = one_low.reshape(step, padded, width)
        inverse_o[...] = jnp.broadcast_to(inverse, (rows, 128)).reshape(step, padded, 128)
        for third in range(3):
            cut = slice(third * width, (third + 1) * width)
            qkv_o[:, :, cut] = dot_nn(one_low, qkv[:, cut]).astype(LOW).reshape(step, padded, width)

    def block(lanes):
        return pl.BlockSpec((step, padded, lanes), lambda i: (i, 0, 0))

    per_video = pl.BlockSpec((1, patches, slots, width), lambda i: (i // per, 0, 0, 0))
    return pl.pallas_call(
        body,
        grid=(frames // step,),
        in_specs=[SCALARS, per_video, per_video, WHOLE, held(qkv)],
        out_specs=[
            block(width), block(3 * width),
            pl.BlockSpec((slots, padded, width), lambda i: (i // per, 0, 0)), block(128),
        ],
        out_shape=[
            shape((frames, padded, width), LOW),
            shape((frames, padded, 3 * width), LOW),
            shape((frames, padded, width), LOW),
            shape((frames, padded, 128), F32),
        ],
        scratch_shapes=[
            pltpu.VMEM((patches, slots, width), F32),
            pltpu.VMEM((slots, padded, width), F32),
            pltpu.VMEM((padded, width), F32),
        ],
        compiler_params=params(50),
        cost_estimate=cost(4 * frames * padded * width * width, 16 * frames * padded * width),
        name="frame_project",
    )(alive, far(tokens_in), far(cotangent), gain, qkv)


def frame_attend(tokens_in, message, message_one, message_qkv, one, qkv_rows, gain, out, step, after=()):
    videos, patches, slots, width = tokens_in.shape
    frames, padded, _ = qkv_rows.shape
    per = slots // step
    rows = step * padded

    def body(
        tokens, message, message_one, message_qkv, one, rows_qkv, gain, out, *rest
    ):
        one_o, full_o, context_o, log_o, hidden_o, two_o, split_s, stream_s = rest[len(after) :]
        index = pl.program_id(0)
        video, part = index // per, index % per

        @pl.when(index == 0)
        def _():
            stream_s[...] = jnp.zeros_like(stream_s)

        @pl.when(part == 0)
        def _():
            split_s[...] = tokens[0].astype(F32)
            for slot in range(slots):
                stream_s[slot, :patches, :] = split_s[:, slot, :]
                stream_s[slot, patches : patches + 1, :] = message[pl.ds(video * slots + slot, 1), :]

        here = lax.broadcasted_iota(jnp.int32, (padded, 1), 0) == patches
        for frame in range(step):
            row = message_one[pl.ds(index * step + frame, 1), :]
            one_o[frame] = jnp.where(here, row, one[frame].astype(F32)).astype(LOW)
            row = message_qkv[pl.ds(index * step + frame, 1), :]
            full_o[frame] = jnp.where(here, row, rows_qkv[frame].astype(F32)).astype(LOW)
        bias = key_bias(patches + 1, padded)
        for frame in range(step):

            def read(at):
                return full_o[frame, :, at : at + PAIR]

            def write(at, value):
                context_o[frame, :, at : at + PAIR] = value

            def write_log(head, value):
                log_o[frame, head : head + 1, :] = value

            heads_forward(read, write, write_log, width, bias)
        stream = stream_s[pl.ds(part * step, step)].reshape(rows, width)
        hidden = stream + dot_nn(context_o[...].reshape(rows, width), out[...])
        hidden_o[...] = hidden.reshape(step, padded, width)
        two_o[...] = (normalise(hidden)[0] * gain[...]).astype(LOW).reshape(step, padded, width)

    def block(lanes):
        return pl.BlockSpec((step, padded, lanes), lambda i: (i, 0, 0))

    per_video = pl.BlockSpec((1, patches, slots, width), lambda i: (i // per, 0, 0, 0))
    return pl.pallas_call(
        body,
        grid=(frames // step,),
        in_specs=[
            per_video, WHOLE, WHOLE, WHOLE, block(width), block(3 * width), WHOLE, held(out),
        ]
        + [ANY] * len(after),
        out_specs=[
            block(width), block(3 * width), block(width), pl.BlockSpec((step, LOG_ROWS, padded), lambda i: (i, 0, 0)),
            block(width), block(width),
        ],
        out_shape=[
            shape((frames, padded, width), LOW),
            shape((frames, padded, 3 * width), LOW),
            shape((frames, padded, width), LOW),
            shape((frames, LOG_ROWS, padded), F32),
            shape((frames, padded, width), F32),
            shape((frames, padded, width), LOW),
        ],
        scratch_shapes=[
            pltpu.VMEM((patches, slots, width), F32),
            pltpu.VMEM((slots, padded, width), F32),
        ],
        compiler_params=params(52),
        cost_estimate=cost(8 * frames * padded * width * width, 24 * frames * padded * width),
        name="frame_attend",
    )(
        far(tokens_in), message, message_one, message_qkv, far(one), far(qkv_rows), gain, out, *after
    )


def place_of(index, part, core, ids):
    away = index ^ ids[1]
    x, y = away & 1, part ^ (ids[2] & 1)
    straight = core == 0
    return jnp.where(straight, x, y), jnp.where(straight, y, x), away >> 1


def place_shares(ref, value, core, ids, count):
    rows = value.shape[0] // count // 2
    for index in range(count):
        for part in range(2):
            at = (2 * index + part) * rows
            first, second, z = place_of(index, part, core, ids)
            ref[first, second, z, 0] = value[at : at + rows]


def pitch_of(rows):
    return -(-rows // 16) * 16


def store_shares(full, keep, send, core, place):
    half = full.shape[1] // 2
    left, right = full[:, :half].astype(LOW), full[:, half:].astype(LOW)
    first = core == 0
    place(keep, jnp.where(first, left, right), core)
    place(send, jnp.where(first, right, left), 1 - core)


def feed_forward(ids, alive, hidden, two, final, context, gain, up, down, dims, count, after=()):
    videos, patches, slots, padded = dims
    rows, width = hidden.shape
    inner = up.shape[1]
    blocks = inner // width
    half = width // 2
    step = min(2, slots)
    per = slots // step
    last = blocks - 1
    tile = step * padded
    tails = rows // tile
    share, down_share = width // count, inner // count
    half_share = share // 2
    pitch = pitch_of(half_share)
    per_block = width // down_share
    low_count = per_block // 2

    def body(
        ids, alive, hidden, two, final, context, gain, up, down, *rest
    ):
        encoded_o, grad_o, grad_low_o, keep_o, send_o = rest[len(after) :][:5]
        (
            total_s, back_sum_s, act_s, back_s, join_s, split_s, out_s,
            up_keep, up_send, down_keep, down_send, sem,
        ) = rest[len(after) + 5 :]
        index = pl.program_id(0)
        core = ids[0]

        def up_moves(step):
            rows = pl.ds(pl.multiple_of(jnp.minimum(step, blocks) * pitch, pitch), pitch)
            return [
                pltpu.make_async_copy(
                    stage.at[step % 2], place.at[:, :, :, rows, :], sem.at[step % 2, n]
                )
                for n, (stage, place) in enumerate(((up_keep, keep_o), (up_send, send_o)))
            ]

        def down_moves(step):
            block = jnp.minimum(step, last) ^ ((ids[1] >> 1) // low_count)
            zs = pl.ds(block * low_count, low_count)
            rows = pl.ds((blocks + 1) * pitch, down_share // 2)
            return [
                pltpu.make_async_copy(
                    stage.at[step % 2], place.at[:, :, zs, rows, :], sem.at[step % 2, 2 + n]
                )
                for n, (stage, place) in enumerate(((down_keep, keep_o), (down_send, send_o)))
            ]

        def start(copies):
            for copy in copies:
                copy.start()

        def wait(copies):
            for copy in copies:
                copy.wait()

        def place_rows(ref, value, core):
            rows = half_share
            for at in range(count):
                for part in range(2):
                    first, second, z = place_of(at, part, core, ids)
                    row = (2 * at + part) * rows
                    ref[index % 2, first, second, z, :rows, :] = value[row : row + rows]

        def place_down(ref, value, core):
            for at in range(per_block):
                for part in range(2):
                    row = (2 * at + part) * down_share // 2
                    first, second, z = place_of(at, part, core, ids)
                    ref[index % 2, first, second, z % low_count] = value[row : row + down_share // 2]

        @pl.when(index == 0)
        def _():
            total_s[...] = jnp.zeros_like(total_s)
            back_sum_s[...] = jnp.zeros_like(back_sum_s)
            out_s[...] = jnp.zeros_like(out_s)

        @pl.when(index < blocks)
        def _():
            for part in range(rows // tile):
                cut = slice(part * tile, (part + 1) * tile)
                value = dot_nn(two[cut, :], up[...])
                act_grad = dot_nt(final[cut, :], down[...])
                sigma = 0.5 * jnp.tanh(0.851 * value) + 0.5
                act = value * sigma
                slope = sigma + 1.702 * (act - act * sigma)
                act_low = act.astype(LOW)
                back_low = (act_grad * slope).astype(LOW)
                act_s[cut, :] = act_low
                back_s[cut, :] = back_low
                total_s[cut, :] += dot_nn(act_low, down[...])
                back_sum_s[cut, :] += dot_nt(back_low, up[...])

            @pl.when(index >= 2)
            def _():
                wait(up_moves(index - 2) + down_moves(index - 2))

            store_shares(dot_tn(two[...], back_s[...]), up_keep, up_send, core, place_rows)
            store_shares(dot_tn(act_s[...], final[...]), down_keep, down_send, core, place_down)
            start(up_moves(index) + down_moves(index))

        @pl.when(index >= blocks)
        def _():
            tail = index - blocks

            @pl.when(tail == 0)
            def _():
                for step in range(max(0, blocks - 2), blocks):
                    wait(up_moves(step) + down_moves(step))

            cut = pl.ds(pl.multiple_of(tail * tile, tile), tile)
            value = hidden[...]
            total = (value + total_s[cut, :]).reshape(step, padded, width)
            for frame in range(step):
                join_s[(tail % per) * step + frame] = total[frame, :patches] * alive[tail * step + frame]
            normal, inverse = normalise(value)
            back = norm_back(back_sum_s[cut, :], normal, inverse, gain[...])
            back = final[cut, :].astype(F32) + back
            back_low = back.astype(LOW)
            grad_o[...] = back
            grad_low_o[...] = back_low
            out_s[...] += dot_tn(context[...], back_low)

            @pl.when(tail % per == per - 1)
            def _():
                for slot in range(slots):
                    split_s[:, slot, :] = join_s[slot]
                encoded_o[0] = split_s[...].astype(LOW)

            @pl.when(tail == tails - 1)
            def _():
                store_shares(out_s[...], up_keep, up_send, core, place_rows)
                copies = up_moves(index)
                start(copies)
                wait(copies)

    def tail_of(j):
        return jnp.maximum(j - blocks, 0)

    rows_block = pl.BlockSpec((tile, width), lambda j, ids: (tail_of(j), 0))
    packed = shape((2, 2, count // 2, (blocks + 1) * pitch + down_share // 2, half), LOW)
    up_stage = pltpu.VMEM((2, 2, 2, count // 2, pitch, half), LOW)
    down_stage = pltpu.VMEM((2, 2, 2, low_count, down_share // 2, half), LOW)
    return pl.pallas_call(
        body,
        grid_spec=pltpu.PrefetchScalarGridSpec(
            num_scalar_prefetch=1,
            grid=(blocks + tails,),
            in_specs=[
                SCALARS, rows_block, WHOLE, WHOLE, rows_block, WHOLE,
                pl.BlockSpec((width, width), lambda j, ids: (0, jnp.minimum(j, last))),
                pl.BlockSpec((width, width), lambda j, ids: (jnp.minimum(j, last), 0)),
            ]
            + [ANY] * len(after),
            out_specs=[
                pl.BlockSpec((1, patches, slots, width), lambda j, ids: (tail_of(j) // per, 0, 0, 0)),
                rows_block, rows_block, ANY, ANY,
            ],
            scratch_shapes=[
                pltpu.VMEM((rows, width), F32),
                pltpu.VMEM((rows, width), F32),
                pltpu.VMEM((rows, width), LOW),
                pltpu.VMEM((rows, width), LOW),
                pltpu.VMEM((slots, patches, width), F32),
                pltpu.VMEM((patches, slots, width), F32),
                pltpu.VMEM((width, width), F32),
                up_stage, up_stage, down_stage, down_stage,
                pltpu.SemaphoreType.DMA((2, 4)),
            ],
        ),
        out_shape=[
            shape((videos, patches, slots, width), LOW),
            shape((rows, width), F32),
            shape((rows, width), LOW),
            packed, packed,
        ],
        compiler_params=params(60),
        cost_estimate=cost(8 * rows * width * inner, 8 * width * inner + 20 * rows * width),
        name="feed_forward",
    )(ids, alive, far(hidden), two, final, far(context), gain, up, down, *after)


def frame_backward(grad_low, qkv_rows, logs, out, tokens, step, first, steps, into=None, after=()):
    frames, padded, width = grad_low.shape
    rows = step * padded
    into = () if into is None else (into,)
    extra = len(into) + len(after)

    def body(grad, rows_qkv, log, out, *rest):
        triple_o, context_s = rest[extra:]
        context_s[...] = (
            dot_nt(grad[...].reshape(rows, width), out[...]).astype(LOW).reshape(step, padded, width)
        )
        bias = key_bias(tokens, padded)
        for frame in range(step):

            def write(at, value):
                triple_o[frame, :, at : at + PAIR] = value

            heads_backward(
                lambda at: rows_qkv[frame, :, at : at + PAIR],
                lambda at: context_s[frame, :, at : at + PAIR],
                lambda head: log[frame, head : head + 1, :],
                write,
                width,
                bias,
            )

    def block(lanes):
        return pl.BlockSpec((step, padded, lanes), lambda i: (i + first, 0, 0))

    return pl.pallas_call(
        body,
        grid=(steps,),
        in_specs=[
            block(width), block(3 * width),
            pl.BlockSpec((step, LOG_ROWS, padded), lambda i: (i + first, 0, 0)), held(out),
        ]
        + [ANY] * extra,
        out_specs=block(3 * width),
        out_shape=shape((frames, padded, 3 * width), LOW),
        scratch_shapes=[pltpu.VMEM((step, padded, width), LOW)],
        input_output_aliases={4: 0} if into else {},
        compiler_params=params(50),
        cost_estimate=cost(20 * steps * rows * width * width, 16 * steps * rows * width),
        name="frame_backward",
    )(far(grad_low), far(qkv_rows), far(logs), out, *into, *after)


def qkv_weight_grad(ids, one, triple, count, after=()):
    rows, width = one.shape
    blocks = triple.shape[1] // width
    share, half = width // count, width // 2

    def body(ids, one, triple, *rest):
        keep, send = rest[len(after) :]

        def place_rows(ref, value, core):
            place_shares(ref, value, core, ids, count)

        store_shares(dot_tn(one[...], triple[...]), keep, send, ids[0], place_rows)

    block = pl.BlockSpec((2, 2, count // 2, 1, share // 2, half), lambda j: (0, 0, 0, j, 0, 0))
    out = shape((2, 2, count // 2, blocks, share // 2, half), LOW)
    return pl.pallas_call(
        body,
        grid=(blocks,),
        in_specs=[SCALARS, held(one), pl.BlockSpec((rows, width), lambda j: (0, j))]
        + [ANY] * len(after),
        out_specs=[block, block],
        out_shape=[out, out],
        compiler_params=params(48),
        cost_estimate=cost(3 * rows * width * width, 8 * rows * width + 6 * width * width),
        name="qkv_weight_grad",
    )(ids, far(one), far(triple), *after)


def message_rows(triple, message, grad, at, gain, qkv):
    frames, _, width = grad.shape
    tile = 16

    def body(triple, message, grad, gain, qkv, rows_o, triple_s, grad_s):
        triple_s[...] = triple[...].astype(F32)
        grad_s[...] = grad[...]
        normal, inverse = normalise(message[:frames, :])
        upstream = dot_nt(triple_s[:, at % tile, :].astype(LOW), qkv[...])
        back = norm_back(upstream, normal, inverse, gain[...])
        rows_o[...] = (grad_s[:, at % tile, :] + back).astype(LOW)

    def rows(lanes):
        return pl.BlockSpec((frames, tile, lanes), lambda i: (0, at // tile, 0))

    return pl.pallas_call(
        body,
        grid=(1,),
        in_specs=[rows(3 * width), held(message), rows(width), held(gain), held(qkv)],
        out_specs=pl.BlockSpec((frames, width), lambda i: (0, 0)),
        out_shape=shape((frames, width), LOW),
        scratch_shapes=[
            pltpu.VMEM((frames, tile, 3 * width), F32), pltpu.VMEM((frames, tile, width), F32)
        ],
        compiler_params=params(32),
        cost_estimate=cost(20 * frames * width * width, 6 * width * width),
        name="message_rows",
    )(far(triple), message, far(grad), gain, qkv)


def stream_backward(one, inverse, grad, triple, gain, qkv, dims, step, first, steps, into=None, after=()):
    videos, patches, slots, width = dims
    frames, padded, _ = grad.shape
    per = slots // step
    rows = step * padded
    into = () if into is None else (into,)
    extra = len(into) + len(after)

    def body(one, inverse, grad, triple, gain, qkv, *rest):
        stream_o, back_s = rest[extra:]
        part = pl.program_id(0) % per
        upstream = dot_nt(triple[...].reshape(rows, 3 * width), qkv[...])
        normal = one[...].reshape(rows, width).astype(F32) * (1.0 / gain[...])
        back = norm_back(upstream, normal, inverse[...].reshape(rows, 128)[:, :1], gain[...])
        back_s[pl.ds(part * step, step)] = grad[...] + back.reshape(step, padded, width)

        @pl.when(part == per - 1)
        def _():
            for slot in range(slots):
                stream_o[0, :, slot, :] = back_s[slot, :patches, :]

    def block(lanes):
        return pl.BlockSpec((step, padded, lanes), lambda i: (i + first * per, 0, 0))

    return pl.pallas_call(
        body,
        grid=(steps * per,),
        in_specs=[block(width), block(128), block(width), block(3 * width), WHOLE, held(qkv)]
        + [ANY] * extra,
        out_specs=pl.BlockSpec((1, patches, slots, width), lambda i: (first + i // per, 0, 0, 0)),
        out_shape=shape((videos, patches, slots, width), F32),
        scratch_shapes=[pltpu.VMEM((slots, padded, width), F32)],
        input_output_aliases={6: 0} if into else {},
        compiler_params=params(50),
        cost_estimate=cost(6 * steps * per * rows * width * width, 16 * steps * per * rows * width),
        name="stream_backward",
    )(far(one), far(inverse), far(grad), far(triple), gain, qkv, *into, *after)


def join_shares(ids, own, other, sections, after=(), through=None):
    passed = () if through is None else (through,)
    parts = len(own)
    half = own[0].shape[1]
    extra = [(w, g) for _, _, _, w, g in sections if w is not None]

    def body(ids, *refs):
        own_r, other_r = refs[:parts], refs[parts : 2 * parts]
        extra_r = refs[2 * parts : 2 * parts + 2 * len(extra)]
        at = 2 * parts + 2 * len(extra)
        outs = refs[at + len(after) + len(passed) : -1]
        column_s = refs[-1]
        if passed:
            outs[-1][...] = refs[at][...]
        first = ids[0] == 0
        y = ids[2] & 1

        def pick(pieces, part, cut):
            value = pieces[0][cut, :]
            for away in range(1, parts):
                value = jnp.where((part ^ y) == away, pieces[away][cut, :], value)
            return value

        at = given = 0
        for index, (blocks, rows, pitch, weight, _) in enumerate(sections):
            for part in range(parts):
                to = slice(part * rows, (part + 1) * rows)
                total = jnp.zeros((rows, 1), F32)
                for block in range(blocks):
                    cut = slice(at + block * pitch, at + block * pitch + rows)
                    mine, theirs = pick(own_r, part, cut), pick(other_r, part, cut)
                    sides = (jnp.where(first, mine, theirs), jnp.where(first, theirs, mine))
                    for side, value in enumerate(sides):
                        columns = slice((2 * block + side) * half, (2 * block + side + 1) * half)
                        value = value.astype(F32)
                        outs[index][to, columns] = value
                        if weight is not None:
                            product = value * extra_r[2 * given][to, columns].astype(F32)
                            total += jnp.sum(product, axis=1, keepdims=True)
                column_s[to, :] = jnp.broadcast_to(total, (rows, 128))
            at += blocks * pitch
            if weight is not None:
                sums = column_s[...].T[:1, : parts * rows]
                outs[len(sections) + given][...] = sums / extra_r[2 * given + 1][...]
                given += 1

    extra_specs, extra_args = [], []
    for blocks, rows, _, weight, gain in sections:
        if weight is not None:
            extra_specs += [
                pl.BlockSpec((parts * rows, weight.shape[1]), lambda i, ids: (ids[1], 0)), WHOLE
            ]
            extra_args += [weight, gain]
    high = -(-max(parts * rows for _, rows, _, _, _ in sections) // 128) * 128
    return pl.pallas_call(
        body,
        grid_spec=pltpu.PrefetchScalarGridSpec(
            num_scalar_prefetch=1,
            grid=(1,),
            in_specs=[WHOLE] * (2 * parts) + extra_specs + [WHOLE] * len(passed) + [ANY] * len(after),
            out_specs=[WHOLE] * (len(sections) + len(extra) + len(passed)),
            scratch_shapes=[pltpu.VMEM((high, 128), F32)],
        ),
        out_shape=[
            shape((parts * rows, blocks * 2 * half), F32) for blocks, rows, _, _, _ in sections
        ]
        + [shape((1, parts * rows), F32) for _, rows, _, weight, _ in sections if weight is not None]
        + [shape(value.shape, value.dtype) for value in passed],
        compiler_params=params(32),
        cost_estimate=cost(1 << 20, 8 * own[0].size * parts),
        name="join_shares",
    )(ids, *own, *other, *extra_args, *passed, *after)


def swap(value, *bits):
    frames, videos = lax.axis_size("frame"), lax.axis_size("video")
    pairs = []
    for f in range(frames):
        frame_bits, video_bits = bits[f % len(bits)]
        for v in range(videos):
            pairs.append((f * videos + v, (f ^ frame_bits) * videos + (v ^ video_bits)))
    return lax.ppermute(value, BOTH, pairs)


CORE = ((1, 0),)
ACROSS = ((2, 0),)
FIRST = ((0, 1), (2, 0))
SECOND = ((2, 0), (0, 1))


def spread(value, axis, bits):
    return jnp.stack([value] + [swap(value, bit) for bit in bits], axis=axis)


def bits_of(name):
    frames, videos = lax.axis_size("frame"), lax.axis_size("video")
    return {
        "core": [(1, 0)],
        "y": [(2 * y, 0) for y in range(1, frames // 2)],
        "x": [(0, 1)],
        "z": [(0, 2 * z) for z in range(1, videos // 2)],
    }[name]


class Gather:
    def __init__(self, value):
        self.value = value

    def start(self, axis, name):
        self.axis = axis
        self.moved = [swap(self.value, bit) for bit in bits_of(name)]
        return [self.value]

    def finish(self, after=None):
        moved = self.moved if after is None else tie(self.moved, after)
        self.value = jnp.stack([self.value] + moved, axis=self.axis)
        return [self.value]


def wide(value):
    return value.astype(F32)


def add_low(*values):
    return functools.reduce(jnp.add, [wide(v) for v in values]).astype(LOW)


def tie(values, after):
    return lax.optimization_barrier((values, after))[0]


class Share:
    def __init__(self, keep, send):
        self.sums, self.send = [keep], send

    def move(self, send, bits):
        self.moved = [swap(send, *bits)]
        return [send]

    def hold(self, after):
        self.moved = tie(self.moved, after)
        return self

    def core_swap(self):
        return self.move(self.send, CORE)

    def halve(self, bits):
        sums = self.sums + self.moved
        self.sums = [s[0] for s in sums]
        return self.move(add_low(*[s[1] for s in sums]), bits)

    def first_swap(self):
        return self.halve(FIRST)

    def second_swap(self):
        return self.halve(SECOND)

    def z_sends(self):
        sums = self.sums + self.moved
        self.sums, self.moved = [s[0] for s in sums], []
        self.sends = [
            add_low(*[s[z] for s in sums]) for z in range(1, lax.axis_size("video") // 2)
        ]
        return self.sends

    def z_swap(self, zs, after):
        sends = tie([self.sends[z - 1] for z in zs], after)
        self.moved = self.moved + [swap(send, (0, 2 * z)) for send, z in zip(sends, zs)]

    def total(self):
        total = add_low(*self.sums, *self.moved)
        bit = 4
        while bit < lax.axis_size("frame"):
            total = lax.optimization_barrier(total)
            total = add_low(total, swap(total, (bit, 0)))
            bit *= 2
        return lax.optimization_barrier(total)


def rows_of(value, lead):
    return value.reshape(*value.shape[:lead], -1, value.shape[-1])


class Join:
    def __init__(self, total):
        self.own = [total]
        self.moved = [swap(total, *ACROSS), swap(total, *CORE), swap(total, (3, 0))]

    def hold(self, after):
        self.moved = tie(self.moved, after)
        return self

    def parts(self):
        across, core, both = self.moved
        return self.own + [across], [core, both]


class SlowJoin:
    def __init__(self, total):
        self.total = total
        self.across = swap(total, *ACROSS)

    def hold(self, after):
        self.across = tie(self.across, after)
        return self

    def parts(self):
        own = [self.total, self.across]
        return own, [swap(value, *CORE) for value in own]


def flat(value):
    return value.reshape(-1, value.shape[-1])


def on_device(
    frames,
    out_cotangent,
    frame_counts,
    message_proj,
    message_gain,
    message_qkv,
    message_out,
    attn_gain,
    attn_qkv,
    attn_out,
    mlp_gain,
    mlp_up,
    mlp_down,
):
    videos, slots, patches, width = frames.shape
    tokens = patches + 1
    padded = -(-tokens // 16) * 16
    frame_total = videos * slots
    row_total = frame_total * padded
    frame_axis, video_axis = lax.axis_size("frame"), lax.axis_size("video")
    frame_index, video_index = lax.axis_index("frame"), lax.axis_index("video")
    share = width // video_axis
    ids = jnp.stack([frame_index & 1, video_index, frame_index >> 1]).astype(jnp.int32)
    slot_ids = frame_index * slots + jnp.arange(slots, dtype=jnp.int32)
    alive = (slot_ids[None, :] < frame_counts[:, None]).astype(F32).reshape(frame_total)
    gains = [g.reshape(1, width) for g in (message_gain, attn_gain, mlp_gain)]
    tokens_in = frames.transpose(0, 2, 1, 3)
    cotangent = out_cotangent.transpose(0, 2, 1, 3)

    class_rows = tokens_in[:, 0].reshape(frame_total, width)
    flags = jnp.broadcast_to(alive.astype(LOW)[:, None], (frame_total, 128))
    sizes = (frame_axis * frame_total, slots, videos)
    payload = jnp.concatenate([class_rows, flags], axis=1)
    payload = jnp.stack([payload] + [swap(payload, (f, 0)) for f in range(1, frame_axis)])
    payload = payload.reshape(frame_axis // 2, 2, frame_total, -1).transpose(1, 0, 2, 3)
    near = payload.reshape(-1, width + 128)

    step = min(2, slots)
    one, triple, final, inverse_one = frame_project(
        alive, tokens_in, cotangent, gains[1], attn_qkv, padded, step
    )
    classes = Gather(payload)
    classes.start(0, "z")
    message_two, one_rows, triple_rows = message_token(
        sizes, near, gains[0], message_proj, message_qkv, message_out, gains[1], attn_qkv
    )
    waits = classes.finish(message_two)
    classes.start(0, "x")
    one, triple, context, logs, hidden, two = frame_attend(
        tokens_in, message_two, one_rows, triple_rows, one, triple, gains[2], attn_out, step, waits
    )
    waits = classes.finish(two)
    payload = flat(classes.value)
    (
        encoded, hidden_grad, hidden_low, feed_keep, feed_send,
    ) = feed_forward(
        ids,
        alive,
        hidden.reshape(row_total, width),
        two.reshape(row_total, width),
        final.reshape(row_total, width),
        context.reshape(row_total, width),
        gains[2],
        mlp_up,
        mlp_down,
        (videos, patches, slots, padded),
        video_axis,
        waits,
    )

    hidden_low = hidden_low.reshape(frame_total, padded, width)
    hidden_grad = hidden_grad.reshape(frame_total, padded, width)
    feed = Share(feed_keep, feed_send)
    feed.core_swap()
    first_steps = 1
    triple_grad = frame_backward(
        hidden_low, triple, logs, attn_out, tokens, step, 0, first_steps
    )
    waits = feed.hold(triple_grad).first_swap()
    triple_grad = frame_backward(
        hidden_low, triple, logs, attn_out, tokens, step, first_steps,
        frame_total // step - first_steps, triple_grad, waits,
    )
    two_rows = message_rows(
        triple_grad, message_two, hidden_grad, patches, gains[1], attn_qkv
    )
    gather = Gather(two_rows)
    gather.start(0, "z")
    waits = feed.hold(triple_grad).second_swap()
    keep, send = qkv_weight_grad(
        ids, one.reshape(row_total, width), triple_grad.reshape(row_total, 3 * width), video_axis, waits
    )
    rest = Share(rows_of(keep, 3), rows_of(send, 3))
    rest.core_swap()
    zs = list(range(1, video_axis // 2))
    gather.finish(keep)
    waits = feed.hold(keep).z_sends()
    feed.z_swap(zs[:2], keep)
    gather.start(1, "y")
    pre, low, qkv_rows, message_logs, mcontext = message_forward(
        sizes, payload, gains[0], message_proj, message_qkv, message_out, waits
    )
    waits = gather.finish(pre) + rest.hold(pre).first_swap()
    gather.start(0, "x")
    feed.z_swap(zs[2:], pre)
    stream_grad = stream_backward(
        one, inverse_one, hidden_grad, triple_grad, gains[1], attn_qkv, tokens_in.shape, step, 0, 1,
        None, waits,
    )
    waits = gather.finish(stream_grad) + rest.hold(stream_grad).second_swap()
    gather.start(2, "core")
    stream_grad = stream_backward(
        one, inverse_one, hidden_grad, triple_grad, gains[1], attn_qkv, tokens_in.shape, step, 1,
        videos - 1, stream_grad, waits,
    )
    gather.finish(stream_grad)
    feed_total = feed.hold(stream_grad).total()
    feed_join = SlowJoin(feed_total)
    waits = [feed_total] + rest.hold(stream_grad).z_sends()
    rest.z_swap(zs[::-1], stream_grad)
    two_rows = flat(gather.value)
    class_grad, message_gain_grad, proj_sum, mqkv_sum, message_out_sum = message_backward(
        sizes, ids, payload, two_rows, pre, low, qkv_rows, message_logs, mcontext,
        gains[0], message_proj, message_qkv, message_out, share, waits,
    )
    feed_join.hold(class_grad), rest.hold(class_grad)
    cut = video_index * share

    def own_gain(gain):
        return lax.dynamic_slice(gain, (0, cut), (1, share))

    half_share = share // 2
    pitch, down_half = pitch_of(half_share), mlp_down.shape[0] // video_axis // 2
    up_sum, out_sum, down_sum, mlp_gain_sum, class_grad = join_shares(
        ids, *feed_join.parts(),
        [
            (mlp_up.shape[1] // width, half_share, pitch, mlp_up, own_gain(gains[2])),
            (1, half_share, pitch, None, None),
            (1, down_half, down_half, None, None),
        ],
        rest.moved,
        class_grad[:frame_total],
    )
    stream_grad = lax.dynamic_update_slice(
        stream_grad,
        stream_grad[:, :1] + class_grad.reshape(videos, 1, slots, width),
        (0, 0, 0, 0),
    )
    qkv_sum, attn_gain_sum = join_shares(
        ids, *Join(rest.total()).parts(), [(3, half_share, half_share, attn_qkv, own_gain(gains[1]))]
    )
    message_gain_sum = lax.dynamic_slice(message_gain_grad[0], (cut,), (share,))
    attn_gain_sum, mlp_gain_sum = attn_gain_sum[0], mlp_gain_sum[0]
    return (
        encoded.transpose(0, 2, 1, 3),
        stream_grad.transpose(0, 2, 1, 3),
        proj_sum,
        message_gain_sum,
        mqkv_sum,
        message_out_sum,
        attn_gain_sum,
        qkv_sum,
        out_sum,
        mlp_gain_sum,
        up_sum,
        down_sum,
    )


def solution(mesh):
    return jax.shard_map(
        on_device,
        mesh=mesh,
        in_specs=(
            P("video", "frame", None, None),
            P("video", "frame", None, None),
            P("video"),
            P(),
            P(),
            P(),
            P(),
            P(),
            P(),
            P(),
            P(),
            P(),
            P(),
        ),
        out_specs=(
            P("video", "frame", None, None),
            P("video", "frame", None, None),
            P("video", None),
            P("video"),
            P("video", None),
            P("video", None),
            P("video"),
            P("video", None),
            P("video", None),
            P("video"),
            P("video", None),
            P("video", None),
        ),
        check_vma=False,
    )
```

```python
import functools
import math

import jax
import jax.numpy as jnp
from jax import lax
from jax.experimental import pallas as pl
from jax.experimental.pallas import tpu as pltpu
from jax.sharding import PartitionSpec as P

H = 12
HD = 64
EPSILON = 1e-05
LOW = jnp.bfloat16
F32 = jnp.float32
BOTH = ("frame", "video")
SCALE = 1.0 / math.sqrt(HD)
PAIR = 2 * HD
PAIRS = H // 2
LOG_ROWS = 16
MESSAGE_TILE = 256


def dot_nn(left, right):
    return lax.dot_general(
        left, right, (((1,), (0,)), ((), ())), preferred_element_type=F32
    )


def dot_nt(left, right):
    return lax.dot_general(
        left, right, (((1,), (1,)), ((), ())), preferred_element_type=F32
    )


def dot_tn(left, right):
    return lax.dot_general(
        left, right, (((0,), (0,)), ((), ())), preferred_element_type=F32
    )


def normalise(value):
    centred = value - jnp.mean(value, axis=-1, keepdims=True)
    inverse = lax.rsqrt(jnp.mean(centred * centred, axis=-1, keepdims=True) + EPSILON)
    return centred * inverse, inverse


def norm_back(upstream, normal, inverse, gain):
    scaled = upstream * gain
    inner = (
        scaled
        - jnp.mean(scaled, axis=-1, keepdims=True)
        - normal * jnp.mean(scaled * normal, axis=-1, keepdims=True)
    )
    return inner * inverse


def half_masks():
    first = lax.broadcasted_iota(jnp.int32, (1, PAIR), 1) < HD
    plain = (jnp.where(first, 1.0, 0.0).astype(LOW), jnp.where(first, 0.0, 1.0).astype(LOW))
    scaled = (jnp.where(first, SCALE, 0.0).astype(LOW), jnp.where(first, 0.0, SCALE).astype(LOW))
    return plain, scaled


def pair_forward(query, key, value, bias, masks):
    plain, scaled = masks
    context, logs = None, []
    for one, by in zip(plain, scaled):
        score = dot_nt(key, query * by) + bias
        top = jnp.max(score, axis=0, keepdims=True)
        raised = jnp.exp(score - top)
        total = jnp.sum(raised, axis=0, keepdims=True)
        prob_low = (raised * (1.0 / total)).astype(LOW)
        logs.append(top + jnp.log(total))
        part = dot_tn(prob_low, value * one)
        context = part if context is None else context + part
    return context, logs


def pair_backward(query, key, value, grad, logs, bias, masks):
    plain, scaled = masks
    query_grad = key_grad = value_grad = None
    for one, by, log in zip(plain, scaled, logs):
        query_by, grad_one, key_by = query * by, grad * one, key * by
        prob = jnp.exp(dot_nt(key, query_by) + bias - log)
        prob_grad = dot_nt(value, grad_one)
        inner = jnp.sum(prob * prob_grad, axis=0, keepdims=True)
        score_low = (prob * (prob_grad - inner)).astype(LOW)
        parts = (
            dot_tn(score_low, key_by),
            dot_nn(score_low, query_by),
            dot_nn(prob.astype(LOW), grad_one),
        )
        if query_grad is None:
            query_grad, key_grad, value_grad = parts
        else:
            query_grad, key_grad, value_grad = (
                query_grad + parts[0],
                key_grad + parts[1],
                value_grad + parts[2],
            )
    return query_grad, key_grad, value_grad


def heads_forward(read, write, write_log, width, bias):
    masks = half_masks()
    for pair in range(PAIRS):
        at = pair * PAIR
        context, pair_logs = pair_forward(
            read(at), read(width + at), read(2 * width + at), bias, masks
        )
        write(at, context.astype(LOW))
        for head in range(2):
            write_log(2 * pair + head, pair_logs[head])


def heads_backward(read, read_grad, read_log, write, width, bias):
    masks = half_masks()
    for pair in range(PAIRS):
        at = pair * PAIR
        grads = pair_backward(
            read(at),
            read(width + at),
            read(2 * width + at),
            read_grad(at),
            (read_log(2 * pair), read_log(2 * pair + 1)),
            bias,
            masks,
        )
        for part in range(3):
            write(part * width + at, grads[part].astype(LOW))


def key_bias(tokens, padded):
    return jnp.where(lax.broadcasted_iota(jnp.int32, (padded, 1), 0) < tokens, 0.0, -1e30)


def message_bias(flag, per_index, slots, videos):
    rows = flag.shape[0]
    row = lax.broadcasted_iota(jnp.int32, (rows, rows), 0)
    column = lax.broadcasted_iota(jnp.int32, (rows, rows), 1)
    same = (row // per_index == column // per_index) & (
        (row // slots) % videos == (column // slots) % videos
    )
    first = (lax.broadcasted_iota(jnp.int32, (rows, 128), 1) == 0).astype(LOW)
    alive = dot_nt(flag, first) > 0.5
    return jnp.where(same & alive, 0.0, -1e30)


WHOLE = pl.BlockSpec(memory_space=pltpu.VMEM)
SCALARS = pl.BlockSpec(memory_space=pltpu.SMEM)
ANY = pl.BlockSpec(memory_space=pl.ANY)


def held(array):
    zeros = (0,) * array.ndim
    return pl.BlockSpec(array.shape, lambda *_: zeros, pipeline_mode=pl.Buffered(1))


def far(array):
    return pltpu.with_memory_space_constraint(array, pltpu.HBM)


def params(megabytes):
    return pltpu.CompilerParams(vmem_limit_bytes=megabytes << 20)


def cost(macs, moved, raised=0):
    return pl.CostEstimate(flops=2 * macs * 8, bytes_accessed=moved * 8, transcendentals=raised)


def shape(dims, dtype):
    return jax.ShapeDtypeStruct(dims, dtype)


def message_forward(sizes, payload, gain, proj, qkv, out, after=()):
    rows, wide = payload.shape
    width = proj.shape[0]
    tile = min(MESSAGE_TILE, rows)

    def body(pay, gain, proj, qkv, out, *rest):
        pre_o, low_o, qkv_o, log_o, context_o = rest[len(after) :]
        pre = dot_nn(pay[:, :width], proj[...])
        pre_o[...] = pre
        normal, _ = normalise(pre)
        message = normal * gain[...]
        low = message.astype(LOW)
        low_o[...] = low
        qkv_o[...] = dot_nn(low, qkv[...]).astype(LOW)
        bias = message_bias(pay[:, width:], *sizes)

        def write(at, value):
            context_o[:, at : at + PAIR] = value

        def write_log(head, value):
            log_o[head : head + 1, :] = value

        heads_forward(lambda at: qkv_o[:, at : at + PAIR], write, write_log, width, bias)

    def block(lanes):
        return pl.BlockSpec((tile, lanes), lambda i: (i, 0))

    return pl.pallas_call(
        body,
        grid=(rows // tile,),
        in_specs=[block(wide), WHOLE, held(proj), held(qkv), held(out)] + [ANY] * len(after),
        out_specs=[
            block(width), block(width), block(3 * width),
            pl.BlockSpec((LOG_ROWS, tile), lambda i: (0, i)), block(width),
        ],
        out_shape=[
            shape((rows, width), F32),
            shape((rows, width), LOW),
            shape((rows, 3 * width), LOW),
            shape((LOG_ROWS, rows), F32),
            shape((rows, width), LOW),
        ],
        compiler_params=params(48),
        cost_estimate=cost(5 * rows * width * width, 12 * width * width + 20 * rows * width),
        name="message_forward",
    )(payload, gain, proj, qkv, out, *after)


def message_token(sizes, payload, gain, proj, qkv, out, next_gain, next_qkv):
    rows, wide = payload.shape
    width = proj.shape[0]

    def body(pay, gain, proj, qkv, out, next_gain, next_qkv, two_o, one_o, triple_o, rows_s, context_s):
        message = normalise(dot_nn(pay[:, :width], proj[...]))[0] * gain[...]
        rows_s[...] = dot_nn(message.astype(LOW), qkv[...]).astype(LOW)
        bias = message_bias(pay[:, width:], *sizes)

        def write(at, value):
            context_s[:, at : at + PAIR] = value

        heads_forward(
            lambda at: rows_s[:, at : at + PAIR], write, lambda head, value: None, width, bias
        )
        two = message + dot_nn(context_s[...], out[...])
        two_o[...] = two
        one_low = (normalise(two)[0] * next_gain[...]).astype(LOW)
        one_o[...] = one_low.astype(F32)
        triple_o[...] = dot_nn(one_low, next_qkv[...])

    return pl.pallas_call(
        body,
        grid=(1,),
        in_specs=[
            WHOLE, WHOLE, held(proj), held(qkv), held(out), WHOLE, held(next_qkv),
        ],
        out_specs=[WHOLE] * 3,
        out_shape=[shape((rows, width), F32), shape((rows, width), F32), shape((rows, 3 * width), F32)],
        scratch_shapes=[pltpu.VMEM((rows, 3 * width), LOW), pltpu.VMEM((rows, width), LOW)],
        compiler_params=params(48),
        cost_estimate=cost(8 * rows * width * width, 16 * width * width + 20 * rows * width),
        name="message_token",
    )(payload, gain, far(proj), far(qkv), far(out), next_gain, far(next_qkv))


def message_backward(
    sizes, ids, payload, two_low, pre, low, qkv_rows, logs, context, gain, proj, qkv, out, share,
    after=(),
):
    rows, wide = payload.shape
    width = proj.shape[0]
    tile = min(MESSAGE_TILE, rows)

    def body(
        ids, pay, two, pre, low, rows_qkv, log, context, gain, proj, qkv, out, *rest
    ):
        class_o, gain_o, proj_o, qkv_o, out_o, grad_s, triple_s = rest[len(after) :]

        @pl.when(pl.program_id(0) == 0)
        def _():
            gain_o[...] = jnp.zeros_like(gain_o)
            proj_o[...] = jnp.zeros_like(proj_o)
            qkv_o[...] = jnp.zeros_like(qkv_o)
            out_o[...] = jnp.zeros_like(out_o)

        pick = lax.broadcasted_iota(jnp.int32, (width, share), 0) == (
            lax.broadcasted_iota(jnp.int32, (width, share), 1) + ids[1] * share
        )
        pick = jnp.where(pick, 1.0, 0.0).astype(LOW)
        two_rows = two[...]
        grad_s[...] = dot_nt(two_rows, out[...]).astype(LOW)
        out_o[...] += dot_tn(dot_nn(context[...], pick).astype(LOW), two_rows)
        bias = message_bias(pay[:, width:], *sizes)

        def write(at, value):
            triple_s[:, at : at + PAIR] = value

        heads_backward(
            lambda at: rows_qkv[:, at : at + PAIR],
            lambda at: grad_s[:, at : at + PAIR],
            lambda head: log[head : head + 1, :],
            write,
            width,
            bias,
        )
        triple = triple_s[...]
        qkv_o[...] += dot_tn(dot_nn(low[...], pick).astype(LOW), triple)
        upstream = two_rows.astype(F32) + dot_nt(triple, qkv[...])
        normal, inverse = normalise(pre[...])
        gain_o[...] += jnp.sum(upstream * normal, axis=0, keepdims=True)
        pre_low = norm_back(upstream, normal, inverse, gain[...]).astype(LOW)
        proj_o[...] += dot_tn(dot_nn(pay[:, :width], pick).astype(LOW), pre_low)
        class_o[...] = dot_nt(pre_low, proj[...])

    def block(lanes):
        return pl.BlockSpec((tile, lanes), lambda i: (i, 0))

    def fixed(dims):
        return pl.BlockSpec(dims, lambda i: (0, 0))

    return pl.pallas_call(
        body,
        grid=(rows // tile,),
        in_specs=[
            SCALARS, block(wide), block(width), block(width), block(width), block(3 * width),
            pl.BlockSpec((LOG_ROWS, tile), lambda i: (0, i)), block(width), WHOLE,
            held(proj), held(qkv), held(out),
        ]
        + [ANY] * len(after),
        out_specs=[
            block(width), fixed((1, width)), fixed((share, width)), fixed((share, 3 * width)),
            fixed((share, width)),
        ],
        out_shape=[
            shape((rows, width), F32),
            shape((1, width), F32),
            shape((share, width), F32),
            shape((share, 3 * width), F32),
            shape((share, width), F32),
        ],
        scratch_shapes=[pltpu.VMEM((tile, width), LOW), pltpu.VMEM((tile, 3 * width), LOW)],
        compiler_params=params(48),
        cost_estimate=cost(8 * rows * width * width, 16 * width * width + 20 * rows * width),
        name="message_backward",
    )(
        ids, payload, two_low, pre, low, qkv_rows, logs, context, gain, proj, qkv, out,
        *after,
    )


def frame_project(alive, tokens_in, cotangent, gain, qkv, padded, step):
    videos, patches, slots, width = tokens_in.shape
    frames = videos * slots
    per = slots // step
    rows = step * padded

    def body(alive, tokens, grads, gain, qkv, one_o, qkv_o, final_o, inverse_o, split_s, stream_s, grad_s):
        index = pl.program_id(0)
        video, part = index // per, index % per

        @pl.when(index == 0)
        def _():
            stream_s[...] = jnp.zeros_like(stream_s)
            grad_s[...] = jnp.zeros_like(grad_s)

        @pl.when(part == 0)
        def _():
            split_s[...] = tokens[0].astype(F32)
            for slot in range(slots):
                stream_s[slot, :patches, :] = split_s[:, slot, :]
            split_s[...] = grads[0].astype(F32)
            for slot in range(slots):
                grad_s[:patches, :] = split_s[:, slot, :] * alive[video * slots + slot]
                final_o[slot] = grad_s[...].astype(LOW)

        stream = stream_s[pl.ds(part * step, step)].reshape(rows, width)
        normal, inverse = normalise(stream)
        one_low = (normal * gain[...]).astype(LOW)
        one_o[...] = one_low.reshape(step, padded, width)
        inverse_o[...] = jnp.broadcast_to(inverse, (rows, 128)).reshape(step, padded, 128)
        for third in range(3):
            cut = slice(third * width, (third + 1) * width)
            qkv_o[:, :, cut] = dot_nn(one_low, qkv[:, cut]).astype(LOW).reshape(step, padded, width)

    def block(lanes):
        return pl.BlockSpec((step, padded, lanes), lambda i: (i, 0, 0))

    per_video = pl.BlockSpec((1, patches, slots, width), lambda i: (i // per, 0, 0, 0))
    return pl.pallas_call(
        body,
        grid=(frames // step,),
        in_specs=[SCALARS, per_video, per_video, WHOLE, held(qkv)],
        out_specs=[
            block(width), block(3 * width),
            pl.BlockSpec((slots, padded, width), lambda i: (i // per, 0, 0)), block(128),
        ],
        out_shape=[
            shape((frames, padded, width), LOW),
            shape((frames, padded, 3 * width), LOW),
            shape((frames, padded, width), LOW),
            shape((frames, padded, 128), F32),
        ],
        scratch_shapes=[
            pltpu.VMEM((patches, slots, width), F32),
            pltpu.VMEM((slots, padded, width), F32),
            pltpu.VMEM((padded, width), F32),
        ],
        compiler_params=params(50),
        cost_estimate=cost(4 * frames * padded * width * width, 16 * frames * padded * width),
        name="frame_project",
    )(alive, far(tokens_in), far(cotangent), gain, qkv)


def frame_attend(tokens_in, message, message_one, message_qkv, one, qkv_rows, gain, out, step, after=()):
    videos, patches, slots, width = tokens_in.shape
    frames, padded, _ = qkv_rows.shape
    per = slots // step
    rows = step * padded

    def body(
        tokens, message, message_one, message_qkv, one, rows_qkv, gain, out, *rest
    ):
        one_o, full_o, context_o, log_o, hidden_o, two_o, split_s, stream_s = rest[len(after) :]
        index = pl.program_id(0)
        video, part = index // per, index % per

        @pl.when(index == 0)
        def _():
            stream_s[...] = jnp.zeros_like(stream_s)

        @pl.when(part == 0)
        def _():
            split_s[...] = tokens[0].astype(F32)
            for slot in range(slots):
                stream_s[slot, :patches, :] = split_s[:, slot, :]
                stream_s[slot, patches : patches + 1, :] = message[pl.ds(video * slots + slot, 1), :]

        here = lax.broadcasted_iota(jnp.int32, (padded, 1), 0) == patches
        for frame in range(step):
            row = message_one[pl.ds(index * step + frame, 1), :]
            one_o[frame] = jnp.where(here, row, one[frame].astype(F32)).astype(LOW)
            row = message_qkv[pl.ds(index * step + frame, 1), :]
            full_o[frame] = jnp.where(here, row, rows_qkv[frame].astype(F32)).astype(LOW)
        bias = key_bias(patches + 1, padded)
        for frame in range(step):

            def read(at):
                return full_o[frame, :, at : at + PAIR]

            def write(at, value):
                context_o[frame, :, at : at + PAIR] = value

            def write_log(head, value):
                log_o[frame, head : head + 1, :] = value

            heads_forward(read, write, write_log, width, bias)
        stream = stream_s[pl.ds(part * step, step)].reshape(rows, width)
        hidden = stream + dot_nn(context_o[...].reshape(rows, width), out[...])
        hidden_o[...] = hidden.reshape(step, padded, width)
        two_o[...] = (normalise(hidden)[0] * gain[...]).astype(LOW).reshape(step, padded, width)

    def block(lanes):
        return pl.BlockSpec((step, padded, lanes), lambda i: (i, 0, 0))

    per_video = pl.BlockSpec((1, patches, slots, width), lambda i: (i // per, 0, 0, 0))
    return pl.pallas_call(
        body,
        grid=(frames // step,),
        in_specs=[
            per_video, WHOLE, WHOLE, WHOLE, block(width), block(3 * width), WHOLE, held(out),
        ]
        + [ANY] * len(after),
        out_specs=[
            block(width), block(3 * width), block(width), pl.BlockSpec((step, LOG_ROWS, padded), lambda i: (i, 0, 0)),
            block(width), block(width),
        ],
        out_shape=[
            shape((frames, padded, width), LOW),
            shape((frames, padded, 3 * width), LOW),
            shape((frames, padded, width), LOW),
            shape((frames, LOG_ROWS, padded), F32),
            shape((frames, padded, width), F32),
            shape((frames, padded, width), LOW),
        ],
        scratch_shapes=[
            pltpu.VMEM((patches, slots, width), F32),
            pltpu.VMEM((slots, padded, width), F32),
        ],
        compiler_params=params(52),
        cost_estimate=cost(8 * frames * padded * width * width, 24 * frames * padded * width),
        name="frame_attend",
    )(
        far(tokens_in), message, message_one, message_qkv, far(one), far(qkv_rows), gain, far(out), *after
    )


def place_of(index, part, core, ids):
    away = index ^ ids[1]
    x, y = away & 1, part ^ (ids[2] & 1)
    straight = core == 0
    return jnp.where(straight, x, y), jnp.where(straight, y, x), away >> 1


def place_shares(ref, value, core, ids, count):
    rows = value.shape[0] // count // 2
    for index in range(count):
        for part in range(2):
            at = (2 * index + part) * rows
            first, second, z = place_of(index, part, core, ids)
            ref[first, second, z, 0] = value[at : at + rows]


def pitch_of(rows):
    return -(-rows // 16) * 16


def store_shares(full, keep, send, core, place):
    half = full.shape[1] // 2
    left, right = full[:, :half].astype(LOW), full[:, half:].astype(LOW)
    first = core == 0
    place(keep, jnp.where(first, left, right), core)
    place(send, jnp.where(first, right, left), 1 - core)


def feed_forward(ids, alive, hidden, two, final, context, gain, up, down, dims, count, after=()):
    videos, patches, slots, padded = dims
    rows, width = hidden.shape
    inner = up.shape[1]
    blocks = inner // width
    half = width // 2
    step = min(2, slots)
    per = slots // step
    last = blocks - 1
    tile = step * padded
    tails = rows // tile
    share, down_share = width // count, inner // count
    half_share = share // 2
    pitch = pitch_of(half_share)
    per_block = width // down_share
    low_count = per_block // 2

    def body(
        ids, alive, hidden, two, final, context, gain, up, down, *rest
    ):
        encoded_o, grad_o, grad_low_o, keep_o, send_o = rest[len(after) :][:5]
        (
            total_s, back_sum_s, act_s, back_s, join_s, split_s, out_s,
            up_keep, up_send, down_keep, down_send, sem,
        ) = rest[len(after) + 5 :]
        index = pl.program_id(0)
        core = ids[0]

        def up_moves(step):
            rows = pl.ds(pl.multiple_of(jnp.minimum(step, blocks) * pitch, pitch), pitch)
            return [
                pltpu.make_async_copy(
                    stage.at[step % 2], place.at[:, :, :, rows, :], sem.at[step % 2, n]
                )
                for n, (stage, place) in enumerate(((up_keep, keep_o), (up_send, send_o)))
            ]

        def down_moves(step):
            block = jnp.minimum(step, last) ^ ((ids[1] >> 1) // low_count)
            zs = pl.ds(block * low_count, low_count)
            rows = pl.ds((blocks + 1) * pitch, down_share // 2)
            return [
                pltpu.make_async_copy(
                    stage.at[step % 2], place.at[:, :, zs, rows, :], sem.at[step % 2, 2 + n]
                )
                for n, (stage, place) in enumerate(((down_keep, keep_o), (down_send, send_o)))
            ]

        def start(copies):
            for copy in copies:
                copy.start()

        def wait(copies):
            for copy in copies:
                copy.wait()

        def place_rows(ref, value, core):
            rows = half_share
            for at in range(count):
                for part in range(2):
                    first, second, z = place_of(at, part, core, ids)
                    row = (2 * at + part) * rows
                    ref[index % 2, first, second, z, :rows, :] = value[row : row + rows]

        def place_down(ref, value, core):
            for at in range(per_block):
                for part in range(2):
                    row = (2 * at + part) * down_share // 2
                    first, second, z = place_of(at, part, core, ids)
                    ref[index % 2, first, second, z % low_count] = value[row : row + down_share // 2]

        @pl.when(index == 0)
        def _():
            total_s[...] = jnp.zeros_like(total_s)
            back_sum_s[...] = jnp.zeros_like(back_sum_s)
            out_s[...] = jnp.zeros_like(out_s)

        @pl.when(index < blocks)
        def _():
            for part in range(rows // tile):
                cut = slice(part * tile, (part + 1) * tile)
                value = dot_nn(two[cut, :], up[...])
                act_grad = dot_nt(final[cut, :], down[...])
                sigma = 0.5 * jnp.tanh(0.851 * value) + 0.5
                act = value * sigma
                slope = sigma + 1.702 * (act - act * sigma)
                act_low = act.astype(LOW)
                back_low = (act_grad * slope).astype(LOW)
                act_s[cut, :] = act_low
                back_s[cut, :] = back_low
                total_s[cut, :] += dot_nn(act_low, down[...])
                back_sum_s[cut, :] += dot_nt(back_low, up[...])

            @pl.when(index >= 2)
            def _():
                wait(up_moves(index - 2) + down_moves(index - 2))

            store_shares(dot_tn(two[...], back_s[...]), up_keep, up_send, core, place_rows)
            store_shares(dot_tn(act_s[...], final[...]), down_keep, down_send, core, place_down)
            start(up_moves(index) + down_moves(index))

        @pl.when(index >= blocks)
        def _():
            tail = index - blocks

            @pl.when(tail == 0)
            def _():
                for step in range(max(0, blocks - 2), blocks):
                    wait(up_moves(step) + down_moves(step))

            cut = pl.ds(pl.multiple_of(tail * tile, tile), tile)
            value = hidden[...]
            total = (value + total_s[cut, :]).reshape(step, padded, width)
            for frame in range(step):
                join_s[(tail % per) * step + frame] = total[frame, :patches] * alive[tail * step + frame]
            normal, inverse = normalise(value)
            back = norm_back(back_sum_s[cut, :], normal, inverse, gain[...])
            back = final[cut, :].astype(F32) + back
            back_low = back.astype(LOW)
            grad_o[...] = back
            grad_low_o[...] = back_low
            out_s[...] += dot_tn(context[...], back_low)

            @pl.when(tail % per == per - 1)
            def _():
                for slot in range(slots):
                    split_s[:, slot, :] = join_s[slot]
                encoded_o[0] = split_s[...].astype(LOW)

            @pl.when(tail == tails - 1)
            def _():
                store_shares(out_s[...], up_keep, up_send, core, place_rows)
                copies = up_moves(index)
                start(copies)
                wait(copies)

    def tail_of(j):
        return jnp.maximum(j - blocks, 0)

    rows_block = pl.BlockSpec((tile, width), lambda j, ids: (tail_of(j), 0))
    packed = shape((2, 2, count // 2, (blocks + 1) * pitch + down_share // 2, half), LOW)
    up_stage = pltpu.VMEM((2, 2, 2, count // 2, pitch, half), LOW)
    down_stage = pltpu.VMEM((2, 2, 2, low_count, down_share // 2, half), LOW)
    return pl.pallas_call(
        body,
        grid_spec=pltpu.PrefetchScalarGridSpec(
            num_scalar_prefetch=1,
            grid=(blocks + tails,),
            in_specs=[
                SCALARS, rows_block, WHOLE, WHOLE, rows_block, WHOLE,
                pl.BlockSpec((width, width), lambda j, ids: (0, jnp.minimum(j, last))),
                pl.BlockSpec((width, width), lambda j, ids: (jnp.minimum(j, last), 0)),
            ]
            + [ANY] * len(after),
            out_specs=[
                pl.BlockSpec((1, patches, slots, width), lambda j, ids: (tail_of(j) // per, 0, 0, 0)),
                rows_block, rows_block, ANY, ANY,
            ],
            scratch_shapes=[
                pltpu.VMEM((rows, width), F32),
                pltpu.VMEM((rows, width), F32),
                pltpu.VMEM((rows, width), LOW),
                pltpu.VMEM((rows, width), LOW),
                pltpu.VMEM((slots, patches, width), F32),
                pltpu.VMEM((patches, slots, width), F32),
                pltpu.VMEM((width, width), F32),
                up_stage, up_stage, down_stage, down_stage,
                pltpu.SemaphoreType.DMA((2, 4)),
            ],
        ),
        out_shape=[
            shape((videos, patches, slots, width), LOW),
            shape((rows, width), F32),
            shape((rows, width), LOW),
            packed, packed,
        ],
        compiler_params=params(60),
        cost_estimate=cost(8 * rows * width * inner, 8 * width * inner + 20 * rows * width),
        name="feed_forward",
    )(ids, alive, far(hidden), two, final, far(context), gain, up, down, *after)


def frame_backward(grad_low, qkv_rows, logs, out, tokens, step, first, steps, into=None, after=()):
    frames, padded, width = grad_low.shape
    rows = step * padded
    into = () if into is None else (into,)
    extra = len(into) + len(after)

    def body(grad, rows_qkv, log, out, *rest):
        triple_o, context_s = rest[extra:]
        context_s[...] = (
            dot_nt(grad[...].reshape(rows, width), out[...]).astype(LOW).reshape(step, padded, width)
        )
        bias = key_bias(tokens, padded)
        for frame in range(step):

            def write(at, value):
                triple_o[frame, :, at : at + PAIR] = value

            heads_backward(
                lambda at: rows_qkv[frame, :, at : at + PAIR],
                lambda at: context_s[frame, :, at : at + PAIR],
                lambda head: log[frame, head : head + 1, :],
                write,
                width,
                bias,
            )

    def block(lanes):
        return pl.BlockSpec((step, padded, lanes), lambda i: (i + first, 0, 0))

    return pl.pallas_call(
        body,
        grid=(steps,),
        in_specs=[
            block(width), block(3 * width),
            pl.BlockSpec((step, LOG_ROWS, padded), lambda i: (i + first, 0, 0)), held(out),
        ]
        + [ANY] * extra,
        out_specs=block(3 * width),
        out_shape=shape((frames, padded, 3 * width), LOW),
        scratch_shapes=[pltpu.VMEM((step, padded, width), LOW)],
        input_output_aliases={4: 0} if into else {},
        compiler_params=params(50),
        cost_estimate=cost(20 * steps * rows * width * width, 16 * steps * rows * width),
        name="frame_backward",
    )(far(grad_low), far(qkv_rows), far(logs), out, *into, *after)


def qkv_weight_grad(ids, one, triple, count, after=()):
    rows, width = one.shape
    blocks = triple.shape[1] // width
    share, half = width // count, width // 2

    def body(ids, one, triple, *rest):
        keep, send = rest[len(after) :]

        def place_rows(ref, value, core):
            place_shares(ref, value, core, ids, count)

        store_shares(dot_tn(one[...], triple[...]), keep, send, ids[0], place_rows)

    block = pl.BlockSpec((2, 2, count // 2, 1, share // 2, half), lambda j: (0, 0, 0, j, 0, 0))
    out = shape((2, 2, count // 2, blocks, share // 2, half), LOW)
    return pl.pallas_call(
        body,
        grid=(blocks,),
        in_specs=[SCALARS, held(one), pl.BlockSpec((rows, width), lambda j: (0, j))]
        + [ANY] * len(after),
        out_specs=[block, block],
        out_shape=[out, out],
        compiler_params=params(48),
        cost_estimate=cost(3 * rows * width * width, 8 * rows * width + 6 * width * width),
        name="qkv_weight_grad",
    )(ids, far(one), far(triple), *after)


def message_rows(triple, message, grad, at, gain, qkv):
    frames, _, width = grad.shape
    tile = 16

    def body(triple, message, grad, gain, qkv, rows_o, triple_s, grad_s):
        triple_s[...] = triple[...].astype(F32)
        grad_s[...] = grad[...]
        normal, inverse = normalise(message[:frames, :])
        upstream = dot_nt(triple_s[:, at % tile, :].astype(LOW), qkv[...])
        back = norm_back(upstream, normal, inverse, gain[...])
        rows_o[...] = (grad_s[:, at % tile, :] + back).astype(LOW)

    def rows(lanes):
        return pl.BlockSpec((frames, tile, lanes), lambda i: (0, at // tile, 0))

    return pl.pallas_call(
        body,
        grid=(1,),
        in_specs=[rows(3 * width), held(message), rows(width), held(gain), held(qkv)],
        out_specs=pl.BlockSpec((frames, width), lambda i: (0, 0)),
        out_shape=shape((frames, width), LOW),
        scratch_shapes=[
            pltpu.VMEM((frames, tile, 3 * width), F32), pltpu.VMEM((frames, tile, width), F32)
        ],
        compiler_params=params(32),
        cost_estimate=cost(20 * frames * width * width, 6 * width * width),
        name="message_rows",
    )(far(triple), message, far(grad), gain, qkv)


def stream_backward(one, inverse, grad, triple, gain, qkv, dims, step, first, steps, into=None, after=()):
    videos, patches, slots, width = dims
    frames, padded, _ = grad.shape
    per = slots // step
    rows = step * padded
    into = () if into is None else (into,)
    extra = len(into) + len(after)

    def body(one, inverse, grad, triple, gain, qkv, *rest):
        stream_o, back_s = rest[extra:]
        part = pl.program_id(0) % per
        upstream = dot_nt(triple[...].reshape(rows, 3 * width), qkv[...])
        normal = one[...].reshape(rows, width).astype(F32) * (1.0 / gain[...])
        back = norm_back(upstream, normal, inverse[...].reshape(rows, 128)[:, :1], gain[...])
        back_s[pl.ds(part * step, step)] = grad[...] + back.reshape(step, padded, width)

        @pl.when(part == per - 1)
        def _():
            for slot in range(slots):
                stream_o[0, :, slot, :] = back_s[slot, :patches, :]

    def block(lanes):
        return pl.BlockSpec((step, padded, lanes), lambda i: (i + first * per, 0, 0))

    return pl.pallas_call(
        body,
        grid=(steps * per,),
        in_specs=[block(width), block(128), block(width), block(3 * width), WHOLE, held(qkv)]
        + [ANY] * extra,
        out_specs=pl.BlockSpec((1, patches, slots, width), lambda i: (first + i // per, 0, 0, 0)),
        out_shape=shape((videos, patches, slots, width), F32),
        scratch_shapes=[pltpu.VMEM((slots, padded, width), F32)],
        input_output_aliases={6: 0} if into else {},
        compiler_params=params(50),
        cost_estimate=cost(6 * steps * per * rows * width * width, 16 * steps * per * rows * width),
        name="stream_backward",
    )(far(one), far(inverse), far(grad), far(triple), gain, qkv, *into, *after)


def join_shares(ids, own, other, sections, after=(), through=None):
    passed = () if through is None else (through,)
    parts = len(own)
    half = own[0].shape[1]
    extra = [(w, g) for _, _, _, w, g in sections if w is not None]

    def body(ids, *refs):
        own_r, other_r = refs[:parts], refs[parts : 2 * parts]
        extra_r = refs[2 * parts : 2 * parts + 2 * len(extra)]
        at = 2 * parts + 2 * len(extra)
        outs = refs[at + len(after) + len(passed) : -1]
        column_s = refs[-1]
        if passed:
            outs[-1][...] = refs[at][...]
        first = ids[0] == 0
        y = ids[2] & 1

        def pick(pieces, part, cut):
            value = pieces[0][cut, :]
            for away in range(1, parts):
                value = jnp.where((part ^ y) == away, pieces[away][cut, :], value)
            return value

        at = given = 0
        for index, (blocks, rows, pitch, weight, _) in enumerate(sections):
            for part in range(parts):
                to = slice(part * rows, (part + 1) * rows)
                total = jnp.zeros((rows, 1), F32)
                for block in range(blocks):
                    cut = slice(at + block * pitch, at + block * pitch + rows)
                    mine, theirs = pick(own_r, part, cut), pick(other_r, part, cut)
                    sides = (jnp.where(first, mine, theirs), jnp.where(first, theirs, mine))
                    for side, value in enumerate(sides):
                        columns = slice((2 * block + side) * half, (2 * block + side + 1) * half)
                        value = value.astype(F32)
                        outs[index][to, columns] = value
                        if weight is not None:
                            product = value * extra_r[2 * given][to, columns].astype(F32)
                            total += jnp.sum(product, axis=1, keepdims=True)
                column_s[to, :] = jnp.broadcast_to(total, (rows, 128))
            at += blocks * pitch
            if weight is not None:
                sums = column_s[...].T[:1, : parts * rows]
                outs[len(sections) + given][...] = sums / extra_r[2 * given + 1][...]
                given += 1

    extra_specs, extra_args = [], []
    for blocks, rows, _, weight, gain in sections:
        if weight is not None:
            extra_specs += [
                pl.BlockSpec((parts * rows, weight.shape[1]), lambda i, ids: (ids[1], 0)), WHOLE
            ]
            extra_args += [weight, gain]
    high = -(-max(parts * rows for _, rows, _, _, _ in sections) // 128) * 128
    return pl.pallas_call(
        body,
        grid_spec=pltpu.PrefetchScalarGridSpec(
            num_scalar_prefetch=1,
            grid=(1,),
            in_specs=[WHOLE] * (2 * parts) + extra_specs + [WHOLE] * len(passed) + [ANY] * len(after),
            out_specs=[WHOLE] * (len(sections) + len(extra) + len(passed)),
            scratch_shapes=[pltpu.VMEM((high, 128), F32)],
        ),
        out_shape=[
            shape((parts * rows, blocks * 2 * half), F32) for blocks, rows, _, _, _ in sections
        ]
        + [shape((1, parts * rows), F32) for _, rows, _, weight, _ in sections if weight is not None]
        + [shape(value.shape, value.dtype) for value in passed],
        compiler_params=params(32),
        cost_estimate=cost(1 << 20, 8 * own[0].size * parts),
        name="join_shares",
    )(ids, *own, *other, *extra_args, *passed, *after)


def swap(value, *bits):
    frames, videos = lax.axis_size("frame"), lax.axis_size("video")
    pairs = []
    for f in range(frames):
        frame_bits, video_bits = bits[f % len(bits)]
        for v in range(videos):
            pairs.append((f * videos + v, (f ^ frame_bits) * videos + (v ^ video_bits)))
    return lax.ppermute(value, BOTH, pairs)


CORE = ((1, 0),)
ACROSS = ((2, 0),)
FIRST = ((0, 1), (2, 0))
SECOND = ((2, 0), (0, 1))


def spread(value, axis, bits):
    return jnp.stack([value] + [swap(value, bit) for bit in bits], axis=axis)


def bits_of(name):
    frames, videos = lax.axis_size("frame"), lax.axis_size("video")
    return {
        "core": [(1, 0)],
        "y": [(2 * y, 0) for y in range(1, frames // 2)],
        "x": [(0, 1)],
        "z": [(0, 2 * z) for z in range(1, videos // 2)],
    }[name]


class Gather:
    def __init__(self, value):
        self.value = value

    def start(self, axis, name):
        self.axis = axis
        self.moved = [swap(self.value, bit) for bit in bits_of(name)]
        return [self.value]

    def finish(self, after=None):
        moved = self.moved if after is None else tie(self.moved, after)
        self.value = jnp.stack([self.value] + moved, axis=self.axis)
        return [self.value]


def wide(value):
    return value.astype(F32)


def add_low(*values):
    return functools.reduce(jnp.add, [wide(v) for v in values]).astype(LOW)


def tie(values, after):
    return lax.optimization_barrier((values, after))[0]


class Share:
    def __init__(self, keep, send):
        self.sums, self.send = [keep], send

    def move(self, send, bits):
        self.moved = [swap(send, *bits)]
        return [send]

    def hold(self, after):
        self.moved = tie(self.moved, after)
        return self

    def core_swap(self):
        return self.move(self.send, CORE)

    def halve(self, bits):
        sums = self.sums + self.moved
        self.sums = [s[0] for s in sums]
        return self.move(add_low(*[s[1] for s in sums]), bits)

    def first_swap(self):
        return self.halve(FIRST)

    def second_swap(self):
        return self.halve(SECOND)

    def z_sends(self):
        sums = self.sums + self.moved
        self.sums, self.moved = [s[0] for s in sums], []
        self.sends = [
            add_low(*[s[z] for s in sums]) for z in range(1, lax.axis_size("video") // 2)
        ]
        return self.sends

    def z_swap(self, zs, after):
        sends = tie([self.sends[z - 1] for z in zs], after)
        self.moved = self.moved + [swap(send, (0, 2 * z)) for send, z in zip(sends, zs)]

    def total(self):
        total = add_low(*self.sums, *self.moved)
        bit = 4
        while bit < lax.axis_size("frame"):
            total = lax.optimization_barrier(total)
            total = add_low(total, swap(total, (bit, 0)))
            bit *= 2
        return lax.optimization_barrier(total)


def rows_of(value, lead):
    return value.reshape(*value.shape[:lead], -1, value.shape[-1])


class Join:
    def __init__(self, total):
        self.own = [total]
        self.moved = [swap(total, *ACROSS), swap(total, *CORE), swap(total, (3, 0))]

    def hold(self, after):
        self.moved = tie(self.moved, after)
        return self

    def parts(self):
        across, core, both = self.moved
        return self.own + [across], [core, both]


class SlowJoin:
    def __init__(self, total):
        self.total = total
        self.across = swap(total, *ACROSS)

    def hold(self, after):
        self.across = tie(self.across, after)
        return self

    def parts(self):
        own = [self.total, self.across]
        return own, [swap(value, *CORE) for value in own]


def flat(value):
    return value.reshape(-1, value.shape[-1])


def on_device(
    frames,
    out_cotangent,
    frame_counts,
    message_proj,
    message_gain,
    message_qkv,
    message_out,
    attn_gain,
    attn_qkv,
    attn_out,
    mlp_gain,
    mlp_up,
    mlp_down,
):
    videos, slots, patches, width = frames.shape
    tokens = patches + 1
    padded = -(-tokens // 16) * 16
    frame_total = videos * slots
    row_total = frame_total * padded
    frame_axis, video_axis = lax.axis_size("frame"), lax.axis_size("video")
    frame_index, video_index = lax.axis_index("frame"), lax.axis_index("video")
    share = width // video_axis
    ids = jnp.stack([frame_index & 1, video_index, frame_index >> 1]).astype(jnp.int32)
    slot_ids = frame_index * slots + jnp.arange(slots, dtype=jnp.int32)
    alive = (slot_ids[None, :] < frame_counts[:, None]).astype(F32).reshape(frame_total)
    gains = [g.reshape(1, width) for g in (message_gain, attn_gain, mlp_gain)]
    tokens_in = frames.transpose(0, 2, 1, 3)
    cotangent = out_cotangent.transpose(0, 2, 1, 3)

    class_rows = tokens_in[:, 0].reshape(frame_total, width)
    flags = jnp.broadcast_to(alive.astype(LOW)[:, None], (frame_total, 128))
    sizes = (frame_axis * frame_total, slots, videos)
    payload = jnp.concatenate([class_rows, flags], axis=1)
    payload = jnp.stack([payload] + [swap(payload, (f, 0)) for f in range(1, frame_axis)])
    payload = payload.reshape(frame_axis // 2, 2, frame_total, -1).transpose(1, 0, 2, 3)
    near = payload.reshape(-1, width + 128)

    step = min(2, slots)
    one, triple, final, inverse_one = frame_project(
        alive, tokens_in, cotangent, gains[1], attn_qkv, padded, step
    )
    classes = Gather(payload)
    classes.start(0, "z")
    message_two, one_rows, triple_rows = message_token(
        sizes, near, gains[0], message_proj, message_qkv, message_out, gains[1], attn_qkv
    )
    waits = classes.finish(message_two)
    classes.start(0, "x")
    one, triple, context, logs, hidden, two = frame_attend(
        tokens_in, message_two, one_rows, triple_rows, one, triple, gains[2], attn_out, step, waits
    )
    waits = classes.finish(two)
    payload = flat(classes.value)
    (
        encoded, hidden_grad, hidden_low, feed_keep, feed_send,
    ) = feed_forward(
        ids,
        alive,
        hidden.reshape(row_total, width),
        two.reshape(row_total, width),
        final.reshape(row_total, width),
        context.reshape(row_total, width),
        gains[2],
        mlp_up,
        mlp_down,
        (videos, patches, slots, padded),
        video_axis,
        waits,
    )

    hidden_low = hidden_low.reshape(frame_total, padded, width)
    hidden_grad = hidden_grad.reshape(frame_total, padded, width)
    feed = Share(feed_keep, feed_send)
    feed.core_swap()
    first_steps = 1
    triple_grad = frame_backward(
        hidden_low, triple, logs, attn_out, tokens, step, 0, first_steps
    )
    waits = feed.hold(triple_grad).first_swap()
    triple_grad = frame_backward(
        hidden_low, triple, logs, attn_out, tokens, step, first_steps,
        frame_total // step - first_steps, triple_grad, waits,
    )
    two_rows = message_rows(
        triple_grad, message_two, hidden_grad, patches, gains[1], attn_qkv
    )
    gather = Gather(two_rows)
    gather.start(0, "z")
    waits = feed.hold(triple_grad).second_swap()
    keep, send = qkv_weight_grad(
        ids, one.reshape(row_total, width), triple_grad.reshape(row_total, 3 * width), video_axis, waits
    )
    rest = Share(rows_of(keep, 3), rows_of(send, 3))
    rest.core_swap()
    zs = list(range(1, video_axis // 2))
    gather.finish(keep)
    waits = feed.hold(keep).z_sends()
    feed.z_swap(zs[:2], keep)
    gather.start(1, "y")
    pre, low, qkv_rows, message_logs, mcontext = message_forward(
        sizes, payload, gains[0], message_proj, message_qkv, message_out, waits
    )
    waits = gather.finish(pre) + rest.hold(pre).first_swap()
    gather.start(0, "x")
    feed.z_swap(zs[2:], pre)
    stream_grad = stream_backward(
        one, inverse_one, hidden_grad, triple_grad, gains[1], attn_qkv, tokens_in.shape, step, 0, 1,
        None, waits,
    )
    waits = gather.finish(stream_grad) + rest.hold(stream_grad).second_swap()
    gather.start(2, "core")
    stream_grad = stream_backward(
        one, inverse_one, hidden_grad, triple_grad, gains[1], attn_qkv, tokens_in.shape, step, 1,
        videos - 1, stream_grad, waits,
    )
    gather.finish(stream_grad)
    feed_total = feed.hold(stream_grad).total()
    feed_join = SlowJoin(feed_total)
    waits = [feed_total] + rest.hold(stream_grad).z_sends()
    rest.z_swap(zs[::-1], stream_grad)
    two_rows = flat(gather.value)
    class_grad, message_gain_grad, proj_sum, mqkv_sum, message_out_sum = message_backward(
        sizes, ids, payload, two_rows, pre, low, qkv_rows, message_logs, mcontext,
        gains[0], message_proj, message_qkv, message_out, share, waits,
    )
    feed_join.hold(class_grad), rest.hold(class_grad)
    cut = video_index * share

    def own_gain(gain):
        return lax.dynamic_slice(gain, (0, cut), (1, share))

    half_share = share // 2
    pitch, down_half = pitch_of(half_share), mlp_down.shape[0] // video_axis // 2
    up_sum, out_sum, down_sum, mlp_gain_sum, class_grad = join_shares(
        ids, *feed_join.parts(),
        [
            (mlp_up.shape[1] // width, half_share, pitch, mlp_up, own_gain(gains[2])),
            (1, half_share, pitch, None, None),
            (1, down_half, down_half, None, None),
        ],
        rest.moved,
        class_grad[:frame_total],
    )
    stream_grad = lax.dynamic_update_slice(
        stream_grad,
        stream_grad[:, :1] + class_grad.reshape(videos, 1, slots, width),
        (0, 0, 0, 0),
    )
    qkv_sum, attn_gain_sum = join_shares(
        ids, *Join(rest.total()).parts(), [(3, half_share, half_share, attn_qkv, own_gain(gains[1]))]
    )
    message_gain_sum = lax.dynamic_slice(message_gain_grad[0], (cut,), (share,))
    attn_gain_sum, mlp_gain_sum = attn_gain_sum[0], mlp_gain_sum[0]
    return (
        encoded.transpose(0, 2, 1, 3),
        stream_grad.transpose(0, 2, 1, 3),
        proj_sum,
        message_gain_sum,
        mqkv_sum,
        message_out_sum,
        attn_gain_sum,
        qkv_sum,
        out_sum,
        mlp_gain_sum,
        up_sum,
        down_sum,
    )


def solution(mesh):
    return jax.shard_map(
        on_device,
        mesh=mesh,
        in_specs=(
            P("video", "frame", None, None),
            P("video", "frame", None, None),
            P("video"),
            P(),
            P(),
            P(),
            P(),
            P(),
            P(),
            P(),
            P(),
            P(),
            P(),
        ),
        out_specs=(
            P("video", "frame", None, None),
            P("video", "frame", None, None),
            P("video", None),
            P("video"),
            P("video", None),
            P("video", None),
            P("video"),
            P("video", None),
            P("video", None),
            P("video"),
            P("video", None),
            P("video", None),
        ),
        check_vma=False,
    )
```
